32 devices in a mesh: wide: 16 (over z, y, core), narrow: 2 (over x).
Axes of the slice: x: 2, y: 2, z: 4, core: 2. Of those that a mesh axis runs over, the one named last changes fastest.
Arguments:
- activations: bfloat16 [16896, 768], P(('wide', 'narrow')), may hold values from -6 to 6
- cotangent: bfloat16 [16896, 768], P(('wide', 'narrow')), may hold values from -6 to 6
- item_kinds: int32 [32, 8], P(('wide', 'narrow')), may hold values from 0 to 3, as said below
- attn_norm_gain: bfloat16 [768], P('wide'), may hold values from 0.5 to 1.5
- attn_norm_bias: bfloat16 [768], P('wide'), may hold values from -1.25 to 1.25
- query_weight: bfloat16 [768, 768], P('wide'), may hold values from -0.21875 to 0.21875
- query_bias: bfloat16 [768], P('wide'), may hold values from -1.25 to 1.25
- key_weight: bfloat16 [768, 768], P('wide'), may hold values from -0.21875 to 0.21875
- value_weight: bfloat16 [768, 768], P('wide'), may hold values from -0.21875 to 0.21875
- value_bias: bfloat16 [768], P('wide'), may hold values from -1.25 to 1.25
- output_weight: bfloat16 [768, 768], P('wide'), may hold values from -1.75 to 1.75
- output_bias: bfloat16 [768], P('wide'), may hold values from -1.25 to 1.25
- ffn_norm_gain: bfloat16 [768], P('wide'), may hold values from 0.5 to 1.5
- ffn_norm_bias: bfloat16 [768], P('wide'), may hold values from -1.25 to 1.25
- up_weight: bfloat16 [3, 768, 3072], P(None, 'wide'), may hold values from -0.21875 to 0.21875
- up_bias: bfloat16 [3, 3072], P(None, 'wide'), may hold values from -1.25 to 1.25
- down_weight: bfloat16 [3, 3072, 768], P(None, 'wide'), may hold values from -0.109375 to 0.109375
- down_bias: bfloat16 [3, 768], P(None, 'wide'), may hold values from -1.25 to 1.25
Outputs:
- mixed: bfloat16 [16896, 768], P(('wide', 'narrow'))
- input_grad: float32 [16896, 768], P(('wide', 'narrow'))
- attn_norm_gain_grad: float32 [768], P('wide')
- attn_norm_bias_grad: float32 [768], P('wide')
- query_weight_grad: float32 [768, 768], P('wide')
- query_bias_grad: float32 [768], P('wide')
- key_weight_grad: float32 [768, 768], P('wide')
- value_weight_grad: float32 [768, 768], P('wide')
- value_bias_grad: float32 [768], P('wide')
- output_weight_grad: float32 [768, 768], P('wide')
- output_bias_grad: float32 [768], P('wide')
- ffn_norm_gain_grad: float32 [768], P('wide')
- ffn_norm_bias_grad: float32 [768], P('wide')
- up_weight_grad: float32 [3, 768, 3072], P(None, 'wide')
- up_bias_grad: float32 [3, 3072], P(None, 'wide')
- down_weight_grad: float32 [3, 3072, 768], P(None, 'wide')
- down_bias_grad: float32 [3, 768], P(None, 'wide')
The draws below stay inside these ranges and needn't reach their ends.
Inputs may be any that keep to these rules, and one draw needn't show every extreme that they name: `item_kinds`: each row lists one window's items in order; 3 marks an empty item place and comes only after all items; the items of a window fill at most 522 of its rows.
All inputs are finite; a program needn't handle non-finite values.
Results may differ from the reference program's by a relative error of at most 0.019.
Values may be sent and summed in bfloat16 or wider, within the bound.
A program may use at most 256 MiB of HBM per device.

```python
import jax
import jax.numpy as jnp
from jax import lax

D = 768
HEADS = 12
FF = 3072
EXPERTS = 3
IMG_LEN = 197
TXT_LEN = 64
BLOCK = 128
WINDOWS = 1
HEAD_DIM = 64
WINDOW = 528
WINS = 32
TOKENS = 16896
DEVICES = 32


def draw_item_kinds(key, part):
    key = jax.random.fold_in(key, 11)
    table = jnp.array([[2, 2, 3, 3, 3, 3, 3, 3], [0, 2, 1, 3, 3, 3, 3, 3], [1, 0, 0, 1, 3, 3, 3, 3], [1, 1, 1, 1, 1, 1, 1, 1], [2, 1, 0, 3, 3, 3, 3, 3], [0, 1, 1, 1, 1, 3, 3, 3], [2, 0, 3, 3, 3, 3, 3, 3], [0, 0, 1, 3, 3, 3, 3, 3]], jnp.int32)
    picks = jax.random.randint(key, (WINDOWS * DEVICES,), 0, 8)
    return table[picks]


def block_scale(own_key, shape, shards, least, largest):
    def one(position, parts):
        steps = jax.random.uniform(jax.random.fold_in(jax.random.fold_in(own_key, 6), position), (parts,), jnp.float32, least / len(shards), largest / len(shards))
        return jnp.repeat(jnp.exp(steps), shape[position] // parts).reshape((-1,) + (1,) * (len(shape) - position - 1))

    gain = one(*shards[0])
    for cut in shards[1:]:
        gain = gain * one(*cut)
    return gain


def centred(key, shape, width, bound, cuts=(), kind=jnp.bfloat16):
    factor_of = block_scale(key, shape, cuts, -0.22, 0.18) if cuts else 1.0
    values = jax.random.normal(key, shape, jnp.float32) * width * factor_of
    return jnp.minimum(jnp.maximum(values, -bound), bound).astype(kind)


def setup_inputs(seed: int = 0) -> dict:
    splits = jax.random.split(jax.random.key(seed), 19)
    activations = centred(splits[0], (TOKENS, D), 1.0, 6.0, ((0, 32),))
    cotangent = centred(splits[1], (TOKENS, D), 1.0, 6.0, ((0, 32),))
    item_kinds = draw_item_kinds(jax.random.fold_in(splits[18], 71), 0)
    attn_norm_gain = jnp.clip(1.0 + 0.1 * jax.random.normal(splits[3], (D,), jnp.float32), 0.5, 1.5).astype(jnp.bfloat16)
    attn_norm_bias = centred(splits[4], (D,), 0.2, 1.25, ((0, 16),))
    query_weight = centred(splits[5], (D, D), D ** -0.5, 0.21875, ((0, 16),))
    query_bias = centred(splits[6], (D,), 0.2, 1.25, ((0, 16),))
    key_weight = centred(splits[7], (D, D), D ** -0.5, 0.21875, ((0, 16),))
    value_weight = centred(splits[8], (D, D), D ** -0.5, 0.21875, ((0, 16),))
    value_bias = centred(splits[9], (D,), 0.2, 1.25, ((0, 16),))
    output_weight = centred(splits[10], (D, D), (max(D // 64, 1)) ** -0.5, 1.75, ((0, 16),))
    output_bias = centred(splits[11], (D,), 0.2, 1.25, ((0, 16),))
    ffn_norm_gain = jnp.clip(1.0 + 0.1 * jax.random.normal(splits[12], (D,), jnp.float32), 0.5, 1.5).astype(jnp.bfloat16)
    ffn_norm_bias = centred(splits[13], (D,), 0.2, 1.25, ((0, 16),))
    up_weight = centred(splits[14], (EXPERTS, D, FF), D ** -0.5, 0.21875, ((1, 16),))
    up_bias = centred(splits[15], (EXPERTS, FF), 0.2, 1.25, ((1, 16),))
    down_weight = centred(splits[16], (EXPERTS, FF, D), FF ** -0.5, 0.109375, ((1, 16),))
    down_bias = centred(splits[17], (EXPERTS, D), 0.2, 1.25, ((1, 16),))
    return {"activations": activations, "cotangent": cotangent, "item_kinds": item_kinds, "attn_norm_gain": attn_norm_gain, "attn_norm_bias": attn_norm_bias, "query_weight": query_weight, "query_bias": query_bias, "key_weight": key_weight, "value_weight": value_weight, "value_bias": value_bias, "output_weight": output_weight, "output_bias": output_bias, "ffn_norm_gain": ffn_norm_gain, "ffn_norm_bias": ffn_norm_bias, "up_weight": up_weight, "up_bias": up_bias, "down_weight": down_weight, "down_bias": down_bias}


EPS = 1e-05
MASKED = -1e+30
HIGH = lax.Precision.HIGHEST

@jax.custom_vjp
def low(v):
    return lax.optimization_barrier(v.astype(jnp.bfloat16)).astype(jnp.float32)

@jax.custom_vjp
def low_back(v):
    return v

def low_keep(v):
    return (low(v), None)

def low_pass(kept, grad):
    return (grad,)

def back_keep(v):
    return (v, None)

def back_low(kept, grad):
    return (low(grad),)
low.defvjp(low_keep, low_pass)
low_back.defvjp(back_keep, back_low)

def norm_rows(block_rows, gain_vec, offset):
    row_mean = lax.optimization_barrier(jnp.mean(block_rows, axis=-1, keepdims=True))
    centered = block_rows - row_mean
    spread = lax.optimization_barrier(jnp.mean(centered * centered, axis=-1, keepdims=True))
    return centered * lax.rsqrt(spread + EPS) * gain_vec + offset

def layout(item_table, image_len, text_len, window_len):
    lengths = jnp.where(item_table == 0, image_len, jnp.where(item_table == 1, text_len, jnp.where(item_table == 2, image_len + text_len, 0))).astype(jnp.int32)
    item_ends = jnp.cumsum(lengths, axis=1).astype(jnp.int32)
    positions = jnp.arange(window_len, dtype=jnp.int32)
    segment = lax.optimization_barrier(jnp.sum((positions[None, :, None] >= item_ends[:, None, :]).astype(jnp.int32), axis=2)).astype(jnp.int32)
    inside = positions[None, :] < item_ends[:, -1:]
    places = jnp.arange(item_table.shape[1], dtype=jnp.int32)
    picked = lax.optimization_barrier(jnp.sum(jnp.where(segment[:, :, None] == places[None, None, :], item_table[:, None, :], 0), axis=2))
    expert = jnp.where(inside, picked, EXPERTS).astype(jnp.int32)
    return (segment, inside, expert)

def dispatch(expert_flat, block_size, block_count):
    tok_count = expert_flat.shape[0]
    slot_total = block_count * block_size
    onehot = (expert_flat[:, None] == jnp.arange(EXPERTS, dtype=jnp.int32)[None, :]).astype(jnp.int32)
    counts = lax.optimization_barrier(jnp.sum(onehot, axis=0)).astype(jnp.int32)
    blocks_each = (counts + block_size - 1) // block_size
    first_block = (jnp.cumsum(blocks_each) - blocks_each).astype(jnp.int32)
    order_in = lax.optimization_barrier(jnp.sum((jnp.cumsum(onehot, axis=0).astype(jnp.int32) - onehot) * onehot, axis=1)).astype(jnp.int32)
    start_own = lax.optimization_barrier(jnp.sum(first_block[None, :] * onehot, axis=1)).astype(jnp.int32)
    routed = expert_flat < EXPERTS
    slot_of = jnp.where(routed, start_own * block_size + order_in, slot_total).astype(jnp.int32)
    source = jnp.zeros((slot_total,), jnp.int32).at[slot_of].set(jnp.arange(tok_count, dtype=jnp.int32), mode='drop')
    filled = jnp.zeros((slot_total,), jnp.int32).at[slot_of].set(1, mode='drop')
    block_ends = first_block + blocks_each
    block_ids = jnp.arange(block_count, dtype=jnp.int32)
    block_expert = jnp.minimum(lax.optimization_barrier(jnp.sum((block_ids[:, None] >= block_ends[None, :]).astype(jnp.int32), axis=1)), EXPERTS - 1).astype(jnp.int32)
    slot_back = jnp.minimum(slot_of, slot_total - 1).astype(jnp.int32)
    return (slot_back, routed, source, filled, block_expert)

def reference(activations, cotangent, item_kinds, attn_norm_gain, attn_norm_bias, query_weight, query_bias, key_weight, value_weight, value_bias, output_weight, output_bias, ffn_norm_gain, ffn_norm_bias, up_weight, up_bias, down_weight, down_bias):
    segment, inside, expert = layout(item_kinds, IMG_LEN, TXT_LEN, WINDOW)
    block_count = TOKENS // BLOCK + 3
    slot_back, routed, source, filled, block_expert = dispatch(expert.reshape(TOKENS), BLOCK, block_count)
    inside_rows = inside.reshape(TOKENS, 1).astype(jnp.float32)
    routed_rows = routed.reshape(TOKENS, 1).astype(jnp.float32)
    filled_rows = filled.reshape(-1, 1).astype(jnp.float32)
    score_scale = HEAD_DIM ** (-0.5)

    def forward(inputs, gain_one, bias_one, query_mat, query_vec, key_mat, value_mat, value_vec, output_mat, output_vec, gain_two, bias_two, up_mats, up_vecs, down_mats, down_vecs):
        normed_one = low(norm_rows(inputs, gain_one, bias_one))
        queries = low(low_back(jnp.dot(normed_one, query_mat, precision=HIGH) + query_vec))
        keys_all = low(low_back(jnp.dot(normed_one, key_mat, precision=HIGH)))
        values_all = low(low_back(jnp.dot(normed_one, value_mat, precision=HIGH) + value_vec))

        def window_attend(packed):
            query_blk, key_blk, value_blk, seg_blk = packed
            query_h = query_blk.reshape(WINDOW, HEADS, HEAD_DIM)
            key_h = key_blk.reshape(WINDOW, HEADS, HEAD_DIM)
            value_h = value_blk.reshape(WINDOW, HEADS, HEAD_DIM)
            raw_scores = jnp.einsum('qhd,khd->hqk', query_h, key_h, precision=HIGH)
            scores = low_back(raw_scores * score_scale)
            same_item = seg_blk[:, None] == seg_blk[None, :]
            scores = jnp.where(same_item[None], scores, MASKED)
            row_top = lax.optimization_barrier(jnp.max(scores, axis=2, keepdims=True))
            weights_raw = jnp.exp(scores - row_top)
            probs = low(weights_raw / lax.optimization_barrier(jnp.sum(weights_raw, axis=2, keepdims=True)))
            mixed_heads = jnp.einsum('hqk,khd->qhd', probs, value_h, precision=HIGH)
            return mixed_heads.reshape(WINDOW, D)
        heads_out = lax.map(jax.checkpoint(window_attend), (queries.reshape(WINS, WINDOW, D), keys_all.reshape(WINS, WINDOW, D), values_all.reshape(WINS, WINDOW, D), segment))
        heads_out = low(low_back(heads_out.reshape(TOKENS, D)))
        attn_out = low_back(jnp.dot(heads_out, output_mat, precision=HIGH) + output_vec)
        hidden_one = inputs + inside_rows * attn_out
        normed_two = low(norm_rows(hidden_one, gain_two, bias_two))
        buffer = (normed_two[source] * filled_rows).reshape(block_count, BLOCK, D)

        def expert_block(packed):
            block_rows, expert_id = packed
            pre_act = low_back(jnp.dot(block_rows, up_mats[expert_id], precision=HIGH) + up_vecs[expert_id])
            act_rows = low(jax.nn.gelu(pre_act, approximate=False))
            return jnp.dot(act_rows, down_mats[expert_id], precision=HIGH) + down_vecs[expert_id]
        expert_out = lax.map(jax.checkpoint(expert_block), (buffer, block_expert)).reshape(block_count * BLOCK, D)
        token_out = low_back(expert_out[slot_back] * routed_rows)
        return hidden_one + token_out
    primals = [member.astype(jnp.float32) for member in (activations, attn_norm_gain, attn_norm_bias, query_weight, query_bias, key_weight, value_weight, value_bias, output_weight, output_bias, ffn_norm_gain, ffn_norm_bias, up_weight, up_bias, down_weight, down_bias)]
    result, pullback = jax.vjp(forward, *primals)
    gradients = pullback(cotangent.astype(jnp.float32))
    return (result.astype(jnp.bfloat16), gradients[0], gradients[1], gradients[2], gradients[3], gradients[4], gradients[5], gradients[6], gradients[7], gradients[8], gradients[9], gradients[10], gradients[11], gradients[12], gradients[13], gradients[14], gradients[15])
```

```python
import functools

import jax
import jax.numpy as jnp
from jax import lax
from jax.experimental import pallas as pl
from jax.experimental.pallas import tpu as pltpu
from jax.sharding import PartitionSpec as P

HEADS = 12
EXPERTS = 3
IMG_LEN = 197
TXT_LEN = 64
EPS = 1e-05
MASKED = -1e30
GROUP = 4
VROWS = 16
MESH = pl.DeviceIdType.MESH
BF = jnp.bfloat16
F32 = jnp.float32
VMEM_LIMIT = 63 * 1024 * 1024


def dot(a, b):
    return lax.dot_general(a, b, (((1,), (0,)), ((), ())), preferred_element_type=F32)


def dot_nt(a, b):
    return lax.dot_general(a, b, (((1,), (1,)), ((), ())), preferred_element_type=F32)


def dot_tn(a, b):
    return lax.dot_general(a, b, (((0,), (0,)), ((), ())), preferred_element_type=F32)


class Place:
    def __init__(self, wide, narrow):
        self.wide, self.narrow = wide, narrow
        self.ring = wide // GROUP
        w = lax.axis_index("wide")
        self.x = lax.axis_index("narrow")
        self.w = w
        self.a = lax.div(w, GROUP)
        self.q = lax.rem(w, GROUP)
        self.c = lax.rem(w, 2)
        self.y = lax.div(self.q, 2)
        self.h = lax.rem(self.x, 2)
        self.q_core = 2 * self.y + 1 - self.c
        self.q_y = 2 * (1 - self.y) + self.c
        self.q_diag = 2 * (1 - self.y) + 1 - self.c
        self.next = lax.rem(self.a + 1, self.ring)
        self.prev = lax.rem(self.a + self.ring - 1, self.ring)

    def member(self, q):
        return (self.a * GROUP + q, self.x)

    def ring_next(self):
        return (self.next * GROUP + self.q, self.x)

    def ring_prev(self):
        return (self.prev * GROUP + self.q, self.x)

    def pair(self):
        return (self.w, self.x + 1 - 2 * self.h)

    def other_narrow(self, k):
        return (self.w, lax.rem(self.x + k, self.narrow))

    def back(self, s):
        return lax.rem(self.a - s + 2 * self.ring, self.ring)

    def barrier(self, narrow_all):
        sem = pltpu.get_barrier_semaphore()
        who = [self.member(self.q_core), self.member(self.q_y), self.member(self.q_diag)]
        who += [self.ring_next(), self.ring_prev()]
        if narrow_all:
            who += [self.other_narrow(k) for k in range(1, self.narrow)]
        else:
            who += [self.pair()]
        for dev in who:
            pl.semaphore_signal(sem, inc=1, device_id=dev, device_id_type=MESH)
        pl.semaphore_wait(sem, len(who))


def remote(src, dst, sends, recvs, i, dev):
    return pltpu.make_async_remote_copy(
        src_ref=src,
        dst_ref=dst,
        send_sem=sends.at[i],
        recv_sem=recvs.at[i],
        device_id=dev,
        device_id_type=MESH,
    )


def item_bounds(kinds, count):
    start = jnp.int32(0)
    bounds = []
    for i in range(count):
        kind = kinds(i)
        length = jnp.where(
            kind == 0,
            IMG_LEN,
            jnp.where(kind == 1, TXT_LEN, jnp.where(kind == 2, IMG_LEN + TXT_LEN, 0)),
        )
        bounds.append((kind, start, start + length))
        start = start + length
    return bounds


def segments(position, bounds):
    seg = jnp.zeros(position.shape, jnp.int32)
    for _, _, end in bounds:
        seg = seg + jnp.where(position >= end, 1, 0)
    return seg


def expert_of(position, bounds):
    out = jnp.full(position.shape, EXPERTS, jnp.int32)
    for kind, start, end in bounds:
        out = jnp.where((position >= start) & (position < end), kind, out)
    return out


def fill_bias(bias_ref, bounds):
    tokens = bias_ref.shape[0]
    seg_col = segments(lax.broadcasted_iota(jnp.int32, (tokens, 1), 0), bounds)
    seg_row = segments(lax.broadcasted_iota(jnp.int32, (1, tokens), 1), bounds)
    bias_ref[...] = jnp.where(seg_col == seg_row, 0.0, MASKED).astype(F32)


def as_matrix(block):
    n, rows, d = block.shape
    if rows % 16 == 0:
        return block.reshape(n * rows, d)
    return block.astype(F32).reshape(n * rows, d).astype(block.dtype)


def as_slabs(matrix, n):
    total, d = matrix.shape
    rows = total // n
    if rows % 16 == 0:
        return matrix.astype(BF).reshape(n, rows, d)
    return matrix.reshape(n, rows, d).astype(BF)


def spread(width, total, part, index):
    row = lax.broadcasted_iota(jnp.int32, (width, total), 0)
    col = lax.broadcasted_iota(jnp.int32, (width, total), 1)
    return jnp.where((col - index * part == row) & (row < part), 1.0, 0.0).astype(BF)


def normed(v):
    mean = jnp.mean(v, axis=-1, keepdims=True)
    centered = v - mean
    var = jnp.mean(centered * centered, axis=-1, keepdims=True)
    inv = lax.rsqrt(var + EPS)
    return centered * inv, inv


def pair_lanes(p):
    return pl.ds(pl.multiple_of(p * 128, 128), 128)


def softmax_rows(q_half, k2, bias_ref):
    scores = dot_nt(q_half, k2) + bias_ref[...]
    top = jnp.max(scores, axis=1, keepdims=True)
    raw = jnp.exp(scores - top)
    return raw * (1.0 / jnp.sum(raw, axis=1, keepdims=True))


def gather_kernel(
    wide,
    narrow,
    kinds_ref,
    act_ref,
    cot_ref,
    pack_ref,
    up_ref,
    down_ref,
    kpad_ref,
    ap_ref,
    g_ref,
    tn_ref,
    tc_ref,
    kg_ref,
    h1_ref,
    n1_ref,
    q_ref,
    k_ref,
    v_ref,
    heads_ref,
    vec_ref,
    ub_ref,
    xhat_ref,
    bias_ref,
    wbuf_ref,
    vbuf_ref,
    n2_ref,
    ring_s,
    ring_r,
    y_s,
    y_r,
    core_s,
    core_r,
    grp_s,
    grp_r,
    fring_s,
    fring_r,
    pair_s,
    pair_r,
    tok_s,
    tok_r,
    kin_s,
    kin_r,
    loc,
):
    place = Place(wide, narrow)
    ring = place.ring
    tokens, width = act_ref.shape
    sh = width // wide
    fr = EXPERTS * 0 + ub_ref.shape[1] // ring
    a, q, h = place.a, place.q, place.h
    pending = []

    def go(copy):
        copy.start()
        pending.append(copy)
        return copy

    place.barrier(False)

    own_pack = pltpu.make_async_copy(pack_ref, ap_ref.at[place.w], loc.at[0])
    own_pack.start()

    def slab_copies(s):
        mine = place.back(s) * GROUP + q
        return mine

    def pack_ring(s):
        mine = slab_copies(s)
        src = pack_ref if s == 0 else ap_ref.at[mine]
        return remote(src, ap_ref.at[mine], ring_s, ring_r, s, place.ring_next())

    def pack_y(s):
        mine = slab_copies(s)
        src = pack_ref if s == 0 else ap_ref.at[mine]
        return remote(src, ap_ref.at[mine], y_s, y_r, s, place.member(place.q_y))

    def pack_core(s):
        mine = slab_copies(s)
        src = pack_ref if s == 0 else ap_ref.at[mine]
        return remote(src, ap_ref.at[mine], core_s, core_r, s, place.member(place.q_core))

    def pack_relay(s):
        theirs = place.back(s) * GROUP + place.q_y
        slab = ap_ref.at[theirs]
        return remote(slab, slab, core_s, core_r, ring + s, place.member(place.q_core))

    ring_copies = [go(pack_ring(0))]
    y_copies = [go(pack_y(0))]
    core_copies = [go(pack_core(0))]

    def group_send(r, to):
        return remote(
            up_ref.at[to],
            g_ref.at[0, :, place.a * GROUP + q],
            grp_s,
            grp_r,
            r,
            place.member(to),
        )

    own_up = pltpu.make_async_copy(up_ref.at[q], g_ref.at[0, :, place.w], loc.at[1])
    own_down = pltpu.make_async_copy(
        down_ref, g_ref.at[1, :, pl.ds(a * GROUP, GROUP)], loc.at[1]
    )
    others = (place.q_core, place.q_y, place.q_diag)

    @pl.when(h == 0)
    def _():
        for r in range(3):
            group_send(r, others[r]).start()
        own_up.start()

    @pl.when(h == 1)
    def _():
        own_down.start()

    own_kinds = pltpu.make_async_copy(kpad_ref, kg_ref.at[q], loc.at[2])
    own_kinds.start()
    kind_copies = [
        go(remote(kpad_ref, kg_ref.at[q], kin_s, kin_r, r, place.member(others[r])))
        for r in range(3)
    ]

    xhat, _ = normed(act_ref[...].astype(F32))
    xhat_ref[...] = xhat
    bounds = item_bounds(lambda i: kinds_ref[0, i], kinds_ref.shape[1])
    fill_bias(bias_ref, bounds)

    for s in range(1, ring):
        ring_copies[s - 1].wait_recv()
        if s < ring - 1:
            ring_copies.append(go(pack_ring(s)))
        y_copies.append(go(pack_y(s)))
        core_copies.append(go(pack_core(s)))

    @pl.when(h == 0)
    def _():
        for r in range(3):
            copy = group_send(r, others[r])
            copy.wait_recv()
            copy.wait_send()
        own_up.wait()

    @pl.when(h == 1)
    def _():
        own_down.wait()

    def fslab(s, e):
        return g_ref.at[h, e, pl.ds(place.back(s) * GROUP, GROUP)]

    def fring(s, e):
        slab = fslab(s, e)
        return remote(slab, slab, fring_s, fring_r, s * EXPERTS + e, place.ring_next())

    def fpair(s, e):
        slab = fslab(s, e)
        return remote(slab, slab, pair_s, pair_r, s * EXPERTS + e, place.pair())

    fring_copies = {}
    pair_copies = []

    def expert_service(s):
        for e in range(EXPERTS):
            if s > 0:
                fring_copies[s - 1, e].wait_recv()
            if s < ring - 1:
                fring_copies[s, e] = go(fring(s, e))
            pair_copies.append(go(fpair(s, e)))

    expert_service(0)

    relay_copies = []
    for s in range(ring):
        y_copies[s].wait_recv()
        relay_copies.append(go(pack_relay(s)))
    for copy in core_copies:
        copy.wait_recv()
    for copy in relay_copies:
        copy.wait_recv()
    own_pack.wait()

    def load_weight(i):
        return pltpu.make_async_copy(
            ap_ref.at[:, pl.ds(i * sh, sh), :], wbuf_ref.at[i], loc.at[3 + i]
        )

    load_vec = pltpu.make_async_copy(
        ap_ref.at[:, pl.ds(4 * sh, VROWS), pl.ds(0, 256)], vbuf_ref, loc.at[7]
    )
    load_vec.start()
    loads = [load_weight(i) for i in range(4)]
    for load in loads:
        load.start()

    def token_copies(src_own, ref, base):
        own = remote(src_own, ref.at[q], tok_s, tok_r, base, place.member(place.q_y))
        core = remote(src_own, ref.at[q], tok_s, tok_r, base + 1, place.member(place.q_core))
        far = ref.at[place.q_y]
        relay = remote(far, far, tok_s, tok_r, base + 2, place.member(place.q_core))
        return own, core, relay

    own_cot = pltpu.make_async_copy(cot_ref, tc_ref.at[q], loc.at[8])
    own_cot.start()
    cot_y, cot_core, cot_relay = token_copies(cot_ref, tc_ref, 0)
    go(cot_y)
    go(cot_core)

    load_vec.wait()
    lane = 128 if sh <= 128 else 256
    vec_ref[...] = jnp.zeros(vec_ref.shape, F32)
    ub_ref[...] = jnp.zeros(ub_ref.shape, F32)

    def add_vec(w, carry):
        vec_ref[...] += dot(vbuf_ref[w][:, :lane], spread(lane, width, sh, w))
        return carry

    lax.fori_loop(0, wide, add_vec, 0)

    def add_ub(j, carry):
        ub_ref[...] += dot(vbuf_ref[j * GROUP + q], spread(256, ub_ref.shape[1], fr, j))
        return carry

    lax.fori_loop(0, ring, add_ub, 0)

    n1_ref[...] = (xhat_ref[...] * vec_ref[0:1, :] + vec_ref[1:2, :]).astype(BF)
    loads[0].wait()
    q_ref[...] = (dot(n1_ref[...], as_matrix(wbuf_ref[0])) + vec_ref[2:3, :]).astype(BF)
    loads[1].wait()
    k_ref[...] = dot(n1_ref[...], as_matrix(wbuf_ref[1])).astype(BF)
    loads[2].wait()
    v_ref[...] = (dot(n1_ref[...], as_matrix(wbuf_ref[2])) + vec_ref[3:4, :]).astype(BF)
    loads[3].wait()

    pairs = width // 128
    low = lax.broadcasted_iota(jnp.int32, (tokens, 128), 1) < 64

    def attend(p, carry):
        lanes = pair_lanes(p)
        q2, k2, v2 = q_ref[:, lanes] * 0.125, k_ref[:, lanes], v_ref[:, lanes]
        zero = jnp.zeros_like(q2)
        first = softmax_rows(jnp.where(low, q2, zero), k2, bias_ref).astype(BF)
        out_low = dot(first, v2)
        second = softmax_rows(jnp.where(low, zero, q2), k2, bias_ref).astype(BF)
        out_high = dot(second, v2)
        heads_ref[:, lanes] = jnp.where(low, out_low, out_high).astype(BF)
        return carry

    done = 0
    for s in range(1, ring):
        upto = pairs * s // (ring - 1)
        if upto > done:
            lax.fori_loop(done, upto, attend, 0)
        done = upto
        if s == 1:
            cot_y.wait_recv()
            go(cot_relay)
        expert_service(s)

    inside = lax.broadcasted_iota(jnp.int32, (tokens, 1), 0) < bounds[-1][2]
    attn = dot(heads_ref[...], as_matrix(wbuf_ref[3])) + vec_ref[4:5, :]
    h1 = act_ref[...].astype(F32) + jnp.where(inside, attn, 0.0)
    h1_ref[...] = h1
    xhat2, _ = normed(h1)
    n2_ref[...] = (xhat2 * vec_ref[5:6, :] + vec_ref[6:7, :]).astype(BF)

    own_n2 = pltpu.make_async_copy(n2_ref, tn_ref.at[q], loc.at[9])
    own_n2.start()
    n2_y, n2_core, n2_relay = token_copies(n2_ref, tn_ref, 3)
    go(n2_y)
    go(n2_core)
    n2_y.wait_recv()
    go(n2_relay)
    cot_core.wait_recv()
    cot_relay.wait_recv()
    n2_core.wait_recv()
    n2_relay.wait_recv()
    for copy in kind_copies:
        copy.wait_recv()
    for copy in pair_copies:
        copy.wait_recv()
    for copy in pending:
        copy.wait_send()
    own_kinds.wait()
    own_cot.wait()
    own_n2.wait()


def expert_kernel(
    per_member,
    kinds_ref,
    n2_ref,
    cot_ref,
    g_ref,
    ub_ref,
    y_ref,
    gn_ref,
    dw_ref,
    dub_ref,
    acc_ref,
    pre_ref,
    ga_ref,
):
    step = pl.program_id(0)
    rows = n2_ref.shape[0]
    member = lax.div(step, per_member)
    row0 = lax.rem(step, per_member) * rows
    bounds = item_bounds(lambda i: kinds_ref[member, 0, i], 8)
    position = lax.broadcasted_iota(jnp.int32, (rows, 1), 0) + row0
    expert = expert_of(position, bounds)
    present = []
    for e in range(EXPERTS):
        here = False
        for kind, start, end in bounds:
            here = here | ((kind == e) & (start < row0 + rows) & (end > row0) & (end > start))
        present.append(here)

    @pl.when(step == 0)
    def _():
        acc_ref[...] = jnp.zeros(acc_ref.shape, F32)
        dub_ref[...] = jnp.zeros(dub_ref.shape, F32)

    pre_ref[...] = jnp.zeros(pre_ref.shape, F32)
    ga_ref[...] = jnp.zeros(ga_ref.shape, F32)
    for e in range(EXPERTS):

        @pl.when(present[e])
        def _(e=e):
            mine = expert == e
            pre = dot(n2_ref[...], g_ref[0, e]) + ub_ref[10 + e : 11 + e, :]
            pre_ref[...] = jnp.where(mine, pre, pre_ref[...])
            ga = dot_nt(cot_ref[...], g_ref[1, e])
            ga_ref[...] = jnp.where(mine, ga, ga_ref[...])

    pre = pre_ref[...]
    half_cdf = 0.5 + 0.5 * lax.erf(pre * 0.7071067811865476)
    act = (pre * half_cdf).astype(BF)
    slope = half_cdf + pre * (0.3989422804014327 * jnp.exp(-0.5 * pre * pre))
    grad_pre = (ga_ref[...] * slope).astype(BF)

    y_ref[...] = jnp.zeros(y_ref.shape, BF)
    gn_ref[...] = jnp.zeros(gn_ref.shape, BF)
    for e in range(EXPERTS):

        @pl.when(present[e])
        def _(e=e):
            mine = expert == e
            y_ref[...] = jnp.where(mine, dot(act, g_ref[1, e]).astype(BF), y_ref[...])
            gn_ref[...] = jnp.where(mine, dot_nt(grad_pre, g_ref[0, e]).astype(BF), gn_ref[...])
            zero = jnp.zeros_like(grad_pre)
            grad_mine = jnp.where(mine, grad_pre, zero)
            acc_ref[0, e] += dot_tn(n2_ref[...], grad_mine)
            acc_ref[1, e] += dot_tn(act, jnp.where(mine, cot_ref[...], jnp.zeros_like(cot_ref[...])))
            dub_ref[10 + e : 11 + e, :] += jnp.sum(
                grad_mine.astype(F32), axis=0, keepdims=True
            )

    @pl.when(step == pl.num_programs(0) - 1)
    def _():
        dw_ref[...] = acc_ref[...].astype(BF)


class PackSum:
    def __init__(self, place, own, core_in, y_out, y_in, hop_out, hop_in, last, sems):
        self.place = place
        self.own, self.core_in = own, core_in
        self.y_out, self.y_in = y_out, y_in
        self.hop_out, self.hop_in = hop_out, hop_in
        self.last = last
        (self.core_s, self.core_r, self.y_s, self.y_r) = sems[:4]
        (self.hop_s, self.hop_r, self.x_s, self.x_r) = sems[4:]
        self.copies = []

    def go(self, copy):
        copy.start()
        self.copies.append(copy)
        return copy

    def start(self):
        place = self.place
        self.core = {}
        for s in range(place.ring):
            d = place.back(s + 1)
            for far in (1, 0):
                yy = (1 - place.y) if far else place.y
                src = self.own.at[d * GROUP + 2 * yy + 1 - place.c]
                self.core[s, far] = self.go(
                    remote(
                        src,
                        self.core_in.at[s, far],
                        self.core_s,
                        self.core_r,
                        2 * s + far,
                        place.member(place.q_core),
                    )
                )
        self.to_y = {}
        self.hop = {}

    def load(self, ref, *index):
        return ref[index].astype(F32)

    def send_y(self, s):
        place = self.place
        d = place.back(s + 1)
        self.core[s, 1].wait_recv()
        total = self.load(self.own, d * GROUP + place.q_y) + self.load(self.core_in, s, 1)
        self.y_out[s] = total.astype(BF)
        self.to_y[s] = self.go(
            remote(
                self.y_out.at[s],
                self.y_in.at[s],
                self.y_s,
                self.y_r,
                s,
                place.member(place.q_y),
            )
        )

    def step(self, s):
        place = self.place
        d = place.back(s + 1)
        self.core[s, 0].wait_recv()
        self.to_y[s].wait_recv()
        total = self.load(self.own, d * GROUP + place.q) + self.load(self.core_in, s, 0)
        total = total + self.load(self.y_in, s)
        if s > 0:
            self.hop[s - 1].wait_recv()
            total = total + self.load(self.hop_in, s - 1)
        if s < place.ring - 1:
            self.hop_out[s] = total.astype(BF)
            self.hop[s] = self.go(
                remote(
                    self.hop_out.at[s],
                    self.hop_in.at[s],
                    self.hop_s,
                    self.hop_r,
                    s,
                    place.ring_next(),
                )
            )
        else:
            self.last[place.x] = total.astype(BF)
            self.spread = [
                self.go(
                    remote(
                        self.last.at[place.x],
                        self.last.at[place.x],
                        self.x_s,
                        self.x_r,
                        k - 1,
                        place.other_narrow(k),
                    )
                )
                for k in range(1, place.narrow)
            ]

    def finish(self):
        for copy in self.spread:
            copy.wait_recv()
        total = self.load(self.last, 0)
        for i in range(1, self.place.narrow):
            total = total + self.load(self.last, i)
        for copy in self.copies:
            copy.wait_send()
        return total


def grad_kernel(
    wide,
    narrow,
    kinds_ref,
    act_ref,
    cot_ref,
    h1_ref,
    n1_ref,
    q_ref,
    k_ref,
    v_ref,
    heads_ref,
    vec_ref,
    dub_ref,
    ap_ref,
    yp_ref,
    gnp_ref,
    dw_ref,
    mixed_ref,
    ig_ref,
    ug_ref,
    dg_ref,
    go_ref,
    gq_ref,
    gk_ref,
    gv_ref,
    vout_ref,
    tin_ref,
    town_ref,
    pin_ref,
    fout_ref,
    fin_ref,
    flast_ref,
    wbuf_ref,
    bias_ref,
    ga_ref,
    ghd_ref,
    dk_ref,
    dv_ref,
    vg_ref,
    owna_ref,
    cina_ref,
    youta_ref,
    yina_ref,
    houta_ref,
    hina_ref,
    lasta_ref,
    ownb_ref,
    cinb_ref,
    youtb_ref,
    yinb_ref,
    houtb_ref,
    hinb_ref,
    lastb_ref,
    tok_s,
    tok_r,
    pair_s,
    pair_r,
    fring_s,
    fring_r,
    fx_s,
    fx_r,
    fin_s,
    fin_r,
    loc,
    *pack_sems,
):
    place = Place(wide, narrow)
    ring = place.ring
    tokens, width = act_ref.shape
    sh = width // wide
    fr = dub_ref.shape[1] // ring
    a, q, h = place.a, place.q, place.h
    pending = []

    def go(copy):
        copy.start()
        pending.append(copy)
        return copy

    place.barrier(True)

    tok = []
    for i, (ref, whose) in enumerate(
        ((gnp_ref, place.q_diag), (gnp_ref, place.q_core), (yp_ref, place.q_diag), (yp_ref, place.q_core))
    ):
        tok.append(
            go(remote(ref.at[whose], tin_ref.at[i], tok_s, tok_r, i, place.member(place.q_core)))
        )
    own_loads = []
    for i, (ref, whose) in enumerate(
        ((gnp_ref, place.q_y), (gnp_ref, q), (yp_ref, place.q_y), (yp_ref, q))
    ):
        load = pltpu.make_async_copy(ref.at[whose], town_ref.at[i], loc.at[i])
        load.start()
        own_loads.append(load)

    pairs_in = {}
    for s in range(ring):
        d = place.back(s + 1)
        for e in range(EXPERTS):
            pairs_in[s, e] = go(
                remote(
                    dw_ref.at[1 - h, e, pl.ds(d * GROUP, GROUP)],
                    pin_ref.at[s, e],
                    pair_s,
                    pair_r,
                    s * EXPERTS + e,
                    place.pair(),
                )
            )
    mine = lax.div(place.x, 2)

    def own_slot(s):
        return flast_ref.at[mine] if s == ring - 1 else fout_ref.at[s]

    load_dw = []
    for s in range(ring):
        own = dw_ref.at[h, :, pl.ds(place.back(s + 1) * GROUP, GROUP)]
        load_dw.append(pltpu.make_async_copy(own, own_slot(s), loc.at[10 + s]))
        load_dw[s].start()
    load_w = [
        pltpu.make_async_copy(
            ap_ref.at[:, pl.ds(i * sh, sh), :], wbuf_ref.at[i % 3], loc.at[5 + i]
        )
        for i in range(4)
    ]
    for i in (3, 1, 2):
        load_w[i].start()

    fhop = {}
    flast_copies = {}

    def expert_service(s):
        load_dw[s].wait()
        slot = own_slot(s)
        for e in range(EXPERTS):
            pairs_in[s, e].wait_recv()
            total = slot[e].astype(F32) + pin_ref[s, e].astype(F32)
            if s > 0:
                fhop[s - 1, e].wait_recv()
                total = total + fin_ref[s - 1, e].astype(F32)
            slot[e] = total.astype(BF)
            if s < ring - 1:
                fhop[s, e] = go(
                    remote(
                        fout_ref.at[s, e],
                        fin_ref.at[s, e],
                        fring_s,
                        fring_r,
                        s * EXPERTS + e,
                        place.ring_next(),
                    )
                )
            else:
                for k in range(1, narrow // 2):
                    slab = flast_ref.at[mine, e]
                    flast_copies[e, k] = go(
                        remote(
                            slab,
                            slab,
                            fx_s,
                            fx_r,
                            (k - 1) * EXPERTS + e,
                            place.other_narrow(2 * k),
                        )
                    )

    bounds = item_bounds(lambda i: kinds_ref[0, i], kinds_ref.shape[1])
    fill_bias(bias_ref, bounds)
    far = []
    for i, n in ((0, 0), (2, 1)):
        own_loads[i].wait()
        tok[i].wait_recv()
        town_ref[i] = (town_ref[i].astype(F32) + tin_ref[i].astype(F32)).astype(BF)
        far.append(
            go(
                remote(
                    town_ref.at[i],
                    tin_ref.at[4 + n],
                    tok_s,
                    tok_r,
                    4 + n,
                    place.member(place.q_y),
                )
            )
        )

    position = lax.broadcasted_iota(jnp.int32, (tokens, 1), 0)
    expert = expert_of(position, bounds)
    inside = position < bounds[-1][2]
    expert_service(0)

    vg_ref[...] = dub_ref[...]
    cot = cot_ref[...].astype(F32)
    for e in range(EXPERTS):
        vg_ref[7 + e : 8 + e, :] = jnp.sum(
            jnp.where(expert == e, cot, 0.0), axis=0, keepdims=True
        )

    own_loads[1].wait()
    tok[1].wait_recv()
    far[0].wait_recv()
    gn2 = town_ref[1].astype(F32) + tin_ref[1].astype(F32) + tin_ref[4].astype(F32)
    hat, inv = normed(h1_ref[...])
    vg_ref[5:6, :] = jnp.sum(gn2 * hat, axis=0, keepdims=True)
    vg_ref[6:7, :] = jnp.sum(gn2, axis=0, keepdims=True)
    r = gn2 * vec_ref[5:6, :]
    r_mean = jnp.mean(r, axis=-1, keepdims=True)
    rn_mean = jnp.mean(r * hat, axis=-1, keepdims=True)
    gh = cot_ref[...].astype(F32) + (r - r_mean - hat * rn_mean) * inv
    ig_ref[...] = gh
    grad_attn = jnp.where(inside, gh, 0.0).astype(BF)
    ga_ref[...] = grad_attn
    vg_ref[4:5, :] = jnp.sum(grad_attn.astype(F32), axis=0, keepdims=True)

    sum_a = PackSum(
        place, owna_ref, cina_ref, youta_ref, yina_ref, houta_ref, hina_ref, lasta_ref, pack_sems[:8]
    )
    sum_b = PackSum(
        place, ownb_ref, cinb_ref, youtb_ref, yinb_ref, houtb_ref, hinb_ref, lastb_ref, pack_sems[8:]
    )
    owna_ref[...] = as_slabs(dot_tn(heads_ref[...], ga_ref[...]), wide)
    sum_a.start()
    load_w[3].wait()
    ghd_ref[...] = dot_nt(ga_ref[...], as_matrix(wbuf_ref[0])).astype(BF)
    load_w[0].start()
    for s in range(ring):
        sum_a.send_y(s)
    expert_service(1)

    low = lax.broadcasted_iota(jnp.int32, (tokens, 128), 1) < 64
    dq_ref = ga_ref

    def attend_back(p, carry):
        lanes = pair_lanes(p)
        q2, k2, v2 = q_ref[:, lanes] * 0.125, k_ref[:, lanes], v_ref[:, lanes]
        g2 = ghd_ref[:, lanes]
        zero = jnp.zeros_like(q2)
        dq, dk, dv = [], [], []
        for half in (low, jnp.logical_not(low)):
            qh = jnp.where(half, q2, zero)
            gr = jnp.where(half, g2, zero)
            probs = softmax_rows(qh, k2, bias_ref)
            grad_probs = dot_nt(gr, v2)
            inner = jnp.sum(probs * grad_probs, axis=1, keepdims=True)
            grad_scores = (probs * (grad_probs - inner)).astype(BF)
            dq.append(dot(grad_scores, k2))
            dk.append(dot_tn(grad_scores, qh))
            dv.append(dot_tn(probs.astype(BF), gr))
        dq_ref[:, lanes] = (jnp.where(low, dq[0], dq[1]) * 0.125).astype(BF)
        dk_ref[:, lanes] = (dk[0] + dk[1]).astype(BF)
        dv_ref[:, lanes] = (dv[0] + dv[1]).astype(BF)
        return carry

    pairs = width // 128
    done = 0
    for s in range(2, ring):
        upto = pairs * (s - 1) // (ring - 1)
        if upto > done:
            lax.fori_loop(done, upto, attend_back, 0)
        done = upto
        sum_a.step(s - 2)
        expert_service(s)

    for copy in flast_copies.values():
        copy.wait_recv()
    if narrow > 2:
        for e in range(EXPERTS):
            total = flast_ref[0, e].astype(F32)
            for i in range(1, narrow // 2):
                total = total + flast_ref[i, e].astype(F32)
            flast_ref[0, e] = total.astype(BF)
    others = (place.q_core, place.q_y, place.q_diag)

    def piece(r, to):
        return remote(
            flast_ref.at[0, :, to], ug_ref.at[q], fin_s, fin_r, r, place.member(to)
        )

    own_piece = pltpu.make_async_copy(flast_ref.at[0, :, q], ug_ref.at[q], loc.at[9])
    own_down = pltpu.make_async_copy(flast_ref.at[0], dg_ref, loc.at[9])
    send_down = remote(flast_ref.at[0], dg_ref, fin_s, fin_r, 3, place.pair())
    send_up = remote(ug_ref, ug_ref, fin_s, fin_r, 4, place.pair())

    @pl.when(h == 0)
    def _():
        for i in range(3):
            piece(i, others[i]).start()
        own_piece.start()

    @pl.when(h == 1)
    def _():
        send_down.start()
        own_down.start()

    if pairs > done:
        lax.fori_loop(done, pairs, attend_back, 0)
    for s in range(max(ring - 2, 0), ring):
        sum_a.step(s)

    @pl.when(h == 0)
    def _():
        for i in range(3):
            piece(i, others[i]).wait_recv()
        own_piece.wait()
        send_up.start()

    vg_ref[2:3, :] = jnp.sum(dq_ref[...].astype(F32), axis=0, keepdims=True)
    vg_ref[3:4, :] = jnp.sum(dv_ref[...].astype(F32), axis=0, keepdims=True)
    load_w[0].wait()
    gn1 = dot_nt(dq_ref[...], as_matrix(wbuf_ref[0]))
    load_w[1].wait()
    gn1 = gn1 + dot_nt(dk_ref[...], as_matrix(wbuf_ref[1]))
    load_w[2].wait()
    gn1 = gn1 + dot_nt(dv_ref[...], as_matrix(wbuf_ref[2]))
    hat, inv = normed(act_ref[...].astype(F32))
    vg_ref[0:1, :] = jnp.sum(gn1 * hat, axis=0, keepdims=True)
    vg_ref[1:2, :] = jnp.sum(gn1, axis=0, keepdims=True)
    r = gn1 * vec_ref[0:1, :]
    r_mean = jnp.mean(r, axis=-1, keepdims=True)
    rn_mean = jnp.mean(r * hat, axis=-1, keepdims=True)
    ig_ref[...] = ig_ref[...] + (r - r_mean - hat * rn_mean) * inv

    for i, ref in enumerate((dq_ref, dk_ref, dv_ref)):
        ownb_ref[:, i * sh : (i + 1) * sh, :] = as_slabs(dot_tn(n1_ref[...], ref[...]), wide)
    ownb_ref[:, 3 * sh :, :] = jnp.zeros((wide, VROWS, width), BF)
    low_vec = vg_ref[...].astype(BF)
    row = lax.broadcasted_iota(jnp.int32, (VROWS, 1), 0)

    def put_vec(w, carry):
        small = dot_nt(low_vec, spread(256, width, sh, w))
        large = dot_nt(low_vec, spread(256, width, fr, lax.div(w, GROUP)))
        large = jnp.where(lax.rem(w, GROUP) == q, large, 0.0)
        ownb_ref[w, 3 * sh :, 0:256] = jnp.where(row < 10, small, large).astype(BF)
        return carry

    lax.fori_loop(0, wide, put_vec, 0)
    sum_b.start()

    own_loads[3].wait()
    tok[3].wait_recv()
    far[1].wait_recv()
    mixed = h1_ref[...] + town_ref[3].astype(F32) + tin_ref[3].astype(F32) + tin_ref[5].astype(F32)
    for e in range(EXPERTS):
        mixed = mixed + jnp.where(expert == e, vec_ref[7 + e : 8 + e, :], 0.0)
    mixed_ref[...] = mixed.astype(BF)

    for s in range(ring):
        sum_b.send_y(s)
    for s in range(ring):
        sum_b.step(s)
    go_ref[...] = sum_a.finish()

    @pl.when(h == 0)
    def _():
        for i in range(3):
            piece(i, others[i]).wait_send()
        send_up.wait_send()
        send_down.wait_recv()

    @pl.when(h == 1)
    def _():
        own_down.wait()
        send_down.wait_send()
        send_up.wait_recv()

    last = sum_b.finish()
    gq_ref[...] = last[0:sh]
    gk_ref[...] = last[sh : 2 * sh]
    gv_ref[...] = last[2 * sh : 3 * sh]
    vout_ref[...] = last[3 * sh :, 0:256]
    for copy in pending:
        copy.wait_send()


def body(
    wide,
    narrow,
    activations,
    cotangent,
    item_kinds,
    attn_norm_gain,
    attn_norm_bias,
    query_weight,
    query_bias,
    key_weight,
    value_weight,
    value_bias,
    output_weight,
    output_bias,
    ffn_norm_gain,
    ffn_norm_bias,
    up_weight,
    up_bias,
    down_weight,
    down_bias,
):
    ring = wide // GROUP
    tokens, width = activations.shape
    sh = width // wide
    fr = down_weight.shape[1]
    hidden = fr * ring
    kind_count = item_kinds.shape[1]

    small = jnp.stack(
        [
            attn_norm_gain,
            attn_norm_bias,
            query_bias,
            value_bias,
            output_bias,
            ffn_norm_gain,
            ffn_norm_bias,
        ]
    )
    small = jnp.concatenate([small, down_bias], axis=0)
    small = jnp.pad(small, ((0, 0), (0, width - sh)))
    large = jnp.pad(up_bias, ((0, VROWS - 10 - EXPERTS), (0, width - fr)))
    pack = jnp.concatenate(
        [query_weight, key_weight, value_weight, output_weight, small, large], axis=0
    )
    up_parts = up_weight.reshape(EXPERTS, sh, ring, GROUP, fr).transpose(3, 0, 1, 2, 4)
    up_parts = up_parts.reshape(GROUP, EXPERTS, sh, hidden)
    down_parts = down_weight.reshape(EXPERTS, GROUP, sh, width)
    kinds_pad = jnp.pad(item_kinds, ((0, 7), (0, 128 - kind_count)))

    prow = 4 * sh + VROWS
    anyspace = pl.BlockSpec(memory_space=pl.ANY)
    vmem = pl.BlockSpec(memory_space=pltpu.VMEM)
    smem = pl.BlockSpec(memory_space=pltpu.SMEM)
    dma = lambda n: pltpu.SemaphoreType.DMA((max(n, 1),))
    shape = jax.ShapeDtypeStruct
    token_bf = shape((tokens, width), BF)
    fsteps = ring * EXPERTS

    (ap, g, tn, tc, kg, h1, n1, qs, ks, vs, heads, vec, ub) = pl.pallas_call(
        functools.partial(gather_kernel, wide, narrow),
        out_shape=(
            shape((wide, prow, width), BF),
            shape((2, EXPERTS, wide, sh, width), BF),
            shape((GROUP, tokens, width), BF),
            shape((GROUP, tokens, width), BF),
            shape((GROUP, 8, 128), jnp.int32),
            shape((tokens, width), F32),
            token_bf,
            token_bf,
            token_bf,
            token_bf,
            token_bf,
            shape((VROWS, width), F32),
            shape((VROWS, hidden), F32),
        ),
        in_specs=[smem, vmem, anyspace, anyspace, anyspace, anyspace, anyspace],
        out_specs=(anyspace,) * 5 + (vmem,) * 8,
        scratch_shapes=[
            pltpu.VMEM((tokens, width), F32),
            pltpu.VMEM((tokens, tokens), F32),
            pltpu.VMEM((4, wide, sh, width), BF),
            pltpu.VMEM((wide, VROWS, 256), BF),
            pltpu.VMEM((tokens, width), BF),
            dma(ring),
            dma(ring),
            dma(ring),
            dma(ring),
            dma(2 * ring),
            dma(2 * ring),
            dma(3),
            dma(3),
            dma(fsteps),
            dma(fsteps),
            dma(fsteps),
            dma(fsteps),
            dma(6),
            dma(6),
            dma(3),
            dma(3),
            dma(10),
        ],
        compiler_params=pltpu.CompilerParams(
            collective_id=0, has_side_effects=True, vmem_limit_bytes=VMEM_LIMIT
        ),
        name="gather_attend",
    )(item_kinds, activations, cotangent, pack, up_parts, down_parts, kinds_pad)

    per_member = 3
    rows = tokens // per_member
    full = lambda *dims: pl.BlockSpec(
        dims, lambda i: (0,) * len(dims), pipeline_mode=pl.Buffered(1)
    )
    tile = pl.BlockSpec((rows, width), lambda i: (i, 0))
    y, gn, dw, dub = pl.pallas_call(
        functools.partial(expert_kernel, per_member),
        grid=(GROUP * per_member,),
        out_shape=(
            shape((GROUP * tokens, width), BF),
            shape((GROUP * tokens, width), BF),
            shape((2, EXPERTS, width, width), BF),
            shape((VROWS, hidden), F32),
        ),
        in_specs=[
            smem,
            tile,
            tile,
            full(2, EXPERTS, width, width),
            full(VROWS, hidden),
        ],
        out_specs=(tile, tile, full(2, EXPERTS, width, width), full(VROWS, hidden)),
        scratch_shapes=[
            pltpu.VMEM((2, EXPERTS, width, width), F32),
            pltpu.VMEM((rows, hidden), F32),
            pltpu.VMEM((rows, hidden), F32),
        ],
        compiler_params=pltpu.CompilerParams(
            dimension_semantics=("arbitrary",), vmem_limit_bytes=VMEM_LIMIT
        ),
        name="experts",
    )(
        kg,
        tn.reshape(GROUP * tokens, width),
        tc.reshape(GROUP * tokens, width),
        g.reshape(2, EXPERTS, width, width),
        ub,
    )

    def pack_scratch(rows):
        buf = lambda n: pltpu.VMEM((n, rows, width), BF)
        return [
            buf(wide),
            pltpu.VMEM((ring, 2, rows, width), BF),
            buf(ring),
            buf(ring),
            buf(max(ring - 1, 1)),
            buf(max(ring - 1, 1)),
            buf(narrow),
        ]

    pack_sems = [dma(2 * ring)] * 2 + [dma(ring)] * 4 + [dma(narrow - 1)] * 2
    brow = 3 * sh + VROWS
    slab = (EXPERTS, GROUP, sh, width)
    (mixed, ig, ug, dg, g_out, g_query, g_key, g_value, vout) = pl.pallas_call(
        functools.partial(grad_kernel, wide, narrow),
        out_shape=(
            token_bf,
            shape((tokens, width), F32),
            shape((GROUP, EXPERTS, sh, width), BF),
            shape(slab, BF),
            shape((sh, width), F32),
            shape((sh, width), F32),
            shape((sh, width), F32),
            shape((sh, width), F32),
            shape((VROWS, 256), F32),
        ),
        in_specs=[smem] + [vmem] * 10 + [anyspace] * 4,
        out_specs=(vmem, vmem, anyspace, anyspace) + (vmem,) * 5,
        scratch_shapes=[
            pltpu.VMEM((6, tokens, width), BF),
            pltpu.VMEM((4, tokens, width), BF),
            pltpu.VMEM((ring,) + slab[:1] + slab[1:], BF),
            pltpu.VMEM((max(ring - 1, 1),) + slab, BF),
            pltpu.VMEM((max(ring - 1, 1),) + slab, BF),
            pltpu.VMEM((max(narrow // 2, 1),) + slab, BF),
            pltpu.VMEM((3, wide, sh, width), BF),
            pltpu.VMEM((tokens, tokens), F32),
            pltpu.VMEM((tokens, width), BF),
            pltpu.VMEM((tokens, width), BF),
            pltpu.VMEM((tokens, width), BF),
            pltpu.VMEM((tokens, width), BF),
            pltpu.VMEM((VROWS, width), F32),
        ]
        + pack_scratch(sh)
        + pack_scratch(brow)
        + [
            dma(6),
            dma(6),
            dma(fsteps),
            dma(fsteps),
            dma(fsteps),
            dma(fsteps),
            dma(EXPERTS * max(narrow // 2 - 1, 1)),
            dma(EXPERTS * max(narrow // 2 - 1, 1)),
            dma(5),
            dma(5),
            dma(10 + ring),
        ]
        + pack_sems
        + pack_sems,
        compiler_params=pltpu.CompilerParams(
            collective_id=1, has_side_effects=True, vmem_limit_bytes=VMEM_LIMIT
        ),
        name="gradients",
    )(
        item_kinds,
        activations,
        cotangent,
        h1,
        n1,
        qs,
        ks,
        vs,
        heads,
        vec,
        dub,
        ap,
        y.reshape(GROUP, tokens, width),
        gn.reshape(GROUP, tokens, width),
        dw.reshape(2, EXPERTS, wide, sh, width),
    )

    up_grad = ug.reshape(GROUP, EXPERTS, sh, ring, fr).transpose(1, 2, 3, 0, 4)
    up_grad = up_grad.reshape(EXPERTS, sh, GROUP * hidden).astype(F32)
    down_grad = dg.reshape(EXPERTS, fr, width).astype(F32)
    return (
        mixed,
        ig,
        vout[0, :sh],
        vout[1, :sh],
        g_query,
        vout[2, :sh],
        g_key,
        g_value,
        vout[3, :sh],
        g_out,
        vout[4, :sh],
        vout[5, :sh],
        vout[6, :sh],
        up_grad,
        vout[10:13, :fr],
        down_grad,
        vout[7:10, :sh],
    )


def solution(mesh):
    rows = P(("wide", "narrow"), None)
    return jax.shard_map(
        functools.partial(body, mesh.shape["wide"], mesh.shape["narrow"]),
        mesh=mesh,
        in_specs=(
            rows,
            rows,
            rows,
            P("wide"),
            P("wide"),
            P("wide", None),
            P("wide"),
            P("wide", None),
            P("wide", None),
            P("wide"),
            P("wide", None),
            P("wide"),
            P("wide"),
            P("wide"),
            P(None, "wide", None),
            P(None, "wide"),
            P(None, "wide", None),
            P(None, "wide"),
        ),
        out_specs=(
            rows,
            rows,
            P("wide"),
            P("wide"),
            P("wide", None),
            P("wide"),
            P("wide", None),
            P("wide", None),
            P("wide"),
            P("wide", None),
            P("wide"),
            P("wide"),
            P("wide"),
            P(None, "wide", None),
            P(None, "wide"),
            P(None, "wide", None),
            P(None, "wide"),
        ),
        check_vma=False,
    )
```

```python
import functools

import jax
import jax.numpy as jnp
from jax import lax
from jax.experimental import pallas as pl
from jax.experimental.pallas import tpu as pltpu
from jax.sharding import PartitionSpec as P

HEADS = 12
EXPERTS = 3
IMG_LEN = 197
TXT_LEN = 64
EPS = 1e-05
MASKED = -1e30
GROUP = 4
VROWS = 16
MESH = pl.DeviceIdType.MESH
BF = jnp.bfloat16
F32 = jnp.float32
VMEM_LIMIT = 63 * 1024 * 1024


def dot(a, b):
    return lax.dot_general(a, b, (((1,), (0,)), ((), ())), preferred_element_type=F32)


def dot_nt(a, b):
    return lax.dot_general(a, b, (((1,), (1,)), ((), ())), preferred_element_type=F32)


def dot_tn(a, b):
    return lax.dot_general(a, b, (((0,), (0,)), ((), ())), preferred_element_type=F32)


class Place:
    def __init__(self, wide, narrow):
        self.wide, self.narrow = wide, narrow
        self.ring = wide // GROUP
        w = lax.axis_index("wide")
        self.x = lax.axis_index("narrow")
        self.w = w
        self.a = lax.div(w, GROUP)
        self.q = lax.rem(w, GROUP)
        self.c = lax.rem(w, 2)
        self.y = lax.div(self.q, 2)
        self.h = lax.rem(self.x, 2)
        self.q_core = 2 * self.y + 1 - self.c
        self.q_y = 2 * (1 - self.y) + self.c
        self.q_diag = 2 * (1 - self.y) + 1 - self.c
        self.next = lax.rem(self.a + 1, self.ring)
        self.prev = lax.rem(self.a + self.ring - 1, self.ring)

    def member(self, q):
        return (self.a * GROUP + q, self.x)

    def ring_next(self):
        return (self.next * GROUP + self.q, self.x)

    def ring_prev(self):
        return (self.prev * GROUP + self.q, self.x)

    def pair(self):
        return (self.w, self.x + 1 - 2 * self.h)

    def other_narrow(self, k):
        return (self.w, lax.rem(self.x + k, self.narrow))

    def back(self, s):
        return lax.rem(self.a - s + 2 * self.ring, self.ring)

    def barrier(self, narrow_all):
        sem = pltpu.get_barrier_semaphore()
        who = [self.member(self.q_core), self.member(self.q_y), self.member(self.q_diag)]
        who += [self.ring_next(), self.ring_prev()]
        if narrow_all:
            who += [self.other_narrow(k) for k in range(1, self.narrow)]
        else:
            who += [self.pair()]
        for dev in who:
            pl.semaphore_signal(sem, inc=1, device_id=dev, device_id_type=MESH)
        pl.semaphore_wait(sem, len(who))


def remote(src, dst, sends, recvs, i, dev):
    return pltpu.make_async_remote_copy(
        src_ref=src,
        dst_ref=dst,
        send_sem=sends.at[i],
        recv_sem=recvs.at[i],
        device_id=dev,
        device_id_type=MESH,
    )


def item_bounds(kinds, count):
    start = jnp.int32(0)
    bounds = []
    for i in range(count):
        kind = kinds(i)
        length = jnp.where(
            kind == 0,
            IMG_LEN,
            jnp.where(kind == 1, TXT_LEN, jnp.where(kind == 2, IMG_LEN + TXT_LEN, 0)),
        )
        bounds.append((kind, start, start + length))
        start = start + length
    return bounds


def segments(position, bounds):
    seg = jnp.zeros(position.shape, jnp.int32)
    for _, _, end in bounds:
        seg = seg + jnp.where(position >= end, 1, 0)
    return seg


def expert_of(position, bounds):
    out = jnp.full(position.shape, EXPERTS, jnp.int32)
    for kind, start, end in bounds:
        out = jnp.where((position >= start) & (position < end), kind, out)
    return out


def fill_bias(bias_ref, bounds):
    tokens = bias_ref.shape[0]
    seg_col = segments(lax.broadcasted_iota(jnp.int32, (tokens, 1), 0), bounds)
    seg_row = segments(lax.broadcasted_iota(jnp.int32, (1, tokens), 1), bounds)
    bias_ref[...] = jnp.where(seg_col == seg_row, 0.0, MASKED).astype(F32)


def as_matrix(block):
    n, rows, d = block.shape
    if rows % 16 == 0:
        return block.reshape(n * rows, d)
    return block.astype(F32).reshape(n * rows, d).astype(block.dtype)


def as_slabs(matrix, n):
    total, d = matrix.shape
    rows = total // n
    if rows % 16 == 0:
        return matrix.astype(BF).reshape(n, rows, d)
    return matrix.reshape(n, rows, d).astype(BF)


def normed(v):
    mean = jnp.mean(v, axis=-1, keepdims=True)
    centered = v - mean
    var = jnp.mean(centered * centered, axis=-1, keepdims=True)
    inv = lax.rsqrt(var + EPS)
    return centered * inv, inv


def pair_lanes(p):
    return pl.ds(pl.multiple_of(p * 128, 128), 128)


def softmax_rows(q_half, k2, bias_ref):
    scores = dot_nt(q_half, k2) + bias_ref[...]
    top = jnp.max(scores, axis=1, keepdims=True)
    raw = jnp.exp(scores - top)
    return raw * (1.0 / jnp.sum(raw, axis=1, keepdims=True))


def gather_kernel(
    wide,
    narrow,
    kinds_ref,
    kinds_vec_ref,
    act_ref,
    cot_ref,
    wq_ref,
    wk_ref,
    wv_ref,
    wo_ref,
    g1_ref,
    b1_ref,
    bq_ref,
    bv_ref,
    bo_ref,
    g2_ref,
    b2_ref,
    bd_ref,
    bu_ref,
    up_full_ref,
    down_ref,
    ap_ref,
    g_ref,
    tn_ref,
    tc_ref,
    kg_ref,
    h1_ref,
    n1_ref,
    q_ref,
    k_ref,
    v_ref,
    heads_ref,
    vec_ref,
    ub_ref,
    xhat_ref,
    bias_ref,
    wbuf_ref,
    vbuf_ref,
    n2_ref,
    pack_ref,
    small_ref,
    up_ref,
    kpad_ref,
    ring_s,
    ring_r,
    y_s,
    y_r,
    core_s,
    core_r,
    grp_s,
    grp_r,
    fring_s,
    fring_r,
    pair_s,
    pair_r,
    tok_s,
    tok_r,
    kin_s,
    kin_r,
    loc,
):
    place = Place(wide, narrow)
    ring = place.ring
    tokens, width = act_ref.shape
    sh = width // wide
    fr = ub_ref.shape[1] // ring
    a, q, h = place.a, place.q, place.h
    pending = []

    def go(copy):
        copy.start()
        pending.append(copy)
        return copy

    for i, ref in enumerate((wq_ref, wk_ref, wv_ref, wo_ref)):
        pack_ref[i * sh : (i + 1) * sh, :] = ref[...]
    small_ref[...] = jnp.zeros(small_ref.shape, F32)
    for i, ref in enumerate((g1_ref, b1_ref, bq_ref, bv_ref, bo_ref, g2_ref, b2_ref)):
        small_ref[i : i + 1, 0:sh] = ref[...].astype(F32)
    small_ref[7:10, 0:sh] = bd_ref[...].astype(F32)
    small_ref[10:13, 0:fr] = bu_ref[...].astype(F32)
    pack_ref[4 * sh :, 0:256] = small_ref[...].astype(BF)
    pack_ref[4 * sh :, 256:] = jnp.zeros((VROWS, width - 256), BF)
    kpad_ref[...] = jnp.zeros(kpad_ref.shape, jnp.int32)
    kpad_ref[0:1, 0 : kinds_vec_ref.shape[1]] = kinds_vec_ref[...]

    place.barrier(False)

    own_pack = pltpu.make_async_copy(pack_ref, ap_ref.at[place.w], loc.at[0])
    own_pack.start()

    def slab_copies(s):
        mine = place.back(s) * GROUP + q
        return mine

    def pack_ring(s):
        mine = slab_copies(s)
        src = pack_ref if s == 0 else ap_ref.at[mine]
        return remote(src, ap_ref.at[mine], ring_s, ring_r, s, place.ring_next())

    def pack_y(s):
        mine = slab_copies(s)
        src = pack_ref if s == 0 else ap_ref.at[mine]
        return remote(src, ap_ref.at[mine], y_s, y_r, s, place.member(place.q_y))

    def pack_core(s):
        mine = slab_copies(s)
        src = pack_ref if s == 0 else ap_ref.at[mine]
        return remote(src, ap_ref.at[mine], core_s, core_r, s, place.member(place.q_core))

    def pack_relay(s):
        theirs = place.back(s) * GROUP + place.q_y
        slab = ap_ref.at[theirs]
        return remote(slab, slab, core_s, core_r, ring + s, place.member(place.q_core))

    ring_copies = [go(pack_ring(0))]
    y_copies = [go(pack_y(0))]
    core_copies = [go(pack_core(0))]

    for e in range(EXPERTS):
        rows = up_full_ref[e]
        for to in range(GROUP):
            parts = [
                rows[:, (j * GROUP + to) * fr : (j * GROUP + to + 1) * fr] for j in range(ring)
            ]
            up_ref[to, e] = jnp.concatenate(parts, axis=1)

    def group_send(r, to):
        return remote(
            up_ref.at[to],
            g_ref.at[0, :, place.a * GROUP + q],
            grp_s,
            grp_r,
            r,
            place.member(to),
        )

    own_up = pltpu.make_async_copy(up_ref.at[q], g_ref.at[0, :, place.w], loc.at[1])
    own_down = pltpu.make_async_copy(
        down_ref, g_ref.at[1, :, pl.ds(a * GROUP, GROUP)], loc.at[10]
    )
    others = (place.q_core, place.q_y, place.q_diag)

    group_copies = [go(group_send(r, others[r])) for r in range(3)]
    own_up.start()
    own_down.start()

    own_kinds = pltpu.make_async_copy(kpad_ref, kg_ref.at[q], loc.at[2])
    own_kinds.start()
    kind_copies = [
        go(remote(kpad_ref, kg_ref.at[q], kin_s, kin_r, r, place.member(others[r])))
        for r in range(3)
    ]

    xhat, _ = normed(act_ref[...].astype(F32))
    xhat_ref[...] = xhat
    bounds = item_bounds(lambda i: kinds_ref[0, i], kinds_ref.shape[1])
    fill_bias(bias_ref, bounds)

    def fslab(s, e):
        return g_ref.at[h, e, pl.ds(place.back(s) * GROUP, GROUP)]

    def fring(s, e):
        slab = fslab(s, e)
        return remote(slab, slab, fring_s, fring_r, s * EXPERTS + e, place.ring_next())

    def fpair(s, e):
        slab = fslab(s, e)
        return remote(slab, slab, pair_s, pair_r, s * EXPERTS + e, place.pair())

    fring_copies = {}
    pair_copies = []

    def expert_service(s):
        for e in range(EXPERTS):
            if s > 0:
                fring_copies[s - 1, e].wait_recv()
            if s < ring - 1:
                fring_copies[s, e] = go(fring(s, e))
            if s > 0:
                pair_copies.append(go(fpair(s, e)))

    def pack_service(s):
        ring_copies[s - 1].wait_recv()
        if s < ring - 1:
            ring_copies.append(go(pack_ring(s)))
        y_copies.append(go(pack_y(s)))
        core_copies.append(go(pack_core(s)))

    for s in range(1, ring - 1):
        pack_service(s)
    for copy in group_copies:
        copy.wait_recv()
    own_up.wait()
    own_down.wait()
    expert_service(0)
    pack_service(ring - 1)

    relay_copies = []
    for s in range(ring):
        y_copies[s].wait_recv()
        relay_copies.append(go(pack_relay(s)))
    for copy in core_copies:
        copy.wait_recv()
    for copy in relay_copies:
        copy.wait_recv()
    own_pack.wait()

    def load_weight(i):
        return pltpu.make_async_copy(
            ap_ref.at[:, pl.ds(i * sh, sh), :], wbuf_ref.at[i], loc.at[3 + i]
        )

    load_vec = pltpu.make_async_copy(
        ap_ref.at[:, pl.ds(4 * sh, VROWS), pl.ds(0, 256)], vbuf_ref, loc.at[7]
    )
    load_vec.start()
    loads = [load_weight(i) for i in range(4)]
    for load in loads:
        load.start()

    def token_copies(src_own, ref, base):
        own = remote(src_own, ref.at[q], tok_s, tok_r, base, place.member(place.q_y))
        core = remote(src_own, ref.at[q], tok_s, tok_r, base + 1, place.member(place.q_core))
        far = ref.at[place.q_y]
        relay = remote(far, far, tok_s, tok_r, base + 2, place.member(place.q_core))
        return own, core, relay

    own_cot = pltpu.make_async_copy(cot_ref, tc_ref.at[q], loc.at[8])
    own_cot.start()
    cot_y, cot_core, cot_relay = token_copies(cot_ref, tc_ref, 0)
    go(cot_y)
    go(cot_core)

    expert_service(1)
    load_vec.wait()
    vec_ref[...] = jnp.concatenate([vbuf_ref[w][:, :sh] for w in range(wide)], axis=1).astype(F32)
    ub_ref[...] = jnp.concatenate(
        [vbuf_ref[j * GROUP + q][:, :fr] for j in range(ring)], axis=1
    ).astype(F32)

    n1_ref[...] = (xhat_ref[...] * vec_ref[0:1, :] + vec_ref[1:2, :]).astype(BF)
    loads[0].wait()
    q_ref[...] = (dot(n1_ref[...], as_matrix(wbuf_ref[0])) + vec_ref[2:3, :]).astype(BF)
    loads[1].wait()
    k_ref[...] = dot(n1_ref[...], as_matrix(wbuf_ref[1])).astype(BF)
    loads[2].wait()
    v_ref[...] = (dot(n1_ref[...], as_matrix(wbuf_ref[2])) + vec_ref[3:4, :]).astype(BF)
    loads[3].wait()

    pairs = width // 128
    low = lax.broadcasted_iota(jnp.int32, (tokens, 128), 1) < 64

    def attend(p, carry):
        lanes = pair_lanes(p)
        q2, k2, v2 = q_ref[:, lanes] * 0.125, k_ref[:, lanes], v_ref[:, lanes]
        zero = jnp.zeros_like(q2)
        first = softmax_rows(jnp.where(low, q2, zero), k2, bias_ref).astype(BF)
        out_low = dot(first, v2)
        second = softmax_rows(jnp.where(low, zero, q2), k2, bias_ref).astype(BF)
        out_high = dot(second, v2)
        heads_ref[:, lanes] = jnp.where(low, out_low, out_high).astype(BF)
        return carry

    lax.fori_loop(0, pairs, attend, 0)

    inside = lax.broadcasted_iota(jnp.int32, (tokens, 1), 0) < bounds[-1][2]
    attn = dot(heads_ref[...], as_matrix(wbuf_ref[3])) + vec_ref[4:5, :]
    h1 = act_ref[...].astype(F32) + jnp.where(inside, attn, 0.0)
    h1_ref[...] = h1
    xhat2, _ = normed(h1)
    n2_ref[...] = (xhat2 * vec_ref[5:6, :] + vec_ref[6:7, :]).astype(BF)

    own_n2 = pltpu.make_async_copy(n2_ref, tn_ref.at[q], loc.at[9])
    own_n2.start()
    n2_y, n2_core, n2_relay = token_copies(n2_ref, tn_ref, 3)
    go(n2_y)
    go(n2_core)
    cot_y.wait_recv()
    go(cot_relay)
    for s in range(2, ring - 1):
        expert_service(s)
    n2_y.wait_recv()
    go(n2_relay)
    expert_service(ring - 1)
    cot_core.wait_recv()
    cot_relay.wait_recv()
    n2_core.wait_recv()
    n2_relay.wait_recv()
    for copy in kind_copies:
        copy.wait_recv()
    for copy in pair_copies:
        copy.wait_recv()
    for copy in pending:
        copy.wait_send()
    own_kinds.wait()
    own_cot.wait()
    own_n2.wait()


def expert_kernel(
    per_member,
    kinds_ref,
    n2_ref,
    cot_ref,
    g_ref,
    ub_ref,
    y_ref,
    gn_ref,
    dw_ref,
    dub_ref,
    acc_ref,
    pre_ref,
    ga_ref,
):
    step = pl.program_id(0)
    rows = n2_ref.shape[0]
    member = lax.div(step, per_member)
    row0 = lax.rem(step, per_member) * rows
    bounds = item_bounds(lambda i: kinds_ref[member, 0, i], 8)
    position = lax.broadcasted_iota(jnp.int32, (rows, 1), 0) + row0
    expert = expert_of(position, bounds)
    present = []
    for e in range(EXPERTS):
        here = False
        for kind, start, end in bounds:
            here = here | ((kind == e) & (start < row0 + rows) & (end > row0) & (end > start))
        present.append(here)

    @pl.when(step == 0)
    def _():
        acc_ref[...] = jnp.zeros(acc_ref.shape, F32)
        dub_ref[...] = jnp.zeros(dub_ref.shape, F32)

    pre_ref[...] = jnp.zeros(pre_ref.shape, F32)
    ga_ref[...] = jnp.zeros(ga_ref.shape, F32)
    for e in range(EXPERTS):

        @pl.when(present[e])
        def _(e=e):
            mine = expert == e
            pre = dot(n2_ref[...], g_ref[0, e]) + ub_ref[10 + e : 11 + e, :]
            pre_ref[...] = jnp.where(mine, pre, pre_ref[...])
            ga = dot_nt(cot_ref[...], g_ref[1, e])
            ga_ref[...] = jnp.where(mine, ga, ga_ref[...])

    pre = pre_ref[...]
    half_cdf = 0.5 + 0.5 * lax.erf(pre * 0.7071067811865476)
    act = (pre * half_cdf).astype(BF)
    slope = half_cdf + pre * (0.3989422804014327 * jnp.exp(-0.5 * pre * pre))
    grad_pre = (ga_ref[...] * slope).astype(BF)

    y_ref[...] = jnp.zeros(y_ref.shape, BF)
    gn_ref[...] = jnp.zeros(gn_ref.shape, BF)
    for e in range(EXPERTS):

        @pl.when(present[e])
        def _(e=e):
            mine = expert == e
            y_ref[...] = jnp.where(mine, dot(act, g_ref[1, e]).astype(BF), y_ref[...])
            gn_ref[...] = jnp.where(mine, dot_nt(grad_pre, g_ref[0, e]).astype(BF), gn_ref[...])
            zero = jnp.zeros_like(grad_pre)
            grad_mine = jnp.where(mine, grad_pre, zero)
            acc_ref[0, e] += dot_tn(n2_ref[...], grad_mine)
            acc_ref[1, e] += dot_tn(act, jnp.where(mine, cot_ref[...], jnp.zeros_like(cot_ref[...])))
            dub_ref[10 + e : 11 + e, :] += jnp.sum(
                grad_mine.astype(F32), axis=0, keepdims=True
            )

    @pl.when(step == pl.num_programs(0) - 1)
    def _():
        dw_ref[...] = acc_ref[...].astype(BF)


class PackSum:
    def __init__(self, place, own, core_in, y_out, y_in, hop_out, hop_in, last, sems):
        self.place = place
        self.own, self.core_in = own, core_in
        self.y_out, self.y_in = y_out, y_in
        self.hop_out, self.hop_in = hop_out, hop_in
        self.last = last
        (self.core_s, self.core_r, self.y_s, self.y_r) = sems[:4]
        (self.hop_s, self.hop_r, self.x_s, self.x_r) = sems[4:]
        self.copies = []

    def go(self, copy):
        copy.start()
        self.copies.append(copy)
        return copy

    def start(self):
        place = self.place
        self.core = {}
        for s in range(place.ring):
            d = place.back(s + 1)
            for far in (1, 0):
                yy = (1 - place.y) if far else place.y
                src = self.own.at[d * GROUP + 2 * yy + 1 - place.c]
                self.core[s, far] = self.go(
                    remote(
                        src,
                        self.core_in.at[s, far],
                        self.core_s,
                        self.core_r,
                        2 * s + far,
                        place.member(place.q_core),
                    )
                )
        self.to_y = {}
        self.hop = {}

    def load(self, ref, *index):
        return ref[index].astype(F32)

    def send_y(self, s):
        place = self.place
        d = place.back(s + 1)
        self.core[s, 1].wait_recv()
        total = self.load(self.own, d * GROUP + place.q_y) + self.load(self.core_in, s, 1)
        self.y_out[s] = total.astype(BF)
        self.to_y[s] = self.go(
            remote(
                self.y_out.at[s],
                self.y_in.at[s],
                self.y_s,
                self.y_r,
                s,
                place.member(place.q_y),
            )
        )

    def step(self, s):
        place = self.place
        d = place.back(s + 1)
        self.core[s, 0].wait_recv()
        self.to_y[s].wait_recv()
        total = self.load(self.own, d * GROUP + place.q) + self.load(self.core_in, s, 0)
        total = total + self.load(self.y_in, s)
        if s > 0:
            self.hop[s - 1].wait_recv()
            total = total + self.load(self.hop_in, s - 1)
        if s < place.ring - 1:
            self.hop_out[s] = total.astype(BF)
            self.hop[s] = self.go(
                remote(
                    self.hop_out.at[s],
                    self.hop_in.at[s],
                    self.hop_s,
                    self.hop_r,
                    s,
                    place.ring_next(),
                )
            )
        else:
            self.last[place.x] = total.astype(BF)
            self.spread = [
                self.go(
                    remote(
                        self.last.at[place.x],
                        self.last.at[place.x],
                        self.x_s,
                        self.x_r,
                        k - 1,
                        place.other_narrow(k),
                    )
                )
                for k in range(1, place.narrow)
            ]

    def finish(self):
        for copy in self.spread:
            copy.wait_recv()
        total = self.load(self.last, 0)
        for i in range(1, self.place.narrow):
            total = total + self.load(self.last, i)
        for copy in self.copies:
            copy.wait_send()
        return total


def grad_kernel(
    wide,
    narrow,
    kinds_ref,
    act_ref,
    cot_ref,
    h1_ref,
    n1_ref,
    q_ref,
    k_ref,
    v_ref,
    heads_ref,
    vec_ref,
    dub_ref,
    ap_ref,
    yp_ref,
    gnp_ref,
    dw_ref,
    mixed_ref,
    ig_ref,
    ug_ref,
    dg_ref,
    go_ref,
    gq_ref,
    gk_ref,
    gv_ref,
    vout_ref,
    tin_ref,
    town_ref,
    pin_ref,
    fout_ref,
    fin_ref,
    flast_ref,
    wbuf_ref,
    bias_ref,
    ga_ref,
    ghd_ref,
    dk_ref,
    dv_ref,
    vg_ref,
    owna_ref,
    cina_ref,
    youta_ref,
    yina_ref,
    houta_ref,
    hina_ref,
    lasta_ref,
    ownb_ref,
    cinb_ref,
    youtb_ref,
    yinb_ref,
    houtb_ref,
    hinb_ref,
    lastb_ref,
    ownv_ref,
    cinv_ref,
    youtv_ref,
    yinv_ref,
    houtv_ref,
    hinv_ref,
    lastv_ref,
    tok_s,
    tok_r,
    pair_s,
    pair_r,
    fring_s,
    fring_r,
    fx_s,
    fx_r,
    fin_s,
    fin_r,
    loc,
    *pack_sems,
):
    place = Place(wide, narrow)
    ring = place.ring
    tokens, width = act_ref.shape
    sh = width // wide
    fr = dub_ref.shape[1] // ring
    a, q, h = place.a, place.q, place.h
    pending = []

    def go(copy):
        copy.start()
        pending.append(copy)
        return copy

    place.barrier(True)

    tok = []
    for i, (ref, whose) in enumerate(
        ((gnp_ref, place.q_diag), (gnp_ref, place.q_core), (yp_ref, place.q_diag), (yp_ref, place.q_core))
    ):
        tok.append(
            go(remote(ref.at[whose], tin_ref.at[i], tok_s, tok_r, i, place.member(place.q_core)))
        )
    own_loads = []
    for i, (ref, whose) in enumerate(
        ((gnp_ref, place.q_y), (gnp_ref, q), (yp_ref, place.q_y), (yp_ref, q))
    ):
        load = pltpu.make_async_copy(ref.at[whose], town_ref.at[i], loc.at[i])
        load.start()
        own_loads.append(load)

    pairs_in = {}

    def pair_send(s):
        d = place.back(s + 1)
        for e in range(EXPERTS):
            pairs_in[s, e] = go(
                remote(
                    dw_ref.at[1 - h, e, pl.ds(d * GROUP, GROUP)],
                    pin_ref.at[s, e],
                    pair_s,
                    pair_r,
                    s * EXPERTS + e,
                    place.pair(),
                )
            )

    pair_send(0)
    mine = lax.div(place.x, 2)

    def own_slot(s):
        return flast_ref.at[mine] if s == ring - 1 else fout_ref.at[s]

    load_dw = []
    for s in range(ring):
        own = dw_ref.at[h, :, pl.ds(place.back(s + 1) * GROUP, GROUP)]
        load_dw.append(pltpu.make_async_copy(own, own_slot(s), loc.at[10 + s]))
        load_dw[s].start()
    load_w = [
        pltpu.make_async_copy(
            ap_ref.at[:, pl.ds(i * sh, sh), :], wbuf_ref.at[i % 3], loc.at[5 + i]
        )
        for i in range(4)
    ]
    for i in (3, 1, 2):
        load_w[i].start()

    fhop = {}
    flast_copies = {}

    def expert_service(s):
        load_dw[s].wait()
        slot = own_slot(s)
        for e in range(EXPERTS):
            pairs_in[s, e].wait_recv()
            total = slot[e].astype(F32) + pin_ref[s, e].astype(F32)
            if s > 0:
                fhop[s - 1, e].wait_recv()
                total = total + fin_ref[s - 1, e].astype(F32)
            slot[e] = total.astype(BF)
            if s < ring - 1:
                fhop[s, e] = go(
                    remote(
                        fout_ref.at[s, e],
                        fin_ref.at[s, e],
                        fring_s,
                        fring_r,
                        s * EXPERTS + e,
                        place.ring_next(),
                    )
                )
            else:
                for k in range(1, narrow // 2):
                    slab = flast_ref.at[mine, e]
                    flast_copies[e, k] = go(
                        remote(
                            slab,
                            slab,
                            fx_s,
                            fx_r,
                            (k - 1) * EXPERTS + e,
                            place.other_narrow(2 * k),
                        )
                    )

    def far_send(i, n):
        own_loads[i].wait()
        tok[i].wait_recv()
        town_ref[i] = (town_ref[i].astype(F32) + tin_ref[i].astype(F32)).astype(BF)
        return go(
            remote(
                town_ref.at[i], tin_ref.at[4 + n], tok_s, tok_r, 4 + n, place.member(place.q_y)
            )
        )

    far_gn = far_send(0, 0)
    bounds = item_bounds(lambda i: kinds_ref[0, i], kinds_ref.shape[1])
    fill_bias(bias_ref, bounds)
    position = lax.broadcasted_iota(jnp.int32, (tokens, 1), 0)
    expert = expert_of(position, bounds)
    inside = position < bounds[-1][2]
    vg_ref[...] = dub_ref[...]
    cot = cot_ref[...].astype(F32)
    for e in range(EXPERTS):
        vg_ref[7 + e : 8 + e, :] = jnp.sum(
            jnp.where(expert == e, cot, 0.0), axis=0, keepdims=True
        )

    pair_send(1)
    expert_service(0)
    own_loads[1].wait()
    tok[1].wait_recv()
    far_gn.wait_recv()
    far_mixed = far_send(2, 1)
    gn2 = town_ref[1].astype(F32) + tin_ref[1].astype(F32) + tin_ref[4].astype(F32)
    hat, inv = normed(h1_ref[...])
    vg_ref[5:6, :] = jnp.sum(gn2 * hat, axis=0, keepdims=True)
    vg_ref[6:7, :] = jnp.sum(gn2, axis=0, keepdims=True)
    r = gn2 * vec_ref[5:6, :]
    r_mean = jnp.mean(r, axis=-1, keepdims=True)
    rn_mean = jnp.mean(r * hat, axis=-1, keepdims=True)
    gh = cot_ref[...].astype(F32) + (r - r_mean - hat * rn_mean) * inv
    ig_ref[...] = gh
    grad_attn = jnp.where(inside, gh, 0.0).astype(BF)
    ga_ref[...] = grad_attn
    vg_ref[4:5, :] = jnp.sum(grad_attn.astype(F32), axis=0, keepdims=True)
    sum_a = PackSum(
        place,
        owna_ref,
        cina_ref,
        youta_ref,
        yina_ref,
        houta_ref,
        hina_ref,
        lasta_ref,
        pack_sems[:8],
    )
    sum_b = PackSum(
        place,
        ownb_ref,
        cinb_ref,
        youtb_ref,
        yinb_ref,
        houtb_ref,
        hinb_ref,
        lastb_ref,
        pack_sems[8:16],
    )
    sum_v = PackSum(
        place,
        ownv_ref,
        cinv_ref,
        youtv_ref,
        yinv_ref,
        houtv_ref,
        hinv_ref,
        lastv_ref,
        pack_sems[16:],
    )
    owna_ref[...] = as_slabs(dot_tn(heads_ref[...], ga_ref[...]), wide)
    sum_a.start()
    load_w[3].wait()
    ghd_ref[...] = dot_nt(ga_ref[...], as_matrix(wbuf_ref[0])).astype(BF)
    load_w[0].start()
    pair_send(2)
    for s in range(ring):
        sum_a.send_y(s)
    expert_service(1)

    low = lax.broadcasted_iota(jnp.int32, (tokens, 128), 1) < 64
    dq_ref = ga_ref

    def attend_back(p, carry):
        lanes = pair_lanes(p)
        q2, k2, v2 = q_ref[:, lanes] * 0.125, k_ref[:, lanes], v_ref[:, lanes]
        g2 = ghd_ref[:, lanes]
        zero = jnp.zeros_like(q2)
        dq, dk, dv = [], [], []
        for half in (low, jnp.logical_not(low)):
            qh = jnp.where(half, q2, zero)
            gr = jnp.where(half, g2, zero)
            probs = softmax_rows(qh, k2, bias_ref)
            grad_probs = dot_nt(gr, v2)
            inner = jnp.sum(probs * grad_probs, axis=1, keepdims=True)
            grad_scores = (probs * (grad_probs - inner)).astype(BF)
            dq.append(dot(grad_scores, k2))
            dk.append(dot_tn(grad_scores, qh))
            dv.append(dot_tn(probs.astype(BF), gr))
        dq_ref[:, lanes] = (jnp.where(low, dq[0], dq[1]) * 0.125).astype(BF)
        dk_ref[:, lanes] = (dk[0] + dk[1]).astype(BF)
        dv_ref[:, lanes] = (dv[0] + dv[1]).astype(BF)
        return carry

    pairs = width // 128
    lax.fori_loop(0, pairs // 2, attend_back, 0)
    sum_a.step(0)
    lax.fori_loop(pairs // 2, pairs, attend_back, 0)
    for s in range(3, ring):
        pair_send(s)
    expert_service(2)

    for i, ref in enumerate((dq_ref, dk_ref, dv_ref)):
        ownb_ref[:, i * sh : (i + 1) * sh, :] = as_slabs(dot_tn(n1_ref[...], ref[...]), wide)
    sum_b.start()
    sum_a.step(1)

    vg_ref[2:3, :] = jnp.sum(dq_ref[...].astype(F32), axis=0, keepdims=True)
    vg_ref[3:4, :] = jnp.sum(dv_ref[...].astype(F32), axis=0, keepdims=True)
    load_w[0].wait()
    gn1 = dot_nt(dq_ref[...], as_matrix(wbuf_ref[0]))
    load_w[1].wait()
    gn1 = gn1 + dot_nt(dk_ref[...], as_matrix(wbuf_ref[1]))
    load_w[2].wait()
    gn1 = gn1 + dot_nt(dv_ref[...], as_matrix(wbuf_ref[2]))
    for s in range(ring):
        sum_b.send_y(s)
    hat, inv = normed(act_ref[...].astype(F32))
    vg_ref[0:1, :] = jnp.sum(gn1 * hat, axis=0, keepdims=True)
    vg_ref[1:2, :] = jnp.sum(gn1, axis=0, keepdims=True)
    r = gn1 * vec_ref[0:1, :]
    r_mean = jnp.mean(r, axis=-1, keepdims=True)
    rn_mean = jnp.mean(r * hat, axis=-1, keepdims=True)
    ig_ref[...] = ig_ref[...] + (r - r_mean - hat * rn_mean) * inv

    low_vec = vg_ref[...].astype(BF)
    row = lax.broadcasted_iota(jnp.int32, (VROWS, 1), 0)

    for w in range(wide):
        small = low_vec[:, w * sh : (w + 1) * sh]
        small = jnp.concatenate([small, jnp.zeros((VROWS, 256 - sh), BF)], axis=1)
        j = w // GROUP
        large = low_vec[:, j * fr : (j + 1) * fr]
        large = jnp.concatenate([large, jnp.zeros((VROWS, 256 - fr), BF)], axis=1)
        large = jnp.where(q == w % GROUP, large, jnp.zeros_like(large))
        ownv_ref[w] = jnp.where(row < 10, small, large)
    sum_v.start()
    for s in range(ring):
        sum_v.send_y(s)

    own_loads[3].wait()
    tok[3].wait_recv()
    far_mixed.wait_recv()
    mixed = h1_ref[...] + town_ref[3].astype(F32) + tin_ref[3].astype(F32) + tin_ref[5].astype(F32)
    for e in range(EXPERTS):
        mixed = mixed + jnp.where(expert == e, vec_ref[7 + e : 8 + e, :], 0.0)
    mixed_ref[...] = mixed.astype(BF)

    sum_b.step(0)
    sum_v.step(0)
    for s in range(3, ring):
        expert_service(s)

    for copy in flast_copies.values():
        copy.wait_recv()
    if narrow > 2:
        for e in range(EXPERTS):
            total = flast_ref[0, e].astype(F32)
            for i in range(1, narrow // 2):
                total = total + flast_ref[i, e].astype(F32)
            flast_ref[0, e] = total.astype(BF)
    others = (place.q_core, place.q_y, place.q_diag)

    def piece(r, to):
        return remote(
            flast_ref.at[0, :, to], ug_ref.at[q], fin_s, fin_r, r, place.member(to)
        )

    own_piece = pltpu.make_async_copy(flast_ref.at[0, :, q], ug_ref.at[q], loc.at[9])
    own_down = pltpu.make_async_copy(flast_ref.at[0], dg_ref, loc.at[9])
    send_down = remote(flast_ref.at[0], dg_ref, fin_s, fin_r, 3, place.pair())
    send_up = remote(ug_ref, ug_ref, fin_s, fin_r, 4, place.pair())

    @pl.when(h == 0)
    def _():
        for i in range(3):
            piece(i, others[i]).start()
        own_piece.start()

    @pl.when(h == 1)
    def _():
        send_down.start()
        own_down.start()

    for s in range(1, ring):
        if s > 1:
            sum_a.step(s)
        sum_b.step(s)
        sum_v.step(s)
        if s == 1:
            @pl.when(h == 0)
            def _():
                for i in range(3):
                    piece(i, others[i]).wait_recv()
                own_piece.wait()
                send_up.start()

    go_ref[...] = sum_a.finish()

    @pl.when(h == 0)
    def _():
        for i in range(3):
            piece(i, others[i]).wait_send()
        send_up.wait_send()
        send_down.wait_recv()

    @pl.when(h == 1)
    def _():
        own_down.wait()
        send_down.wait_send()
        send_up.wait_recv()

    last = sum_b.finish()
    gq_ref[...] = last[0:sh]
    gk_ref[...] = last[sh : 2 * sh]
    gv_ref[...] = last[2 * sh : 3 * sh]
    vout_ref[...] = sum_v.finish()
    for copy in pending:
        copy.wait_send()


def output_kernel(fr, mixed_in, ig_in, ug_in, dg_in, go_in, gq_in, gk_in, gv_in, v_in, *outs):
    (mixed, ig, g1, b1, gq, bq, gk, gv, bv, go, bo, g2, b2, gu, bu, gd, bd) = outs
    sh = g1.shape[1]
    mixed[...] = mixed_in[...]
    ig[...] = ig_in[...]
    for ref, src in ((gq, gq_in), (gk, gk_in), (gv, gv_in), (go, go_in)):
        ref[...] = src[...]
    for i, ref in enumerate((g1, b1, bq, bv, bo, g2, b2)):
        ref[...] = v_in[i : i + 1, 0:sh]
    bd[...] = v_in[7:10, 0:sh]
    bu[...] = v_in[10:13, 0:fr]
    gd[...] = dg_in[...].astype(F32)
    ring = ug_in.shape[3] // fr
    for e in range(EXPERTS):
        rows = [ug_in[to, e] for to in range(GROUP)]
        parts = [
            rows[to][:, j * fr : (j + 1) * fr] for j in range(ring) for to in range(GROUP)
        ]
        gu[e] = jnp.concatenate(parts, axis=1).astype(F32)


def body(
    wide,
    narrow,
    activations,
    cotangent,
    item_kinds,
    attn_norm_gain,
    attn_norm_bias,
    query_weight,
    query_bias,
    key_weight,
    value_weight,
    value_bias,
    output_weight,
    output_bias,
    ffn_norm_gain,
    ffn_norm_bias,
    up_weight,
    up_bias,
    down_weight,
    down_bias,
):
    ring = wide // GROUP
    tokens, width = activations.shape
    sh = width // wide
    fr = down_weight.shape[1]
    hidden = fr * ring

    flat = lambda v: v.reshape(1, sh)
    down_parts = down_weight.reshape(EXPERTS, GROUP, sh, width)

    prow = 4 * sh + VROWS
    anyspace = pl.BlockSpec(memory_space=pl.ANY)
    vmem = pl.BlockSpec(memory_space=pltpu.VMEM)
    smem = pl.BlockSpec(memory_space=pltpu.SMEM)
    dma = lambda n: pltpu.SemaphoreType.DMA((max(n, 1),))
    shape = jax.ShapeDtypeStruct
    token_bf = shape((tokens, width), BF)
    fsteps = ring * EXPERTS

    (ap, g, tn, tc, kg, h1, n1, qs, ks, vs, heads, vec, ub) = pl.pallas_call(
        functools.partial(gather_kernel, wide, narrow),
        out_shape=(
            shape((wide, prow, width), BF),
            shape((2, EXPERTS, wide, sh, width), BF),
            shape((GROUP, tokens, width), BF),
            shape((GROUP, tokens, width), BF),
            shape((GROUP, 8, 128), jnp.int32),
            shape((tokens, width), F32),
            token_bf,
            token_bf,
            token_bf,
            token_bf,
            token_bf,
            shape((VROWS, width), F32),
            shape((VROWS, hidden), F32),
        ),
        in_specs=[smem] + [vmem] * 18,
        out_specs=(anyspace,) * 5 + (vmem,) * 8,
        scratch_shapes=[
            pltpu.VMEM((tokens, width), F32),
            pltpu.VMEM((tokens, tokens), F32),
            pltpu.VMEM((4, wide, sh, width), BF),
            pltpu.VMEM((wide, VROWS, 256), BF),
            pltpu.VMEM((tokens, width), BF),
            pltpu.VMEM((prow, width), BF),
            pltpu.VMEM((VROWS, 256), F32),
            pltpu.VMEM((GROUP, EXPERTS, sh, hidden), BF),
            pltpu.VMEM((8, 128), jnp.int32),
            dma(ring),
            dma(ring),
            dma(ring),
            dma(ring),
            dma(2 * ring),
            dma(2 * ring),
            dma(3),
            dma(3),
            dma(fsteps),
            dma(fsteps),
            dma(fsteps),
            dma(fsteps),
            dma(6),
            dma(6),
            dma(3),
            dma(3),
            dma(11),
        ],
        compiler_params=pltpu.CompilerParams(
            collective_id=0, has_side_effects=True, vmem_limit_bytes=VMEM_LIMIT
        ),
        name="gather_attend",
    )(
        item_kinds,
        item_kinds,
        activations,
        cotangent,
        query_weight,
        key_weight,
        value_weight,
        output_weight,
        flat(attn_norm_gain),
        flat(attn_norm_bias),
        flat(query_bias),
        flat(value_bias),
        flat(output_bias),
        flat(ffn_norm_gain),
        flat(ffn_norm_bias),
        down_bias,
        up_bias,
        up_weight,
        down_parts,
    )

    per_member = 3
    rows = tokens // per_member
    full = lambda *dims: pl.BlockSpec(
        dims, lambda i: (0,) * len(dims), pipeline_mode=pl.Buffered(1)
    )
    tile = pl.BlockSpec((rows, width), lambda i: (i, 0))
    y, gn, dw, dub = pl.pallas_call(
        functools.partial(expert_kernel, per_member),
        grid=(GROUP * per_member,),
        out_shape=(
            shape((GROUP * tokens, width), BF),
            shape((GROUP * tokens, width), BF),
            shape((2, EXPERTS, width, width), BF),
            shape((VROWS, hidden), F32),
        ),
        in_specs=[
            smem,
            tile,
            tile,
            full(2, EXPERTS, width, width),
            full(VROWS, hidden),
        ],
        out_specs=(tile, tile, full(2, EXPERTS, width, width), full(VROWS, hidden)),
        scratch_shapes=[
            pltpu.VMEM((2, EXPERTS, width, width), F32),
            pltpu.VMEM((rows, hidden), F32),
            pltpu.VMEM((rows, hidden), F32),
        ],
        compiler_params=pltpu.CompilerParams(
            dimension_semantics=("arbitrary",), vmem_limit_bytes=VMEM_LIMIT
        ),
        name="experts",
    )(
        kg,
        tn.reshape(GROUP * tokens, width),
        tc.reshape(GROUP * tokens, width),
        g.reshape(2, EXPERTS, width, width),
        ub,
    )

    def pack_scratch(rows, lanes=width):
        buf = lambda n: pltpu.VMEM((n, rows, lanes), BF)
        return [
            buf(wide),
            pltpu.VMEM((ring, 2, rows, lanes), BF),
            buf(ring),
            buf(ring),
            buf(max(ring - 1, 1)),
            buf(max(ring - 1, 1)),
            buf(narrow),
        ]

    pack_sems = [dma(2 * ring)] * 2 + [dma(ring)] * 4 + [dma(narrow - 1)] * 2
    slab = (EXPERTS, GROUP, sh, width)
    (mixed, ig, ug, dg, g_out, g_query, g_key, g_value, vout) = pl.pallas_call(
        functools.partial(grad_kernel, wide, narrow),
        out_shape=(
            token_bf,
            shape((tokens, width), F32),
            shape((GROUP, EXPERTS, sh, width), BF),
            shape(slab, BF),
            shape((sh, width), F32),
            shape((sh, width), F32),
            shape((sh, width), F32),
            shape((sh, width), F32),
            shape((VROWS, 256), F32),
        ),
        in_specs=[smem] + [vmem] * 10 + [anyspace] * 4,
        out_specs=(vmem, vmem, anyspace, anyspace) + (vmem,) * 5,
        scratch_shapes=[
            pltpu.VMEM((6, tokens, width), BF),
            pltpu.VMEM((4, tokens, width), BF),
            pltpu.VMEM((ring,) + slab[:1] + slab[1:], BF),
            pltpu.VMEM((max(ring - 1, 1),) + slab, BF),
            pltpu.VMEM((max(ring - 1, 1),) + slab, BF),
            pltpu.VMEM((max(narrow // 2, 1),) + slab, BF),
            pltpu.VMEM((3, wide, sh, width), BF),
            pltpu.VMEM((tokens, tokens), F32),
            pltpu.VMEM((tokens, width), BF),
            pltpu.VMEM((tokens, width), BF),
            pltpu.VMEM((tokens, width), BF),
            pltpu.VMEM((tokens, width), BF),
            pltpu.VMEM((VROWS, width), F32),
        ]
        + pack_scratch(sh)
        + pack_scratch(3 * sh)
        + pack_scratch(VROWS, 256)
        + [
            dma(6),
            dma(6),
            dma(fsteps),
            dma(fsteps),
            dma(fsteps),
            dma(fsteps),
            dma(EXPERTS * max(narrow // 2 - 1, 1)),
            dma(EXPERTS * max(narrow // 2 - 1, 1)),
            dma(5),
            dma(5),
            dma(10 + ring),
        ]
        + pack_sems
        + pack_sems
        + pack_sems,
        compiler_params=pltpu.CompilerParams(
            collective_id=1, has_side_effects=True, vmem_limit_bytes=VMEM_LIMIT
        ),
        name="gradients",
    )(
        item_kinds,
        activations,
        cotangent,
        h1,
        n1,
        qs,
        ks,
        vs,
        heads,
        vec,
        dub,
        ap,
        y.reshape(GROUP, tokens, width),
        gn.reshape(GROUP, tokens, width),
        dw.reshape(2, EXPERTS, wide, sh, width),
    )

    vec_shape = shape((1, sh), F32)
    mat_shape = shape((sh, width), F32)
    outs = pl.pallas_call(
        functools.partial(output_kernel, fr),
        out_shape=(
            token_bf,
            shape((tokens, width), F32),
            vec_shape,
            vec_shape,
            mat_shape,
            vec_shape,
            mat_shape,
            mat_shape,
            vec_shape,
            mat_shape,
            vec_shape,
            vec_shape,
            vec_shape,
            shape((EXPERTS, sh, GROUP * hidden), F32),
            shape((EXPERTS, fr), F32),
            shape(slab, F32),
            shape((EXPERTS, sh), F32),
        ),
        in_specs=[vmem] * 9,
        out_specs=(vmem,) * 17,
        compiler_params=pltpu.CompilerParams(vmem_limit_bytes=VMEM_LIMIT),
        name="final_outputs",
    )(mixed, ig, ug, dg, g_out, g_query, g_key, g_value, vout)
    outs = list(outs)
    for i in (2, 3, 5, 8, 10, 11, 12):
        outs[i] = outs[i].reshape(sh)
    outs[15] = outs[15].reshape(EXPERTS, fr, width)
    return tuple(outs)


def solution(mesh):
    rows = P(("wide", "narrow"), None)
    return jax.shard_map(
        functools.partial(body, mesh.shape["wide"], mesh.shape["narrow"]),
        mesh=mesh,
        in_specs=(
            rows,
            rows,
            rows,
            P("wide"),
            P("wide"),
            P("wide", None),
            P("wide"),
            P("wide", None),
            P("wide", None),
            P("wide"),
            P("wide", None),
            P("wide"),
            P("wide"),
            P("wide"),
            P(None, "wide", None),
            P(None, "wide"),
            P(None, "wide", None),
            P(None, "wide"),
        ),
        out_specs=(
            rows,
            rows,
            P("wide"),
            P("wide"),
            P("wide", None),
            P("wide"),
            P("wide", None),
            P("wide", None),
            P("wide"),
            P("wide", None),
            P("wide"),
            P("wide"),
            P("wide"),
            P(None, "wide", None),
            P(None, "wide"),
            P(None, "wide", None),
            P(None, "wide"),
        ),
        check_vma=False,
    )
```

```python
import functools

import jax
import jax.numpy as jnp
from jax import lax
from jax.experimental import pallas as pl
from jax.experimental.pallas import tpu as pltpu
from jax.sharding import PartitionSpec as P

HEADS = 12
EXPERTS = 3
IMG_LEN = 197
TXT_LEN = 64
EPS = 1e-05
MASKED = -1e30
GROUP = 4
VROWS = 16
MESH = pl.DeviceIdType.MESH
BF = jnp.bfloat16
F32 = jnp.float32
VMEM_LIMIT = 63 * 1024 * 1024


def dot(a, b):
    return lax.dot_general(a, b, (((1,), (0,)), ((), ())), preferred_element_type=F32)


def dot_nt(a, b):
    return lax.dot_general(a, b, (((1,), (1,)), ((), ())), preferred_element_type=F32)


def dot_tn(a, b):
    return lax.dot_general(a, b, (((0,), (0,)), ((), ())), preferred_element_type=F32)


class Place:
    def __init__(self, wide, narrow):
        self.wide, self.narrow = wide, narrow
        self.ring = wide // GROUP
        w = lax.axis_index("wide")
        self.x = lax.axis_index("narrow")
        self.w = w
        self.a = lax.div(w, GROUP)
        self.q = lax.rem(w, GROUP)
        self.c = lax.rem(w, 2)
        self.y = lax.div(self.q, 2)
        self.h = lax.rem(self.x, 2)
        self.q_core = 2 * self.y + 1 - self.c
        self.q_y = 2 * (1 - self.y) + self.c
        self.q_diag = 2 * (1 - self.y) + 1 - self.c
        self.next = lax.rem(self.a + 1, self.ring)
        self.prev = lax.rem(self.a + self.ring - 1, self.ring)

    def member(self, q):
        return (self.a * GROUP + q, self.x)

    def ring_next(self):
        return (self.next * GROUP + self.q, self.x)

    def ring_prev(self):
        return (self.prev * GROUP + self.q, self.x)

    def pair(self):
        return (self.w, self.x + 1 - 2 * self.h)

    def other_narrow(self, k):
        return (self.w, lax.rem(self.x + k, self.narrow))

    def back(self, s):
        return lax.rem(self.a - s + 2 * self.ring, self.ring)

    def barrier(self, narrow_all):
        sem = pltpu.get_barrier_semaphore()
        who = [self.member(self.q_core), self.member(self.q_y), self.member(self.q_diag)]
        who += [self.ring_next(), self.ring_prev()]
        if narrow_all:
            who += [self.other_narrow(k) for k in range(1, self.narrow)]
        else:
            who += [self.pair()]
        for dev in who:
            pl.semaphore_signal(sem, inc=1, device_id=dev, device_id_type=MESH)
        pl.semaphore_wait(sem, len(who))


def remote(src, dst, sends, recvs, i, dev):
    return pltpu.make_async_remote_copy(
        src_ref=src,
        dst_ref=dst,
        send_sem=sends.at[i],
        recv_sem=recvs.at[i],
        device_id=dev,
        device_id_type=MESH,
    )


def item_bounds(kinds, count):
    start = jnp.int32(0)
    bounds = []
    for i in range(count):
        kind = kinds(i)
        length = jnp.where(
            kind == 0,
            IMG_LEN,
            jnp.where(kind == 1, TXT_LEN, jnp.where(kind == 2, IMG_LEN + TXT_LEN, 0)),
        )
        bounds.append((kind, start, start + length))
        start = start + length
    return bounds


def segments(position, bounds):
    seg = jnp.zeros(position.shape, jnp.int32)
    for _, _, end in bounds:
        seg = seg + jnp.where(position >= end, 1, 0)
    return seg


def expert_of(position, bounds):
    out = jnp.full(position.shape, EXPERTS, jnp.int32)
    for kind, start, end in bounds:
        out = jnp.where((position >= start) & (position < end), kind, out)
    return out


def fill_bias(bias_ref, bounds):
    tokens = bias_ref.shape[0]
    seg_col = segments(lax.broadcasted_iota(jnp.int32, (tokens, 1), 0), bounds)
    seg_row = segments(lax.broadcasted_iota(jnp.int32, (1, tokens), 1), bounds)
    bias_ref[...] = jnp.where(seg_col == seg_row, 0.0, MASKED).astype(F32)


def as_matrix(block):
    n, rows, d = block.shape
    if rows % 16 == 0:
        return block.reshape(n * rows, d)
    return block.astype(F32).reshape(n * rows, d).astype(block.dtype)


def as_slabs(matrix, n):
    total, d = matrix.shape
    rows = total // n
    if rows % 16 == 0:
        return matrix.astype(BF).reshape(n, rows, d)
    return matrix.reshape(n, rows, d).astype(BF)


def normed(v):
    mean = jnp.mean(v, axis=-1, keepdims=True)
    centered = v - mean
    var = jnp.mean(centered * centered, axis=-1, keepdims=True)
    inv = lax.rsqrt(var + EPS)
    return centered * inv, inv


def pair_lanes(p):
    return pl.ds(pl.multiple_of(p * 128, 128), 128)


def softmax_rows(q_half, k2, bias_ref):
    scores = dot_nt(q_half, k2) + bias_ref[...]
    top = jnp.max(scores, axis=1, keepdims=True)
    raw = jnp.exp(scores - top)
    return raw * (1.0 / jnp.sum(raw, axis=1, keepdims=True))


def gather_kernel(
    wide,
    narrow,
    kinds_ref,
    kinds_vec_ref,
    act_ref,
    cot_ref,
    wq_ref,
    wk_ref,
    wv_ref,
    wo_ref,
    g1_ref,
    b1_ref,
    bq_ref,
    bv_ref,
    bo_ref,
    g2_ref,
    b2_ref,
    bd_ref,
    bu_ref,
    up_full_ref,
    down_ref,
    ap_ref,
    g_ref,
    tn_ref,
    tc_ref,
    kg_ref,
    h1_out,
    n1_out,
    q_out,
    k_out,
    v_out,
    heads_out,
    vec_ref,
    ub_ref,
    h1_ref,
    n1_ref,
    q_ref,
    k_ref,
    v_ref,
    heads_ref,
    flush,
    xhat_ref,
    bias_ref,
    wbuf_ref,
    vbuf_ref,
    n2_ref,
    pack_ref,
    small_ref,
    up_ref,
    kpad_ref,
    ring_s,
    ring_r,
    y_s,
    y_r,
    core_s,
    core_r,
    grp_s,
    grp_r,
    fring_s,
    fring_r,
    pair_s,
    pair_r,
    tok_s,
    tok_r,
    kin_s,
    kin_r,
    loc,
):
    place = Place(wide, narrow)
    ring = place.ring
    tokens, width = act_ref.shape
    sh = width // wide
    fr = ub_ref.shape[1] // ring
    a, q, h = place.a, place.q, place.h
    pending = []
    flushes = []

    def keep(i, ref, out):
        copy = pltpu.make_async_copy(ref, out, flush.at[i])
        copy.start()
        flushes.append(copy)


    def go(copy):
        copy.start()
        pending.append(copy)
        return copy

    for i, ref in enumerate((wq_ref, wk_ref, wv_ref, wo_ref)):
        pack_ref[i * sh : (i + 1) * sh, :] = ref[...]
    small_ref[...] = jnp.zeros(small_ref.shape, F32)
    for i, ref in enumerate((g1_ref, b1_ref, bq_ref, bv_ref, bo_ref, g2_ref, b2_ref)):
        small_ref[i : i + 1, 0:sh] = ref[...].astype(F32)
    small_ref[7:10, 0:sh] = bd_ref[...].astype(F32)
    small_ref[10:13, 0:fr] = bu_ref[...].astype(F32)
    pack_ref[4 * sh :, 0:256] = small_ref[...].astype(BF)
    pack_ref[4 * sh :, 256:] = jnp.zeros((VROWS, width - 256), BF)
    kpad_ref[...] = jnp.zeros(kpad_ref.shape, jnp.int32)
    kpad_ref[0:1, 0 : kinds_vec_ref.shape[1]] = kinds_vec_ref[...]

    place.barrier(False)

    own_pack = pltpu.make_async_copy(pack_ref, ap_ref.at[place.w], loc.at[0])
    own_pack.start()

    def slab_copies(s):
        mine = place.back(s) * GROUP + q
        return mine

    def pack_ring(s):
        mine = slab_copies(s)
        src = pack_ref if s == 0 else ap_ref.at[mine]
        return remote(src, ap_ref.at[mine], ring_s, ring_r, s, place.ring_next())

    def pack_y(s):
        mine = slab_copies(s)
        src = pack_ref if s == 0 else ap_ref.at[mine]
        return remote(src, ap_ref.at[mine], y_s, y_r, s, place.member(place.q_y))

    def pack_core(s):
        mine = slab_copies(s)
        src = pack_ref if s == 0 else ap_ref.at[mine]
        return remote(src, ap_ref.at[mine], core_s, core_r, s, place.member(place.q_core))

    def pack_relay(s):
        theirs = place.back(s) * GROUP + place.q_y
        slab = ap_ref.at[theirs]
        return remote(slab, slab, core_s, core_r, ring + s, place.member(place.q_core))

    ring_copies = [go(pack_ring(0))]
    y_copies = [go(pack_y(0))]
    core_copies = [go(pack_core(0))]

    for e in range(EXPERTS):
        rows = up_full_ref[e]
        for to in range(GROUP):
            parts = [
                rows[:, (j * GROUP + to) * fr : (j * GROUP + to + 1) * fr] for j in range(ring)
            ]
            up_ref[to, e] = jnp.concatenate(parts, axis=1)

    def group_send(r, to):
        return remote(
            up_ref.at[to],
            g_ref.at[0, :, place.a * GROUP + q],
            grp_s,
            grp_r,
            r,
            place.member(to),
        )

    own_up = pltpu.make_async_copy(up_ref.at[q], g_ref.at[0, :, place.w], loc.at[1])
    own_down = pltpu.make_async_copy(
        down_ref, g_ref.at[1, :, pl.ds(a * GROUP, GROUP)], loc.at[10]
    )
    others = (place.q_core, place.q_y, place.q_diag)

    group_copies = [go(group_send(r, others[r])) for r in range(3)]
    own_up.start()
    own_down.start()

    own_kinds = pltpu.make_async_copy(kpad_ref, kg_ref.at[q], loc.at[2])
    own_kinds.start()
    kind_copies = [
        go(remote(kpad_ref, kg_ref.at[q], kin_s, kin_r, r, place.member(others[r])))
        for r in range(3)
    ]

    xhat, _ = normed(act_ref[...].astype(F32))
    xhat_ref[...] = xhat
    bounds = item_bounds(lambda i: kinds_ref[0, i], kinds_ref.shape[1])
    fill_bias(bias_ref, bounds)

    def fslab(s, e):
        return g_ref.at[h, e, pl.ds(place.back(s) * GROUP, GROUP)]

    def fring(s, e):
        slab = fslab(s, e)
        return remote(slab, slab, fring_s, fring_r, s * EXPERTS + e, place.ring_next())

    def fpair(s, e):
        slab = fslab(s, e)
        return remote(slab, slab, pair_s, pair_r, s * EXPERTS + e, place.pair())

    fring_copies = {}
    pair_copies = []

    def expert_service(s, chunks=range(EXPERTS)):
        for e in chunks:
            if s > 0:
                fring_copies[s - 1, e].wait_recv()
            if s < ring - 1:
                fring_copies[s, e] = go(fring(s, e))
            if s > 0:
                pair_copies.append(go(fpair(s, e)))

    def pack_service(s):
        ring_copies[s - 1].wait_recv()
        if s < ring - 1:
            ring_copies.append(go(pack_ring(s)))
        y_copies.append(go(pack_y(s)))
        core_copies.append(go(pack_core(s)))

    for s in range(1, ring - 1):
        pack_service(s)
    for copy in group_copies:
        copy.wait_recv()
    own_up.wait()
    own_down.wait()
    expert_service(0)
    pack_service(ring - 1)

    relay_copies = []
    for s in range(ring):
        y_copies[s].wait_recv()
        relay_copies.append(go(pack_relay(s)))
    for copy in core_copies:
        copy.wait_recv()
    for copy in relay_copies:
        copy.wait_recv()
    own_pack.wait()

    def load_weight(i):
        return pltpu.make_async_copy(
            ap_ref.at[:, pl.ds(i * sh, sh), :], wbuf_ref.at[i], loc.at[3 + i]
        )

    load_vec = pltpu.make_async_copy(
        ap_ref.at[:, pl.ds(4 * sh, VROWS), pl.ds(0, 256)], vbuf_ref, loc.at[7]
    )
    load_vec.start()
    loads = [load_weight(i) for i in range(4)]
    for load in loads:
        load.start()

    def token_copies(src_own, ref, base):
        own = remote(src_own, ref.at[q], tok_s, tok_r, base, place.member(place.q_y))
        core = remote(src_own, ref.at[q], tok_s, tok_r, base + 1, place.member(place.q_core))
        far = ref.at[place.q_y]
        relay = remote(far, far, tok_s, tok_r, base + 2, place.member(place.q_core))
        return own, core, relay

    own_cot = pltpu.make_async_copy(cot_ref, tc_ref.at[q], loc.at[8])
    own_cot.start()
    cot_y, cot_core, cot_relay = token_copies(cot_ref, tc_ref, 0)
    go(cot_y)
    go(cot_core)

    expert_service(1)
    load_vec.wait()
    vec_ref[...] = jnp.concatenate([vbuf_ref[w][:, :sh] for w in range(wide)], axis=1).astype(F32)
    ub_ref[...] = jnp.concatenate(
        [vbuf_ref[j * GROUP + q][:, :fr] for j in range(ring)], axis=1
    ).astype(F32)

    n1_ref[...] = (xhat_ref[...] * vec_ref[0:1, :] + vec_ref[1:2, :]).astype(BF)
    loads[0].wait()
    q_ref[...] = (dot(n1_ref[...], as_matrix(wbuf_ref[0])) + vec_ref[2:3, :]).astype(BF)
    loads[1].wait()
    k_ref[...] = dot(n1_ref[...], as_matrix(wbuf_ref[1])).astype(BF)
    loads[2].wait()
    v_ref[...] = (dot(n1_ref[...], as_matrix(wbuf_ref[2])) + vec_ref[3:4, :]).astype(BF)
    keep(0, n1_ref, n1_out)
    keep(1, q_ref, q_out)
    keep(2, k_ref, k_out)
    keep(3, v_ref, v_out)
    loads[3].wait()

    pairs = width // 128
    low = lax.broadcasted_iota(jnp.int32, (tokens, 128), 1) < 64

    def attend(p, carry):
        lanes = pair_lanes(p)
        q2, k2, v2 = q_ref[:, lanes] * 0.125, k_ref[:, lanes], v_ref[:, lanes]
        zero = jnp.zeros_like(q2)
        first = softmax_rows(jnp.where(low, q2, zero), k2, bias_ref).astype(BF)
        out_low = dot(first, v2)
        second = softmax_rows(jnp.where(low, zero, q2), k2, bias_ref).astype(BF)
        out_high = dot(second, v2)
        heads_ref[:, lanes] = jnp.where(low, out_low, out_high).astype(BF)
        return carry

    lax.fori_loop(0, pairs, attend, 0)

    inside = lax.broadcasted_iota(jnp.int32, (tokens, 1), 0) < bounds[-1][2]
    attn = dot(heads_ref[...], as_matrix(wbuf_ref[3])) + vec_ref[4:5, :]
    h1 = act_ref[...].astype(F32) + jnp.where(inside, attn, 0.0)
    h1_ref[...] = h1
    keep(4, heads_ref, heads_out)
    keep(5, h1_ref, h1_out)
    xhat2, _ = normed(h1)
    n2_ref[...] = (xhat2 * vec_ref[5:6, :] + vec_ref[6:7, :]).astype(BF)

    own_n2 = pltpu.make_async_copy(n2_ref, tn_ref.at[q], loc.at[9])
    own_n2.start()
    n2_y, n2_core, n2_relay = token_copies(n2_ref, tn_ref, 3)
    go(n2_y)
    go(n2_core)
    for s in range(2, ring - 2):
        expert_service(s)
    expert_service(ring - 2)
    cot_y.wait_recv()
    go(cot_relay)
    n2_y.wait_recv()
    go(n2_relay)
    expert_service(ring - 1)
    cot_core.wait_recv()
    cot_relay.wait_recv()
    n2_core.wait_recv()
    n2_relay.wait_recv()
    for copy in kind_copies:
        copy.wait_recv()
    for copy in pair_copies:
        copy.wait_recv()
    for copy in pending:
        copy.wait_send()
    own_kinds.wait()
    for copy in flushes:
        copy.wait()
    own_cot.wait()
    own_n2.wait()


def expert_kernel(
    per_member,
    tiles,
    kinds_ref,
    n2_ref,
    cot_ref,
    g_ref,
    ub_ref,
    y_ref,
    gn_ref,
    dw_ref,
    dub_ref,
    acc_ref,
):
    step = pl.program_id(0)
    working = step < tiles
    rows = n2_ref.shape[0]
    tile = jnp.minimum(step, tiles - 1)
    member = lax.div(tile, per_member)
    row0 = lax.rem(tile, per_member) * rows
    bounds = item_bounds(lambda i: kinds_ref[member, 0, i], 8)
    position = lax.broadcasted_iota(jnp.int32, (rows, 1), 0) + row0
    present = []
    for e in range(EXPERTS):
        here = False
        for kind, start, end in bounds:
            here = here | ((kind == e) & (start < row0 + rows) & (end > row0) & (end > start))
        present.append(here)
    count = sum(here.astype(jnp.int32) for here in present)
    @pl.when(step == 0)
    def _():
        acc_ref[...] = jnp.zeros(acc_ref.shape, F32)
        dub_ref[...] = jnp.zeros(dub_ref.shape, F32)

    def run(which):
        expert = expert_of(position, bounds)
        masks = [expert == e for e in which]
        mine = functools.reduce(jnp.logical_or, masks)
        n2, cot = n2_ref[...], cot_ref[...]

        def merged(product):
            out = product(which[0])
            for e, mask in zip(which[1:], masks[1:]):
                out = jnp.where(mask, product(e), out)
            return out

        def bias(e):
            later = jnp.where(e == 1, ub_ref[11:12, :], ub_ref[12:13, :])
            return jnp.where(e == 0, ub_ref[10:11, :], later)

        pre = merged(lambda e: dot(n2, g_ref[e]) + bias(e))
        ga = merged(lambda e: dot_nt(cot, g_ref[EXPERTS + e]))
        half_cdf = 0.5 + 0.5 * lax.erf(pre * 0.7071067811865476)
        slope = half_cdf + pre * (0.3989422804014327 * jnp.exp(-0.5 * pre * pre))
        act = (pre * half_cdf).astype(BF)
        grad = jnp.where(mine, ga * slope, 0.0).astype(BF)
        out = merged(lambda e: dot(act, g_ref[EXPERTS + e]))
        y_ref[...] = jnp.where(mine, out, 0.0).astype(BF)
        gn_ref[...] = merged(lambda e: dot_nt(grad, g_ref[e])).astype(BF)
        for e, mask in zip(which, masks):
            part = grad if len(which) == 1 else jnp.where(mask, grad, jnp.zeros_like(grad))
            acc_ref[e] += dot_tn(n2, part)
            acc_ref[EXPERTS + e] += dot_tn(act, jnp.where(mask, cot, jnp.zeros_like(cot)))
            total = jnp.sum(part.astype(F32), axis=0, keepdims=True)
            for i in range(EXPERTS):
                dub_ref[10 + i : 11 + i, :] += jnp.where(e == i, total, 0.0)

    lowest = jnp.where(present[0], 0, jnp.where(present[1], 1, 2))
    highest = jnp.where(present[2], 2, jnp.where(present[1], 1, 0))

    @pl.when(working & (count == 1))
    def _():
        run((lowest,))

    @pl.when(working & (count == 2))
    def _():
        run((lowest, highest))

    @pl.when(working & (count == 3))
    def _():
        run((0, 1, 2))

    @pl.when(working & (count == 0))
    def _():
        y_ref[...] = jnp.zeros(y_ref.shape, BF)
        gn_ref[...] = jnp.zeros(gn_ref.shape, BF)

    @pl.when(jnp.logical_not(working))
    def _():
        dw_ref[0] = acc_ref[step - tiles].astype(BF)


class PackSum:
    def __init__(self, place, own, core_in, y_out, y_in, hop_out, hop_in, last, sems):
        self.place = place
        self.own, self.core_in = own, core_in
        self.y_out, self.y_in = y_out, y_in
        self.hop_out, self.hop_in = hop_out, hop_in
        self.last = last
        (self.core_s, self.core_r, self.y_s, self.y_r) = sems[:4]
        (self.hop_s, self.hop_r, self.x_s, self.x_r) = sems[4:]
        self.copies = []

    def go(self, copy):
        copy.start()
        self.copies.append(copy)
        return copy

    def start(self):
        place = self.place
        self.core = {}
        for s in range(place.ring):
            d = place.back(s + 1)
            for far in (1, 0):
                yy = (1 - place.y) if far else place.y
                src = self.own.at[d * GROUP + 2 * yy + 1 - place.c]
                self.core[s, far] = self.go(
                    remote(
                        src,
                        self.core_in.at[s, far],
                        self.core_s,
                        self.core_r,
                        2 * s + far,
                        place.member(place.q_core),
                    )
                )
        self.to_y = {}
        self.hop = {}

    def load(self, ref, *index):
        return ref[index].astype(F32)

    def send_y(self, s):
        place = self.place
        d = place.back(s + 1)
        self.core[s, 1].wait_recv()
        total = self.load(self.own, d * GROUP + place.q_y) + self.load(self.core_in, s, 1)
        self.y_out[s] = total.astype(BF)
        self.to_y[s] = self.go(
            remote(
                self.y_out.at[s],
                self.y_in.at[s],
                self.y_s,
                self.y_r,
                s,
                place.member(place.q_y),
            )
        )

    def step(self, s):
        place = self.place
        d = place.back(s + 1)
        self.core[s, 0].wait_recv()
        self.to_y[s].wait_recv()
        total = self.load(self.own, d * GROUP + place.q) + self.load(self.core_in, s, 0)
        total = total + self.load(self.y_in, s)
        if s > 0:
            self.hop[s - 1].wait_recv()
            total = total + self.load(self.hop_in, s - 1)
        if s < place.ring - 1:
            self.hop_out[s] = total.astype(BF)
            self.hop[s] = self.go(
                remote(
                    self.hop_out.at[s],
                    self.hop_in.at[s],
                    self.hop_s,
                    self.hop_r,
                    s,
                    place.ring_next(),
                )
            )
        else:
            self.last[place.x] = total.astype(BF)
            self.spread = [
                self.go(
                    remote(
                        self.last.at[place.x],
                        self.last.at[place.x],
                        self.x_s,
                        self.x_r,
                        k - 1,
                        place.other_narrow(k),
                    )
                )
                for k in range(1, place.narrow)
            ]

    def finish(self):
        for copy in self.spread:
            copy.wait_recv()
        total = self.load(self.last, 0)
        for i in range(1, self.place.narrow):
            total = total + self.load(self.last, i)
        for copy in self.copies:
            copy.wait_send()
        return total


def grad_kernel(
    wide,
    narrow,
    kinds_ref,
    act_in,
    cot_in,
    h1_in,
    n1_in,
    q_in,
    k_in,
    v_in,
    heads_in,
    vec_ref,
    dub_ref,
    ap_ref,
    yp_ref,
    gnp_ref,
    dw_ref,
    mixed_ref,
    ig_ref,
    ug_ref,
    dg_ref,
    go_ref,
    gq_ref,
    gk_ref,
    gv_ref,
    vout_ref,
    act_ref,
    cot_ref,
    h1_ref,
    n1_ref,
    q_ref,
    k_ref,
    v_ref,
    heads_ref,
    arrive,
    tin_ref,
    town_ref,
    pin_ref,
    fout_ref,
    fin_ref,
    flast_ref,
    wbuf_ref,
    bias_ref,
    ga_ref,
    ghd_ref,
    dk_ref,
    dv_ref,
    vg_ref,
    owna_ref,
    cina_ref,
    youta_ref,
    yina_ref,
    houta_ref,
    hina_ref,
    lasta_ref,
    ownb_ref,
    cinb_ref,
    youtb_ref,
    yinb_ref,
    houtb_ref,
    hinb_ref,
    lastb_ref,
    ownv_ref,
    cinv_ref,
    youtv_ref,
    yinv_ref,
    houtv_ref,
    hinv_ref,
    lastv_ref,
    tok_s,
    tok_r,
    pair_s,
    pair_r,
    fring_s,
    fring_r,
    fx_s,
    fx_r,
    last_s,
    last_r,
    loc,
    *pack_sems,
):
    place = Place(wide, narrow)
    ring = place.ring
    tokens, width = act_in.shape
    sh = width // wide
    fr = dub_ref.shape[1] // ring
    a, q, h = place.a, place.q, place.h
    pending = []

    def go(copy):
        copy.start()
        pending.append(copy)
        return copy

    place.barrier(True)

    tok = []
    for i, (ref, whose) in enumerate(
        ((gnp_ref, place.q_diag), (gnp_ref, place.q_core), (yp_ref, place.q_diag), (yp_ref, place.q_core))
    ):
        tok.append(
            go(remote(ref.at[whose], tin_ref.at[i], tok_s, tok_r, i, place.member(place.q_core)))
        )
    own_loads = []
    for i, (ref, whose) in enumerate(
        ((gnp_ref, place.q_y), (gnp_ref, q), (yp_ref, place.q_y), (yp_ref, q))
    ):
        load = pltpu.make_async_copy(ref.at[whose], town_ref.at[i], loc.at[i])
        load.start()
        own_loads.append(load)

    pairs_in = {}

    def pair_send(s):
        d = place.back(s + 1)
        for e in range(EXPERTS):
            pairs_in[s, e] = go(
                remote(
                    dw_ref.at[1 - h, e, pl.ds(d * GROUP, GROUP)],
                    pin_ref.at[s, e],
                    pair_s,
                    pair_r,
                    s * EXPERTS + e,
                    place.pair(),
                )
            )

    pair_send(0)
    mine = lax.div(place.x, 2)

    def own_slot(s):
        return flast_ref.at[mine] if s == ring - 1 else fout_ref.at[s]

    load_dw = []
    for s in range(ring):
        own = dw_ref.at[h, :, pl.ds(place.back(s + 1) * GROUP, GROUP)]
        load_dw.append(pltpu.make_async_copy(own, own_slot(s), loc.at[10 + s]))
        load_dw[s].start()
    load_w = [
        pltpu.make_async_copy(
            ap_ref.at[:, pl.ds(i * sh, sh), :], wbuf_ref.at[i % 3], loc.at[5 + i]
        )
        for i in range(4)
    ]
    for i in (3, 1, 2):
        load_w[i].start()

    fhop = {}
    flast_copies = {}

    def expert_service(s, chunks=range(EXPERTS)):
        slot = own_slot(s)
        for e in chunks:
            if e == 0:
                load_dw[s].wait()
            pairs_in[s, e].wait_recv()
            total = slot[e].astype(F32) + pin_ref[s, e].astype(F32)
            if s > 0:
                fhop[s - 1, e].wait_recv()
                total = total + fin_ref[s - 1, e].astype(F32)
            slot[e] = total.astype(BF)
            if s < ring - 1:
                fhop[s, e] = go(
                    remote(
                        fout_ref.at[s, e],
                        fin_ref.at[s, e],
                        fring_s,
                        fring_r,
                        s * EXPERTS + e,
                        place.ring_next(),
                    )
                )
            else:
                for k in range(1, narrow // 2):
                    slab = flast_ref.at[mine, e]
                    flast_copies[e, k] = remote(
                        slab,
                        slab,
                        fx_s,
                        fx_r,
                        (k - 1) * EXPERTS + e,
                        place.other_narrow(2 * k),
                    )
                    flast_copies[e, k].start()

    others = (place.q_core, place.q_y, place.q_diag)

    def piece(r, e):
        return remote(
            flast_ref.at[0, e, others[r]],
            ug_ref.at[q, e],
            last_s,
            last_r,
            r * EXPERTS + e,
            place.member(others[r]),
        )

    own_piece = [
        pltpu.make_async_copy(flast_ref.at[0, e, q], ug_ref.at[q, e], loc.at[10 + ring + e])
        for e in range(EXPERTS)
    ]
    own_down = pltpu.make_async_copy(flast_ref.at[0], dg_ref, loc.at[9])
    send_down = [
        remote(flast_ref.at[0, e], dg_ref.at[e], last_s, last_r, 9 + e, place.pair())
        for e in range(EXPERTS)
    ]
    send_up = [
        remote(ug_ref.at[:, e], ug_ref.at[:, e], last_s, last_r, 12 + e, place.pair())
        for e in range(EXPERTS)
    ]

    def final_start(e):
        for k in range(1, narrow // 2):
            flast_copies[e, k].wait_recv()
            flast_copies[e, k].wait_send()
        if narrow > 2:
            total = flast_ref[0, e].astype(F32)
            for i in range(1, narrow // 2):
                total = total + flast_ref[i, e].astype(F32)
            flast_ref[0, e] = total.astype(BF)

        @pl.when(h == 0)
        def _():
            for r in range(3):
                piece(r, e).start()
            own_piece[e].start()

        @pl.when(h == 1)
        def _():
            send_down[e].start()

    def final_give(e):
        @pl.when(h == 0)
        def _():
            for r in range(3):
                piece(r, e).wait_recv()
            own_piece[e].wait()
            send_up[e].start()

    def final_finish():
        @pl.when(h == 0)
        def _():
            for e in range(EXPERTS):
                for r in range(3):
                    piece(r, e).wait_send()
                send_up[e].wait_send()
                send_down[e].wait_recv()

        @pl.when(h == 1)
        def _():
            own_down.start()
            for e in range(EXPERTS):
                send_down[e].wait_send()
                send_up[e].wait_recv()
            own_down.wait()

    def far_send(i, n):
        own_loads[i].wait()
        tok[i].wait_recv()
        town_ref[i] = (town_ref[i].astype(F32) + tin_ref[i].astype(F32)).astype(BF)
        return go(
            remote(
                town_ref.at[i], tin_ref.at[4 + n], tok_s, tok_r, 4 + n, place.member(place.q_y)
            )
        )

    kept = (
        (cot_in, cot_ref),
        (h1_in, h1_ref),
        (heads_in, heads_ref),
        (q_in, q_ref),
        (k_in, k_ref),
        (v_in, v_ref),
        (n1_in, n1_ref),
        (act_in, act_ref),
    )
    loads = [
        pltpu.make_async_copy(src, dst, arrive.at[i]) for i, (src, dst) in enumerate(kept)
    ]
    for load in loads:
        load.start()
    far_gn = far_send(0, 0)
    bounds = item_bounds(lambda i: kinds_ref[0, i], kinds_ref.shape[1])
    fill_bias(bias_ref, bounds)
    position = lax.broadcasted_iota(jnp.int32, (tokens, 1), 0)
    expert = expert_of(position, bounds)
    inside = position < bounds[-1][2]
    vg_ref[...] = dub_ref[...]
    loads[0].wait()
    cot = cot_ref[...].astype(F32)
    for e in range(EXPERTS):
        vg_ref[7 + e : 8 + e, :] = jnp.sum(
            jnp.where(expert == e, cot, 0.0), axis=0, keepdims=True
        )

    pair_send(1)
    expert_service(0)
    own_loads[1].wait()
    tok[1].wait_recv()
    far_gn.wait_recv()
    pair_send(2)
    far_mixed = far_send(2, 1)
    gn2 = town_ref[1].astype(F32) + tin_ref[1].astype(F32) + tin_ref[4].astype(F32)
    loads[1].wait()
    hat, inv = normed(h1_ref[...])
    vg_ref[5:6, :] = jnp.sum(gn2 * hat, axis=0, keepdims=True)
    vg_ref[6:7, :] = jnp.sum(gn2, axis=0, keepdims=True)
    r = gn2 * vec_ref[5:6, :]
    r_mean = jnp.mean(r, axis=-1, keepdims=True)
    rn_mean = jnp.mean(r * hat, axis=-1, keepdims=True)
    gh = cot_ref[...].astype(F32) + (r - r_mean - hat * rn_mean) * inv
    ig_ref[...] = gh
    grad_attn = jnp.where(inside, gh, 0.0).astype(BF)
    ga_ref[...] = grad_attn
    vg_ref[4:5, :] = jnp.sum(grad_attn.astype(F32), axis=0, keepdims=True)
    sum_a = PackSum(
        place,
        owna_ref,
        cina_ref,
        youta_ref,
        yina_ref,
        houta_ref,
        hina_ref,
        lasta_ref,
        pack_sems[:8],
    )
    sum_b = PackSum(
        place,
        ownb_ref,
        cinb_ref,
        youtb_ref,
        yinb_ref,
        houtb_ref,
        hinb_ref,
        lastb_ref,
        pack_sems[8:16],
    )
    sum_v = PackSum(
        place,
        ownv_ref,
        cinv_ref,
        youtv_ref,
        yinv_ref,
        houtv_ref,
        hinv_ref,
        lastv_ref,
        pack_sems[16:],
    )
    for i in range(2, 8):
        loads[i].wait()
    owna_ref[...] = as_slabs(dot_tn(heads_ref[...], ga_ref[...]), wide)
    sum_a.start()
    load_w[3].wait()
    ghd_ref[...] = dot_nt(ga_ref[...], as_matrix(wbuf_ref[0])).astype(BF)
    load_w[0].start()
    for s in range(ring):
        sum_a.send_y(s)
    expert_service(1)
    for s in range(3, ring):
        pair_send(s)

    low = lax.broadcasted_iota(jnp.int32, (tokens, 128), 1) < 64
    dq_ref = ga_ref

    def attend_back(p, carry):
        lanes = pair_lanes(p)
        q2, k2, v2 = q_ref[:, lanes] * 0.125, k_ref[:, lanes], v_ref[:, lanes]
        g2 = ghd_ref[:, lanes]
        zero = jnp.zeros_like(q2)
        dq, dk, dv = [], [], []
        for half in (low, jnp.logical_not(low)):
            qh = jnp.where(half, q2, zero)
            gr = jnp.where(half, g2, zero)
            probs = softmax_rows(qh, k2, bias_ref)
            grad_probs = dot_nt(gr, v2)
            inner = jnp.sum(probs * grad_probs, axis=1, keepdims=True)
            grad_scores = (probs * (grad_probs - inner)).astype(BF)
            dq.append(dot(grad_scores, k2))
            dk.append(dot_tn(grad_scores, qh))
            dv.append(dot_tn(probs.astype(BF), gr))
        dq_ref[:, lanes] = (jnp.where(low, dq[0], dq[1]) * 0.125).astype(BF)
        dk_ref[:, lanes] = (dk[0] + dk[1]).astype(BF)
        dv_ref[:, lanes] = (dv[0] + dv[1]).astype(BF)
        return carry

    pairs = width // 128
    lax.fori_loop(0, pairs // 2, attend_back, 0)
    sum_a.step(0)
    lax.fori_loop(pairs // 2, pairs, attend_back, 0)
    for s in range(2, ring - 2):
        expert_service(s)
    expert_service(ring - 2, (0,))

    for i, ref in enumerate((dq_ref, dk_ref, dv_ref)):
        ownb_ref[:, i * sh : (i + 1) * sh, :] = as_slabs(dot_tn(n1_ref[...], ref[...]), wide)
    sum_b.start()
    expert_service(ring - 2, (1,))
    sum_a.step(1)

    vg_ref[2:3, :] = jnp.sum(dq_ref[...].astype(F32), axis=0, keepdims=True)
    vg_ref[3:4, :] = jnp.sum(dv_ref[...].astype(F32), axis=0, keepdims=True)
    load_w[0].wait()
    gn1 = dot_nt(dq_ref[...], as_matrix(wbuf_ref[0]))
    load_w[1].wait()
    gn1 = gn1 + dot_nt(dk_ref[...], as_matrix(wbuf_ref[1]))
    load_w[2].wait()
    gn1 = gn1 + dot_nt(dv_ref[...], as_matrix(wbuf_ref[2]))
    for s in range(ring):
        sum_b.send_y(s)
    hat, inv = normed(act_ref[...].astype(F32))
    vg_ref[0:1, :] = jnp.sum(gn1 * hat, axis=0, keepdims=True)
    vg_ref[1:2, :] = jnp.sum(gn1, axis=0, keepdims=True)
    r = gn1 * vec_ref[0:1, :]
    r_mean = jnp.mean(r, axis=-1, keepdims=True)
    rn_mean = jnp.mean(r * hat, axis=-1, keepdims=True)
    ig_ref[...] = ig_ref[...] + (r - r_mean - hat * rn_mean) * inv

    low_vec = vg_ref[...].astype(BF)
    row = lax.broadcasted_iota(jnp.int32, (VROWS, 1), 0)

    for w in range(wide):
        small = low_vec[:, w * sh : (w + 1) * sh]
        small = jnp.concatenate([small, jnp.zeros((VROWS, 256 - sh), BF)], axis=1)
        j = w // GROUP
        large = low_vec[:, j * fr : (j + 1) * fr]
        large = jnp.concatenate([large, jnp.zeros((VROWS, 256 - fr), BF)], axis=1)
        large = jnp.where(q == w % GROUP, large, jnp.zeros_like(large))
        ownv_ref[w] = jnp.where(row < 10, small, large)
    sum_v.start()
    expert_service(ring - 2, (2,))
    for s in range(ring):
        sum_v.send_y(s)

    own_loads[3].wait()
    tok[3].wait_recv()
    far_mixed.wait_recv()
    mixed = h1_ref[...] + town_ref[3].astype(F32) + tin_ref[3].astype(F32) + tin_ref[5].astype(F32)
    for e in range(EXPERTS):
        mixed = mixed + jnp.where(expert == e, vec_ref[7 + e : 8 + e, :], 0.0)
    mixed_ref[...] = mixed.astype(BF)

    sum_b.step(0)
    sum_v.step(0)
    expert_service(ring - 1, (0,))
    final_start(0)
    sum_a.step(2)
    sum_b.step(1)
    sum_v.step(1)
    expert_service(ring - 1, (1,))
    final_start(1)
    final_give(0)
    expert_service(ring - 1, (2,))
    final_start(2)
    final_give(1)
    for s in range(2, ring):
        if s > 2:
            sum_a.step(s)
        sum_b.step(s)
        sum_v.step(s)
        if s == 2:
            final_give(2)
    go_ref[...] = sum_a.finish()
    final_finish()
    last = sum_b.finish()
    gq_ref[...] = last[0:sh]
    gk_ref[...] = last[sh : 2 * sh]
    gv_ref[...] = last[2 * sh : 3 * sh]
    vout_ref[...] = sum_v.finish()
    for copy in pending:
        copy.wait_send()


def output_kernel(fr, mixed_in, ig_in, ug_in, dg_in, go_in, gq_in, gk_in, gv_in, v_in, *outs):
    (mixed, ig, g1, b1, gq, bq, gk, gv, bv, go, bo, g2, b2, gu, bu, gd, bd) = outs
    sh = g1.shape[1]
    mixed[...] = mixed_in[...]
    ig[...] = ig_in[...]
    for ref, src in ((gq, gq_in), (gk, gk_in), (gv, gv_in), (go, go_in)):
        ref[...] = src[...]
    for i, ref in enumerate((g1, b1, bq, bv, bo, g2, b2)):
        ref[...] = v_in[i : i + 1, 0:sh]
    bd[...] = v_in[7:10, 0:sh]
    bu[...] = v_in[10:13, 0:fr]
    gd[...] = dg_in[...].astype(F32)
    ring = ug_in.shape[3] // fr
    for e in range(EXPERTS):
        rows = [ug_in[to, e] for to in range(GROUP)]
        parts = [
            rows[to][:, j * fr : (j + 1) * fr] for j in range(ring) for to in range(GROUP)
        ]
        gu[e] = jnp.concatenate(parts, axis=1).astype(F32)


def body(
    wide,
    narrow,
    activations,
    cotangent,
    item_kinds,
    attn_norm_gain,
    attn_norm_bias,
    query_weight,
    query_bias,
    key_weight,
    value_weight,
    value_bias,
    output_weight,
    output_bias,
    ffn_norm_gain,
    ffn_norm_bias,
    up_weight,
    up_bias,
    down_weight,
    down_bias,
):
    ring = wide // GROUP
    tokens, width = activations.shape
    sh = width // wide
    fr = down_weight.shape[1]
    hidden = fr * ring

    flat = lambda v: v.reshape(1, sh)
    down_parts = down_weight.reshape(EXPERTS, GROUP, sh, width)

    prow = 4 * sh + VROWS
    anyspace = pl.BlockSpec(memory_space=pl.ANY)
    vmem = pl.BlockSpec(memory_space=pltpu.VMEM)
    smem = pl.BlockSpec(memory_space=pltpu.SMEM)
    dma = lambda n: pltpu.SemaphoreType.DMA((max(n, 1),))
    shape = jax.ShapeDtypeStruct
    token_bf = shape((tokens, width), BF)
    fsteps = ring * EXPERTS

    (ap, g, tn, tc, kg, h1, n1, qs, ks, vs, heads, vec, ub) = pl.pallas_call(
        functools.partial(gather_kernel, wide, narrow),
        out_shape=(
            shape((wide, prow, width), BF),
            shape((2, EXPERTS, wide, sh, width), BF),
            shape((GROUP, tokens, width), BF),
            shape((GROUP, tokens, width), BF),
            shape((GROUP, 8, 128), jnp.int32),
            shape((tokens, width), F32),
            token_bf,
            token_bf,
            token_bf,
            token_bf,
            token_bf,
            shape((VROWS, width), F32),
            shape((VROWS, hidden), F32),
        ),
        in_specs=[smem] + [vmem] * 18,
        out_specs=(anyspace,) * 11 + (vmem,) * 2,
        scratch_shapes=[
            pltpu.VMEM((tokens, width), F32),
        ]
        + [pltpu.VMEM((tokens, width), BF)] * 5
        + [
            dma(6),
            pltpu.VMEM((tokens, width), F32),
            pltpu.VMEM((tokens, tokens), F32),
            pltpu.VMEM((4, wide, sh, width), BF),
            pltpu.VMEM((wide, VROWS, 256), BF),
            pltpu.VMEM((tokens, width), BF),
            pltpu.VMEM((prow, width), BF),
            pltpu.VMEM((VROWS, 256), F32),
            pltpu.VMEM((GROUP, EXPERTS, sh, hidden), BF),
            pltpu.VMEM((8, 128), jnp.int32),
            dma(ring),
            dma(ring),
            dma(ring),
            dma(ring),
            dma(2 * ring),
            dma(2 * ring),
            dma(3),
            dma(3),
            dma(fsteps),
            dma(fsteps),
            dma(fsteps),
            dma(fsteps),
            dma(6),
            dma(6),
            dma(3),
            dma(3),
            dma(11),
        ],
        compiler_params=pltpu.CompilerParams(
            collective_id=0, has_side_effects=True, vmem_limit_bytes=VMEM_LIMIT
        ),
        name="gather_attend",
    )(
        item_kinds,
        item_kinds,
        activations,
        cotangent,
        query_weight,
        key_weight,
        value_weight,
        output_weight,
        flat(attn_norm_gain),
        flat(attn_norm_bias),
        flat(query_bias),
        flat(value_bias),
        flat(output_bias),
        flat(ffn_norm_gain),
        flat(ffn_norm_bias),
        down_bias,
        up_bias,
        up_weight,
        down_parts,
    )

    per_member = 3
    rows = tokens // per_member
    full = lambda *dims: pl.BlockSpec(
        dims, lambda i: (0,) * len(dims), pipeline_mode=pl.Buffered(1)
    )
    tiles = GROUP * per_member
    tile = pl.BlockSpec((rows, width), lambda i: (jnp.minimum(i, tiles - 1), 0))
    matrix = pl.BlockSpec((1, width, width), lambda i: (jnp.maximum(i - tiles, 0), 0, 0))
    y, gn, dw, dub = pl.pallas_call(
        functools.partial(expert_kernel, per_member, tiles),
        grid=(tiles + 2 * EXPERTS,),
        out_shape=(
            shape((GROUP * tokens, width), BF),
            shape((GROUP * tokens, width), BF),
            shape((2 * EXPERTS, width, width), BF),
            shape((VROWS, hidden), F32),
        ),
        in_specs=[
            smem,
            tile,
            tile,
            full(2 * EXPERTS, width, width),
            full(VROWS, hidden),
        ],
        out_specs=(tile, tile, matrix, full(VROWS, hidden)),
        scratch_shapes=[
            pltpu.VMEM((2 * EXPERTS, width, width), F32),
        ],
        compiler_params=pltpu.CompilerParams(
            dimension_semantics=("arbitrary",), vmem_limit_bytes=VMEM_LIMIT
        ),
        name="experts",
    )(
        kg,
        tn.reshape(GROUP * tokens, width),
        tc.reshape(GROUP * tokens, width),
        g.reshape(2 * EXPERTS, width, width),
        ub,
    )

    def pack_scratch(rows, lanes=width):
        buf = lambda n: pltpu.VMEM((n, rows, lanes), BF)
        return [
            buf(wide),
            pltpu.VMEM((ring, 2, rows, lanes), BF),
            buf(ring),
            buf(ring),
            buf(max(ring - 1, 1)),
            buf(max(ring - 1, 1)),
            buf(narrow),
        ]

    pack_sems = [dma(2 * ring)] * 2 + [dma(ring)] * 4 + [dma(narrow - 1)] * 2
    slab = (EXPERTS, GROUP, sh, width)
    (mixed, ig, ug, dg, g_out, g_query, g_key, g_value, vout) = pl.pallas_call(
        functools.partial(grad_kernel, wide, narrow),
        out_shape=(
            token_bf,
            shape((tokens, width), F32),
            shape((GROUP, EXPERTS, sh, width), BF),
            shape(slab, BF),
            shape((sh, width), F32),
            shape((sh, width), F32),
            shape((sh, width), F32),
            shape((sh, width), F32),
            shape((VROWS, 256), F32),
        ),
        in_specs=[smem] + [anyspace] * 8 + [vmem] * 2 + [anyspace] * 4,
        out_specs=(vmem, vmem, anyspace, anyspace) + (vmem,) * 5,
        scratch_shapes=[
            pltpu.VMEM((tokens, width), BF),
            pltpu.VMEM((tokens, width), BF),
            pltpu.VMEM((tokens, width), F32),
        ]
        + [pltpu.VMEM((tokens, width), BF)] * 5
        + [
            dma(8),
            pltpu.VMEM((6, tokens, width), BF),
            pltpu.VMEM((4, tokens, width), BF),
            pltpu.VMEM((ring,) + slab[:1] + slab[1:], BF),
            pltpu.VMEM((max(ring - 1, 1),) + slab, BF),
            pltpu.VMEM((max(ring - 1, 1),) + slab, BF),
            pltpu.VMEM((max(narrow // 2, 1),) + slab, BF),
            pltpu.VMEM((3, wide, sh, width), BF),
            pltpu.VMEM((tokens, tokens), F32),
            pltpu.VMEM((tokens, width), BF),
            pltpu.VMEM((tokens, width), BF),
            pltpu.VMEM((tokens, width), BF),
            pltpu.VMEM((tokens, width), BF),
            pltpu.VMEM((VROWS, width), F32),
        ]
        + pack_scratch(sh)
        + pack_scratch(3 * sh)
        + pack_scratch(VROWS, 256)
        + [
            dma(6),
            dma(6),
            dma(fsteps),
            dma(fsteps),
            dma(fsteps),
            dma(fsteps),
            dma(EXPERTS * max(narrow // 2 - 1, 1)),
            dma(EXPERTS * max(narrow // 2 - 1, 1)),
            dma(15),
            dma(15),
            dma(10 + ring + EXPERTS),
        ]
        + pack_sems
        + pack_sems
        + pack_sems,
        compiler_params=pltpu.CompilerParams(
            collective_id=1, has_side_effects=True, vmem_limit_bytes=VMEM_LIMIT
        ),
        name="gradients",
    )(
        item_kinds,
        activations,
        cotangent,
        h1,
        n1,
        qs,
        ks,
        vs,
        heads,
        vec,
        dub,
        ap,
        y.reshape(GROUP, tokens, width),
        gn.reshape(GROUP, tokens, width),
        dw.reshape(2, EXPERTS, wide, sh, width),
    )

    vec_shape = shape((1, sh), F32)
    mat_shape = shape((sh, width), F32)
    outs = pl.pallas_call(
        functools.partial(output_kernel, fr),
        out_shape=(
            token_bf,
            shape((tokens, width), F32),
            vec_shape,
            vec_shape,
            mat_shape,
            vec_shape,
            mat_shape,
            mat_shape,
            vec_shape,
            mat_shape,
            vec_shape,
            vec_shape,
            vec_shape,
            shape((EXPERTS, sh, GROUP * hidden), F32),
            shape((EXPERTS, fr), F32),
            shape(slab, F32),
            shape((EXPERTS, sh), F32),
        ),
        in_specs=[vmem] * 9,
        out_specs=(vmem,) * 17,
        compiler_params=pltpu.CompilerParams(vmem_limit_bytes=VMEM_LIMIT),
        name="final_outputs",
    )(mixed, ig, ug, dg, g_out, g_query, g_key, g_value, vout)
    outs = list(outs)
    for i in (2, 3, 5, 8, 10, 11, 12):
        outs[i] = outs[i].reshape(sh)
    outs[15] = outs[15].reshape(EXPERTS, fr, width)
    return tuple(outs)


def solution(mesh):
    rows = P(("wide", "narrow"), None)
    return jax.shard_map(
        functools.partial(body, mesh.shape["wide"], mesh.shape["narrow"]),
        mesh=mesh,
        in_specs=(
            rows,
            rows,
            rows,
            P("wide"),
            P("wide"),
            P("wide", None),
            P("wide"),
            P("wide", None),
            P("wide", None),
            P("wide"),
            P("wide", None),
            P("wide"),
            P("wide"),
            P("wide"),
            P(None, "wide", None),
            P(None, "wide"),
            P(None, "wide", None),
            P(None, "wide"),
        ),
        out_specs=(
            rows,
            rows,
            P("wide"),
            P("wide"),
            P("wide", None),
            P("wide"),
            P("wide", None),
            P("wide", None),
            P("wide"),
            P("wide", None),
            P("wide"),
            P("wide"),
            P("wide"),
            P(None, "wide", None),
            P(None, "wide"),
            P(None, "wide", None),
            P(None, "wide"),
        ),
        check_vma=False,
    )
```

```python
import functools

import jax
import jax.numpy as jnp
from jax import lax
from jax.experimental import pallas as pl
from jax.experimental.pallas import tpu as pltpu
from jax.sharding import PartitionSpec as P

HEADS = 12
EXPERTS = 3
IMG_LEN = 197
TXT_LEN = 64
EPS = 1e-05
MASKED = -1e30
GROUP = 4
VROWS = 16
MESH = pl.DeviceIdType.MESH
BF = jnp.bfloat16
F32 = jnp.float32
VMEM_LIMIT = 63 * 1024 * 1024


def dot(a, b):
    return lax.dot_general(a, b, (((1,), (0,)), ((), ())), preferred_element_type=F32)


def dot_nt(a, b):
    return lax.dot_general(a, b, (((1,), (1,)), ((), ())), preferred_element_type=F32)


def dot_tn(a, b):
    return lax.dot_general(a, b, (((0,), (0,)), ((), ())), preferred_element_type=F32)


class Place:
    def __init__(self, wide, narrow):
        self.wide, self.narrow = wide, narrow
        self.ring = wide // GROUP
        w = lax.axis_index("wide")
        self.x = lax.axis_index("narrow")
        self.w = w
        self.a = lax.div(w, GROUP)
        self.q = lax.rem(w, GROUP)
        self.c = lax.rem(w, 2)
        self.y = lax.div(self.q, 2)
        self.h = lax.rem(self.x, 2)
        self.q_core = 2 * self.y + 1 - self.c
        self.q_y = 2 * (1 - self.y) + self.c
        self.q_diag = 2 * (1 - self.y) + 1 - self.c
        self.next = lax.rem(self.a + 1, self.ring)
        self.prev = lax.rem(self.a + self.ring - 1, self.ring)

    def member(self, q):
        return (self.a * GROUP + q, self.x)

    def ring_next(self):
        return (self.next * GROUP + self.q, self.x)

    def ring_prev(self):
        return (self.prev * GROUP + self.q, self.x)

    def pair(self):
        return (self.w, self.x + 1 - 2 * self.h)

    def pair_member(self, q):
        return (self.a * GROUP + q, self.x + 1 - 2 * self.h)

    def other_narrow(self, k):
        return (self.w, lax.rem(self.x + k, self.narrow))

    def back(self, s):
        return lax.rem(self.a - s + 2 * self.ring, self.ring)

    def barrier(self, narrow_all):
        sem = pltpu.get_barrier_semaphore()
        who = [self.member(self.q_core), self.member(self.q_y), self.member(self.q_diag)]
        who += [self.ring_next(), self.ring_prev()]
        if narrow_all:
            who += [self.other_narrow(k) for k in range(1, self.narrow)]
            who += [self.pair_member(m) for m in (self.q_core, self.q_y, self.q_diag)]
        else:
            who += [self.pair()]
        for dev in who:
            pl.semaphore_signal(sem, inc=1, device_id=dev, device_id_type=MESH)
        pl.semaphore_wait(sem, len(who))


def remote(src, dst, sends, recvs, i, dev):
    return pltpu.make_async_remote_copy(
        src_ref=src,
        dst_ref=dst,
        send_sem=sends.at[i],
        recv_sem=recvs.at[i],
        device_id=dev,
        device_id_type=MESH,
    )


def item_bounds(kinds, count):
    start = jnp.int32(0)
    bounds = []
    for i in range(count):
        kind = kinds(i)
        length = jnp.where(
            kind == 0,
            IMG_LEN,
            jnp.where(kind == 1, TXT_LEN, jnp.where(kind == 2, IMG_LEN + TXT_LEN, 0)),
        )
        bounds.append((kind, start, start + length))
        start = start + length
    return bounds


def segments(position, bounds):
    seg = jnp.zeros(position.shape, jnp.int32)
    for _, _, end in bounds:
        seg = seg + jnp.where(position >= end, 1, 0)
    return seg


def expert_of(position, bounds):
    out = jnp.full(position.shape, EXPERTS, jnp.int32)
    for kind, start, end in bounds:
        out = jnp.where((position >= start) & (position < end), kind, out)
    return out


def fill_bias(bias_ref, bounds):
    tokens = bias_ref.shape[0]
    seg_col = segments(lax.broadcasted_iota(jnp.int32, (tokens, 1), 0), bounds)
    seg_row = segments(lax.broadcasted_iota(jnp.int32, (1, tokens), 1), bounds)
    bias_ref[...] = jnp.where(seg_col == seg_row, 0.0, MASKED).astype(F32)


def as_matrix(block):
    n, rows, d = block.shape
    if rows % 16 == 0:
        return block.reshape(n * rows, d)
    return block.astype(F32).reshape(n * rows, d).astype(block.dtype)


def as_slabs(matrix, n):
    total, d = matrix.shape
    rows = total // n
    if rows % 16 == 0:
        return matrix.astype(BF).reshape(n, rows, d)
    return matrix.reshape(n, rows, d).astype(BF)


def normed(v):
    mean = jnp.mean(v, axis=-1, keepdims=True)
    centered = v - mean
    var = jnp.mean(centered * centered, axis=-1, keepdims=True)
    inv = lax.rsqrt(var + EPS)
    return centered * inv, inv


def pair_lanes(p):
    return pl.ds(pl.multiple_of(p * 128, 128), 128)


def softmax_rows(q_half, k2, bias_ref):
    scores = dot_nt(q_half, k2) + bias_ref[...]
    top = jnp.max(scores, axis=1, keepdims=True)
    raw = jnp.exp(scores - top)
    return raw * (1.0 / jnp.sum(raw, axis=1, keepdims=True))


def gather_kernel(
    wide,
    narrow,
    kinds_ref,
    kinds_vec_ref,
    act_ref,
    cot_ref,
    wq_ref,
    wk_ref,
    wv_ref,
    wo_ref,
    g1_ref,
    b1_ref,
    bq_ref,
    bv_ref,
    bo_ref,
    g2_ref,
    b2_ref,
    bd_ref,
    bu_ref,
    up_full_ref,
    down_ref,
    ap_ref,
    g_ref,
    tn_ref,
    tc_ref,
    kg_ref,
    h1_out,
    n1_out,
    q_out,
    k_out,
    v_out,
    heads_out,
    vec_ref,
    ub_ref,
    h1_ref,
    n1_ref,
    q_ref,
    k_ref,
    v_ref,
    heads_ref,
    flush,
    xhat_ref,
    bias_ref,
    wbuf_ref,
    vbuf_ref,
    n2_ref,
    pack_ref,
    small_ref,
    up_ref,
    kpad_ref,
    ring_s,
    ring_r,
    y_s,
    y_r,
    core_s,
    core_r,
    grp_s,
    grp_r,
    fring_s,
    fring_r,
    pair_s,
    pair_r,
    tok_s,
    tok_r,
    kin_s,
    kin_r,
    loc,
):
    place = Place(wide, narrow)
    ring = place.ring
    tokens, width = act_ref.shape
    sh = width // wide
    fr = ub_ref.shape[1] // ring
    a, q, h = place.a, place.q, place.h
    pending = []
    flushes = []

    def keep(i, ref, out):
        copy = pltpu.make_async_copy(ref, out, flush.at[i])
        copy.start()
        flushes.append(copy)


    def go(copy):
        copy.start()
        pending.append(copy)
        return copy

    for i, ref in enumerate((wq_ref, wk_ref, wv_ref, wo_ref)):
        pack_ref[i * sh : (i + 1) * sh, :] = ref[...]
    small_ref[...] = jnp.zeros(small_ref.shape, F32)
    for i, ref in enumerate((g1_ref, b1_ref, bq_ref, bv_ref, bo_ref, g2_ref, b2_ref)):
        small_ref[i : i + 1, 0:sh] = ref[...].astype(F32)
    small_ref[7:10, 0:sh] = bd_ref[...].astype(F32)
    small_ref[10:13, 0:fr] = bu_ref[...].astype(F32)
    pack_ref[4 * sh :, 0:256] = small_ref[...].astype(BF)
    pack_ref[4 * sh :, 256:] = jnp.zeros((VROWS, width - 256), BF)
    kpad_ref[...] = jnp.zeros(kpad_ref.shape, jnp.int32)
    kpad_ref[0:1, 0 : kinds_vec_ref.shape[1]] = kinds_vec_ref[...]

    place.barrier(False)

    own_pack = pltpu.make_async_copy(pack_ref, ap_ref.at[place.w], loc.at[0])
    own_pack.start()

    def slab_copies(s):
        mine = place.back(s) * GROUP + q
        return mine

    def pack_ring(s):
        mine = slab_copies(s)
        src = pack_ref if s == 0 else ap_ref.at[mine]
        return remote(src, ap_ref.at[mine], ring_s, ring_r, s, place.ring_next())

    def pack_y(s):
        mine = slab_copies(s)
        src = pack_ref if s == 0 else ap_ref.at[mine]
        return remote(src, ap_ref.at[mine], y_s, y_r, s, place.member(place.q_y))

    def pack_core(s):
        mine = slab_copies(s)
        src = pack_ref if s == 0 else ap_ref.at[mine]
        return remote(src, ap_ref.at[mine], core_s, core_r, s, place.member(place.q_core))

    def pack_relay(s):
        theirs = place.back(s) * GROUP + place.q_y
        slab = ap_ref.at[theirs]
        return remote(slab, slab, core_s, core_r, ring + s, place.member(place.q_core))

    ring_copies = [go(pack_ring(0))]
    y_copies = [go(pack_y(0))]
    core_copies = [go(pack_core(0))]

    for e in range(EXPERTS):
        rows = up_full_ref[e]
        for to in range(GROUP):
            parts = [
                rows[:, (j * GROUP + to) * fr : (j * GROUP + to + 1) * fr] for j in range(ring)
            ]
            up_ref[to, e] = jnp.concatenate(parts, axis=1)

    def group_send(r, to):
        return remote(
            up_ref.at[to],
            g_ref.at[0, :, place.a * GROUP + q],
            grp_s,
            grp_r,
            r,
            place.member(to),
        )

    own_up = pltpu.make_async_copy(up_ref.at[q], g_ref.at[0, :, place.w], loc.at[1])
    own_down = pltpu.make_async_copy(
        down_ref, g_ref.at[1, :, pl.ds(a * GROUP, GROUP)], loc.at[10]
    )
    others = (place.q_core, place.q_y, place.q_diag)

    group_copies = [go(group_send(r, others[r])) for r in range(3)]
    own_up.start()
    own_down.start()

    own_kinds = pltpu.make_async_copy(kpad_ref, kg_ref.at[q], loc.at[2])
    own_kinds.start()
    kind_copies = [
        go(remote(kpad_ref, kg_ref.at[q], kin_s, kin_r, r, place.member(others[r])))
        for r in range(3)
    ]

    xhat, _ = normed(act_ref[...].astype(F32))
    xhat_ref[...] = xhat
    bounds = item_bounds(lambda i: kinds_ref[0, i], kinds_ref.shape[1])
    fill_bias(bias_ref, bounds)

    def fslab(s, e):
        return g_ref.at[h, e, pl.ds(place.back(s) * GROUP, GROUP)]

    def fring(s, e):
        slab = fslab(s, e)
        return remote(slab, slab, fring_s, fring_r, s * EXPERTS + e, place.ring_next())

    def fpair(s, e):
        slab = fslab(s, e)
        return remote(slab, slab, pair_s, pair_r, s * EXPERTS + e, place.pair())

    fring_copies = {}
    pair_copies = []

    def expert_service(s, chunks=range(EXPERTS)):
        for e in chunks:
            if s > 0:
                fring_copies[s - 1, e].wait_recv()
            if s < ring - 1:
                fring_copies[s, e] = go(fring(s, e))
            if s > 0:
                pair_copies.append(go(fpair(s, e)))

    def pack_service(s):
        ring_copies[s - 1].wait_recv()
        if s < ring - 1:
            ring_copies.append(go(pack_ring(s)))
        y_copies.append(go(pack_y(s)))
        core_copies.append(go(pack_core(s)))

    for s in range(1, ring - 1):
        pack_service(s)
    for copy in group_copies:
        copy.wait_recv()
    own_up.wait()
    own_down.wait()
    expert_service(0)
    pack_service(ring - 1)

    relay_copies = []
    for s in range(ring):
        y_copies[s].wait_recv()
        relay_copies.append(go(pack_relay(s)))
    for copy in core_copies:
        copy.wait_recv()
    for copy in relay_copies:
        copy.wait_recv()
    own_pack.wait()

    def load_weight(i):
        return pltpu.make_async_copy(
            ap_ref.at[:, pl.ds(i * sh, sh), :], wbuf_ref.at[i], loc.at[3 + i]
        )

    load_vec = pltpu.make_async_copy(
        ap_ref.at[:, pl.ds(4 * sh, VROWS), pl.ds(0, 256)], vbuf_ref, loc.at[7]
    )
    load_vec.start()
    loads = [load_weight(i) for i in range(4)]
    for load in loads:
        load.start()

    def token_copies(src_own, ref, base):
        own = remote(src_own, ref.at[q], tok_s, tok_r, base, place.member(place.q_y))
        core = remote(src_own, ref.at[q], tok_s, tok_r, base + 1, place.member(place.q_core))
        far = ref.at[place.q_y]
        relay = remote(far, far, tok_s, tok_r, base + 2, place.member(place.q_core))
        return own, core, relay

    own_cot = pltpu.make_async_copy(cot_ref, tc_ref.at[q], loc.at[8])
    own_cot.start()
    cot_y, cot_core, cot_relay = token_copies(cot_ref, tc_ref, 0)
    go(cot_y)
    go(cot_core)

    expert_service(1)
    load_vec.wait()
    vec_ref[...] = jnp.concatenate([vbuf_ref[w][:, :sh] for w in range(wide)], axis=1).astype(F32)
    ub_ref[...] = jnp.concatenate(
        [vbuf_ref[j * GROUP + q][:, :fr] for j in range(ring)], axis=1
    ).astype(F32)

    n1_ref[...] = (xhat_ref[...] * vec_ref[0:1, :] + vec_ref[1:2, :]).astype(BF)
    loads[0].wait()
    q_ref[...] = (dot(n1_ref[...], as_matrix(wbuf_ref[0])) + vec_ref[2:3, :]).astype(BF)
    loads[1].wait()
    k_ref[...] = dot(n1_ref[...], as_matrix(wbuf_ref[1])).astype(BF)
    loads[2].wait()
    v_ref[...] = (dot(n1_ref[...], as_matrix(wbuf_ref[2])) + vec_ref[3:4, :]).astype(BF)
    keep(0, n1_ref, n1_out)
    keep(1, q_ref, q_out)
    keep(2, k_ref, k_out)
    keep(3, v_ref, v_out)
    loads[3].wait()

    pairs = width // 128
    low = lax.broadcasted_iota(jnp.int32, (tokens, 128), 1) < 64

    def attend(p, carry):
        lanes = pair_lanes(p)
        q2, k2, v2 = q_ref[:, lanes] * 0.125, k_ref[:, lanes], v_ref[:, lanes]
        zero = jnp.zeros_like(q2)
        first = softmax_rows(jnp.where(low, q2, zero), k2, bias_ref).astype(BF)
        out_low = dot(first, v2)
        second = softmax_rows(jnp.where(low, zero, q2), k2, bias_ref).astype(BF)
        out_high = dot(second, v2)
        heads_ref[:, lanes] = jnp.where(low, out_low, out_high).astype(BF)
        return carry

    lax.fori_loop(0, pairs, attend, 0)

    inside = lax.broadcasted_iota(jnp.int32, (tokens, 1), 0) < bounds[-1][2]
    attn = dot(heads_ref[...], as_matrix(wbuf_ref[3])) + vec_ref[4:5, :]
    h1 = act_ref[...].astype(F32) + jnp.where(inside, attn, 0.0)
    h1_ref[...] = h1
    keep(4, heads_ref, heads_out)
    keep(5, h1_ref, h1_out)
    xhat2, _ = normed(h1)
    n2_ref[...] = (xhat2 * vec_ref[5:6, :] + vec_ref[6:7, :]).astype(BF)

    own_n2 = pltpu.make_async_copy(n2_ref, tn_ref.at[q], loc.at[9])
    own_n2.start()
    n2_y, n2_core, n2_relay = token_copies(n2_ref, tn_ref, 3)
    go(n2_y)
    go(n2_core)
    for s in range(2, ring - 2):
        expert_service(s)
    expert_service(ring - 2)
    cot_y.wait_recv()
    go(cot_relay)
    n2_y.wait_recv()
    go(n2_relay)
    expert_service(ring - 1)
    cot_core.wait_recv()
    cot_relay.wait_recv()
    n2_core.wait_recv()
    n2_relay.wait_recv()
    for copy in kind_copies:
        copy.wait_recv()
    for copy in pair_copies:
        copy.wait_recv()
    for copy in pending:
        copy.wait_send()
    own_kinds.wait()
    for copy in flushes:
        copy.wait()
    own_cot.wait()
    own_n2.wait()


def expert_kernel(
    per_member,
    tiles,
    kinds_ref,
    n2_ref,
    cot_ref,
    g_ref,
    ub_ref,
    y_ref,
    gn_ref,
    dw_ref,
    dub_ref,
    acc_ref,
):
    step = pl.program_id(0)
    working = step < tiles
    rows = n2_ref.shape[0]
    tile = jnp.minimum(step, tiles - 1)
    member = lax.div(tile, per_member)
    row0 = lax.rem(tile, per_member) * rows
    bounds = item_bounds(lambda i: kinds_ref[member, 0, i], 8)
    position = lax.broadcasted_iota(jnp.int32, (rows, 1), 0) + row0
    present = []
    for e in range(EXPERTS):
        here = False
        for kind, start, end in bounds:
            here = here | ((kind == e) & (start < row0 + rows) & (end > row0) & (end > start))
        present.append(here)
    count = sum(here.astype(jnp.int32) for here in present)
    @pl.when(step == 0)
    def _():
        acc_ref[...] = jnp.zeros(acc_ref.shape, F32)
        dub_ref[...] = jnp.zeros(dub_ref.shape, F32)

    def run(which):
        expert = expert_of(position, bounds)
        masks = [expert == e for e in which]
        mine = functools.reduce(jnp.logical_or, masks)
        n2, cot = n2_ref[...], cot_ref[...]

        def merged(product):
            out = product(which[0])
            for e, mask in zip(which[1:], masks[1:]):
                out = jnp.where(mask, product(e), out)
            return out

        def bias(e):
            later = jnp.where(e == 1, ub_ref[11:12, :], ub_ref[12:13, :])
            return jnp.where(e == 0, ub_ref[10:11, :], later)

        pre = merged(lambda e: dot(n2, g_ref[e]) + bias(e))
        ga = merged(lambda e: dot_nt(cot, g_ref[EXPERTS + e]))
        half_cdf = 0.5 + 0.5 * lax.erf(pre * 0.7071067811865476)
        slope = half_cdf + pre * (0.3989422804014327 * jnp.exp(-0.5 * pre * pre))
        act = (pre * half_cdf).astype(BF)
        grad = jnp.where(mine, ga * slope, 0.0).astype(BF)
        out = merged(lambda e: dot(act, g_ref[EXPERTS + e]))
        y_ref[...] = jnp.where(mine, out, 0.0).astype(BF)
        gn_ref[...] = merged(lambda e: dot_nt(grad, g_ref[e])).astype(BF)
        for e, mask in zip(which, masks):
            part = grad if len(which) == 1 else jnp.where(mask, grad, jnp.zeros_like(grad))
            acc_ref[e] += dot_tn(n2, part)
            acc_ref[EXPERTS + e] += dot_tn(act, jnp.where(mask, cot, jnp.zeros_like(cot)))
            total = jnp.sum(part.astype(F32), axis=0, keepdims=True)
            for i in range(EXPERTS):
                dub_ref[10 + i : 11 + i, :] += jnp.where(e == i, total, 0.0)

    lowest = jnp.where(present[0], 0, jnp.where(present[1], 1, 2))
    highest = jnp.where(present[2], 2, jnp.where(present[1], 1, 0))

    @pl.when(working & (count == 1))
    def _():
        run((lowest,))

    @pl.when(working & (count == 2))
    def _():
        run((lowest, highest))

    @pl.when(working & (count == 3))
    def _():
        run((0, 1, 2))

    @pl.when(working & (count == 0))
    def _():
        y_ref[...] = jnp.zeros(y_ref.shape, BF)
        gn_ref[...] = jnp.zeros(gn_ref.shape, BF)

    @pl.when(jnp.logical_not(working))
    def _():
        dw_ref[0] = acc_ref[step - tiles].astype(BF)


class PackSum:
    def __init__(self, place, own, core_in, y_out, y_in, hop_out, hop_in, last, sems):
        self.place = place
        self.own, self.core_in = own, core_in
        self.y_out, self.y_in = y_out, y_in
        self.hop_out, self.hop_in = hop_out, hop_in
        self.last = last
        (self.core_s, self.core_r, self.y_s, self.y_r) = sems[:4]
        (self.hop_s, self.hop_r, self.x_s, self.x_r) = sems[4:]
        self.copies = []

    def go(self, copy):
        copy.start()
        self.copies.append(copy)
        return copy

    def start(self):
        place = self.place
        self.core = {}
        for s in range(place.ring):
            d = place.back(s + 1)
            for far in (1, 0):
                yy = (1 - place.y) if far else place.y
                src = self.own.at[d * GROUP + 2 * yy + 1 - place.c]
                self.core[s, far] = self.go(
                    remote(
                        src,
                        self.core_in.at[s, far],
                        self.core_s,
                        self.core_r,
                        2 * s + far,
                        place.member(place.q_core),
                    )
                )
        self.to_y = {}
        self.hop = {}

    def load(self, ref, *index):
        return ref[index].astype(F32)

    def send_y(self, s):
        place = self.place
        d = place.back(s + 1)
        self.core[s, 1].wait_recv()
        total = self.load(self.own, d * GROUP + place.q_y) + self.load(self.core_in, s, 1)
        self.y_out[s] = total.astype(BF)
        self.to_y[s] = self.go(
            remote(
                self.y_out.at[s],
                self.y_in.at[s],
                self.y_s,
                self.y_r,
                s,
                place.member(place.q_y),
            )
        )

    def step(self, s):
        place = self.place
        d = place.back(s + 1)
        self.core[s, 0].wait_recv()
        self.to_y[s].wait_recv()
        total = self.load(self.own, d * GROUP + place.q) + self.load(self.core_in, s, 0)
        total = total + self.load(self.y_in, s)
        if s > 0:
            self.hop[s - 1].wait_recv()
            total = total + self.load(self.hop_in, s - 1)
        if s < place.ring - 1:
            self.hop_out[s] = total.astype(BF)
            self.hop[s] = self.go(
                remote(
                    self.hop_out.at[s],
                    self.hop_in.at[s],
                    self.hop_s,
                    self.hop_r,
                    s,
                    place.ring_next(),
                )
            )
        else:
            self.last[place.x] = total.astype(BF)
            self.spread = [
                self.go(
                    remote(
                        self.last.at[place.x],
                        self.last.at[place.x],
                        self.x_s,
                        self.x_r,
                        k - 1,
                        place.other_narrow(k),
                    )
                )
                for k in range(1, place.narrow)
            ]

    def finish(self):
        for copy in self.spread:
            copy.wait_recv()
        total = self.load(self.last, 0)
        for i in range(1, self.place.narrow):
            total = total + self.load(self.last, i)
        for copy in self.copies:
            copy.wait_send()
        return total


def grad_kernel(
    wide,
    narrow,
    kinds_ref,
    act_in,
    cot_in,
    h1_in,
    n1_in,
    q_in,
    k_in,
    v_in,
    heads_in,
    vec_ref,
    dub_ref,
    ap_ref,
    yp_ref,
    gnp_ref,
    dw_ref,
    mixed_ref,
    ig_ref,
    ug_ref,
    dg_ref,
    go_ref,
    gq_ref,
    gk_ref,
    gv_ref,
    vout_ref,
    act_ref,
    cot_ref,
    h1_ref,
    n1_ref,
    q_ref,
    k_ref,
    v_ref,
    heads_ref,
    arrive,
    tin_ref,
    town_ref,
    pin_ref,
    fout_ref,
    fin_ref,
    flast_ref,
    wbuf_ref,
    bias_ref,
    ga_ref,
    ghd_ref,
    dk_ref,
    dv_ref,
    vg_ref,
    owna_ref,
    cina_ref,
    youta_ref,
    yina_ref,
    houta_ref,
    hina_ref,
    lasta_ref,
    ownb_ref,
    cinb_ref,
    youtb_ref,
    yinb_ref,
    houtb_ref,
    hinb_ref,
    lastb_ref,
    ownv_ref,
    cinv_ref,
    youtv_ref,
    yinv_ref,
    houtv_ref,
    hinv_ref,
    lastv_ref,
    tok_s,
    tok_r,
    pair_s,
    pair_r,
    fring_s,
    fring_r,
    fx_s,
    fx_r,
    last_s,
    last_r,
    loc,
    *pack_sems,
):
    place = Place(wide, narrow)
    ring = place.ring
    tokens, width = act_in.shape
    sh = width // wide
    fr = dub_ref.shape[1] // ring
    a, q, h = place.a, place.q, place.h
    pending = []

    def go(copy):
        copy.start()
        pending.append(copy)
        return copy

    place.barrier(True)

    tok = []
    for i, (ref, whose) in enumerate(
        ((gnp_ref, place.q_diag), (gnp_ref, place.q_core), (yp_ref, place.q_diag), (yp_ref, place.q_core))
    ):
        tok.append(
            go(remote(ref.at[whose], tin_ref.at[i], tok_s, tok_r, i, place.member(place.q_core)))
        )
    own_loads = []
    for i, (ref, whose) in enumerate(
        ((gnp_ref, place.q_y), (gnp_ref, q), (yp_ref, place.q_y), (yp_ref, q))
    ):
        load = pltpu.make_async_copy(ref.at[whose], town_ref.at[i], loc.at[i])
        load.start()
        own_loads.append(load)

    pairs_in = {}

    def pair_send(s):
        d = place.back(s + 1)
        for e in range(EXPERTS):
            pairs_in[s, e] = go(
                remote(
                    dw_ref.at[1 - h, e, pl.ds(d * GROUP, GROUP)],
                    pin_ref.at[s, e],
                    pair_s,
                    pair_r,
                    s * EXPERTS + e,
                    place.pair(),
                )
            )

    pair_send(0)
    mine = lax.div(place.x, 2)

    def own_slot(s):
        return flast_ref.at[mine] if s == ring - 1 else fout_ref.at[s]

    load_dw = []
    for s in range(ring):
        own = dw_ref.at[h, :, pl.ds(place.back(s + 1) * GROUP, GROUP)]
        load_dw.append(pltpu.make_async_copy(own, own_slot(s), loc.at[10 + s]))
        load_dw[s].start()
    load_w = [
        pltpu.make_async_copy(
            ap_ref.at[:, pl.ds(i * sh, sh), :], wbuf_ref.at[i % 3], loc.at[5 + i]
        )
        for i in range(4)
    ]
    for i in (3, 1, 2):
        load_w[i].start()

    fhop = {}
    flast_copies = {}

    def expert_service(s, chunks=range(EXPERTS)):
        slot = own_slot(s)
        for e in chunks:
            if e == 0:
                load_dw[s].wait()
            pairs_in[s, e].wait_recv()
            total = slot[e].astype(F32) + pin_ref[s, e].astype(F32)
            if s > 0:
                fhop[s - 1, e].wait_recv()
                total = total + fin_ref[s - 1, e].astype(F32)
            slot[e] = total.astype(BF)
            if s < ring - 1:
                fhop[s, e] = go(
                    remote(
                        fout_ref.at[s, e],
                        fin_ref.at[s, e],
                        fring_s,
                        fring_r,
                        s * EXPERTS + e,
                        place.ring_next(),
                    )
                )
            else:
                for k in range(1, narrow // 2):
                    slab = flast_ref.at[mine, e]
                    flast_copies[e, k] = remote(
                        slab,
                        slab,
                        fx_s,
                        fx_r,
                        (k - 1) * EXPERTS + e,
                        place.other_narrow(2 * k),
                    )
                    flast_copies[e, k].start()

    others = (place.q_core, place.q_y, place.q_diag)

    def piece(r, e):
        return remote(
            flast_ref.at[0, e, others[r]],
            ug_ref.at[q, e],
            last_s,
            last_r,
            r * EXPERTS + e,
            place.member(others[r]),
        )

    everyone = others + (q,)

    def far_piece(r, e):
        return remote(
            flast_ref.at[0, e, everyone[r]],
            ug_ref.at[q, e],
            last_s,
            last_r,
            (4 + r) * EXPERTS + e,
            place.pair_member(everyone[r]),
        )

    own_piece = [
        pltpu.make_async_copy(flast_ref.at[0, e, q], ug_ref.at[q, e], loc.at[10 + ring + e])
        for e in range(EXPERTS)
    ]
    own_down = pltpu.make_async_copy(flast_ref.at[0], dg_ref, loc.at[9])
    send_down = [
        remote(flast_ref.at[0, e], dg_ref.at[e], last_s, last_r, 3 * EXPERTS + e, place.pair())
        for e in range(EXPERTS)
    ]
    def final_start(e):
        for k in range(1, narrow // 2):
            flast_copies[e, k].wait_recv()
            flast_copies[e, k].wait_send()
        if narrow > 2:
            total = flast_ref[0, e].astype(F32)
            for i in range(1, narrow // 2):
                total = total + flast_ref[i, e].astype(F32)
            flast_ref[0, e] = total.astype(BF)

        @pl.when(h == 0)
        def _():
            for r in range(3):
                far_piece(r, e).start()
                piece(r, e).start()
            far_piece(3, e).start()
            own_piece[e].start()

        @pl.when(h == 1)
        def _():
            send_down[e].start()

    def final_finish():
        @pl.when(h == 0)
        def _():
            for e in range(EXPERTS):
                for r in range(3):
                    piece(r, e).wait_recv()
                    piece(r, e).wait_send()
                for r in range(4):
                    far_piece(r, e).wait_send()
                own_piece[e].wait()
                send_down[e].wait_recv()

        @pl.when(h == 1)
        def _():
            own_down.start()
            for e in range(EXPERTS):
                send_down[e].wait_send()
                for r in range(4):
                    far_piece(r, e).wait_recv()
            own_down.wait()

    def far_send(i, n):
        own_loads[i].wait()
        tok[i].wait_recv()
        town_ref[i] = (town_ref[i].astype(F32) + tin_ref[i].astype(F32)).astype(BF)
        return go(
            remote(
                town_ref.at[i], tin_ref.at[4 + n], tok_s, tok_r, 4 + n, place.member(place.q_y)
            )
        )

    kept = (
        (cot_in, cot_ref),
        (h1_in, h1_ref),
        (heads_in, heads_ref),
        (q_in, q_ref),
        (k_in, k_ref),
        (v_in, v_ref),
        (n1_in, n1_ref),
        (act_in, act_ref),
    )
    loads = [
        pltpu.make_async_copy(src, dst, arrive.at[i]) for i, (src, dst) in enumerate(kept)
    ]
    for load in loads:
        load.start()
    far_gn = far_send(0, 0)
    bounds = item_bounds(lambda i: kinds_ref[0, i], kinds_ref.shape[1])
    fill_bias(bias_ref, bounds)
    position = lax.broadcasted_iota(jnp.int32, (tokens, 1), 0)
    expert = expert_of(position, bounds)
    inside = position < bounds[-1][2]
    vg_ref[...] = dub_ref[...]
    loads[0].wait()
    cot = cot_ref[...].astype(F32)
    for e in range(EXPERTS):
        vg_ref[7 + e : 8 + e, :] = jnp.sum(
            jnp.where(expert == e, cot, 0.0), axis=0, keepdims=True
        )

    pair_send(1)
    expert_service(0)
    own_loads[1].wait()
    tok[1].wait_recv()
    far_gn.wait_recv()
    pair_send(2)
    far_mixed = far_send(2, 1)
    gn2 = town_ref[1].astype(F32) + tin_ref[1].astype(F32) + tin_ref[4].astype(F32)
    loads[1].wait()
    hat, inv = normed(h1_ref[...])
    vg_ref[5:6, :] = jnp.sum(gn2 * hat, axis=0, keepdims=True)
    vg_ref[6:7, :] = jnp.sum(gn2, axis=0, keepdims=True)
    r = gn2 * vec_ref[5:6, :]
    r_mean = jnp.mean(r, axis=-1, keepdims=True)
    rn_mean = jnp.mean(r * hat, axis=-1, keepdims=True)
    gh = cot_ref[...].astype(F32) + (r - r_mean - hat * rn_mean) * inv
    ig_ref[...] = gh
    grad_attn = jnp.where(inside, gh, 0.0).astype(BF)
    ga_ref[...] = grad_attn
    vg_ref[4:5, :] = jnp.sum(grad_attn.astype(F32), axis=0, keepdims=True)
    sum_a = PackSum(
        place,
        owna_ref,
        cina_ref,
        youta_ref,
        yina_ref,
        houta_ref,
        hina_ref,
        lasta_ref,
        pack_sems[:8],
    )
    sum_b = PackSum(
        place,
        ownb_ref,
        cinb_ref,
        youtb_ref,
        yinb_ref,
        houtb_ref,
        hinb_ref,
        lastb_ref,
        pack_sems[8:16],
    )
    sum_v = PackSum(
        place,
        ownv_ref,
        cinv_ref,
        youtv_ref,
        yinv_ref,
        houtv_ref,
        hinv_ref,
        lastv_ref,
        pack_sems[16:],
    )
    for i in range(2, 8):
        loads[i].wait()
    owna_ref[...] = as_slabs(dot_tn(heads_ref[...], ga_ref[...]), wide)
    sum_a.start()
    load_w[3].wait()
    ghd_ref[...] = dot_nt(ga_ref[...], as_matrix(wbuf_ref[0])).astype(BF)
    load_w[0].start()
    for s in range(ring):
        sum_a.send_y(s)
    expert_service(1)
    for s in range(3, ring):
        pair_send(s)

    low = lax.broadcasted_iota(jnp.int32, (tokens, 128), 1) < 64
    dq_ref = ga_ref

    def attend_back(p, carry):
        lanes = pair_lanes(p)
        q2, k2, v2 = q_ref[:, lanes] * 0.125, k_ref[:, lanes], v_ref[:, lanes]
        g2 = ghd_ref[:, lanes]
        zero = jnp.zeros_like(q2)
        dq, dk, dv = [], [], []
        for half in (low, jnp.logical_not(low)):
            qh = jnp.where(half, q2, zero)
            gr = jnp.where(half, g2, zero)
            probs = softmax_rows(qh, k2, bias_ref)
            grad_probs = dot_nt(gr, v2)
            inner = jnp.sum(probs * grad_probs, axis=1, keepdims=True)
            grad_scores = (probs * (grad_probs - inner)).astype(BF)
            dq.append(dot(grad_scores, k2))
            dk.append(dot_tn(grad_scores, qh))
            dv.append(dot_tn(probs.astype(BF), gr))
        dq_ref[:, lanes] = (jnp.where(low, dq[0], dq[1]) * 0.125).astype(BF)
        dk_ref[:, lanes] = (dk[0] + dk[1]).astype(BF)
        dv_ref[:, lanes] = (dv[0] + dv[1]).astype(BF)
        return carry

    pairs = width // 128
    lax.fori_loop(0, pairs // 2, attend_back, 0)
    sum_a.step(0)
    lax.fori_loop(pairs // 2, pairs, attend_back, 0)
    for s in range(2, ring - 2):
        expert_service(s)
    expert_service(ring - 2, (0,))

    for i, ref in enumerate((dq_ref, dk_ref, dv_ref)):
        ownb_ref[:, i * sh : (i + 1) * sh, :] = as_slabs(dot_tn(n1_ref[...], ref[...]), wide)
    sum_b.start()
    expert_service(ring - 2, (1,))
    sum_a.step(1)

    vg_ref[2:3, :] = jnp.sum(dq_ref[...].astype(F32), axis=0, keepdims=True)
    vg_ref[3:4, :] = jnp.sum(dv_ref[...].astype(F32), axis=0, keepdims=True)
    load_w[0].wait()
    gn1 = dot_nt(dq_ref[...], as_matrix(wbuf_ref[0]))
    load_w[1].wait()
    gn1 = gn1 + dot_nt(dk_ref[...], as_matrix(wbuf_ref[1]))
    load_w[2].wait()
    gn1 = gn1 + dot_nt(dv_ref[...], as_matrix(wbuf_ref[2]))
    for s in range(ring):
        sum_b.send_y(s)
    hat, inv = normed(act_ref[...].astype(F32))
    vg_ref[0:1, :] = jnp.sum(gn1 * hat, axis=0, keepdims=True)
    vg_ref[1:2, :] = jnp.sum(gn1, axis=0, keepdims=True)
    r = gn1 * vec_ref[0:1, :]
    r_mean = jnp.mean(r, axis=-1, keepdims=True)
    rn_mean = jnp.mean(r * hat, axis=-1, keepdims=True)
    ig_ref[...] = ig_ref[...] + (r - r_mean - hat * rn_mean) * inv

    low_vec = vg_ref[...].astype(BF)
    row = lax.broadcasted_iota(jnp.int32, (VROWS, 1), 0)

    for w in range(wide):
        small = low_vec[:, w * sh : (w + 1) * sh]
        small = jnp.concatenate([small, jnp.zeros((VROWS, 256 - sh), BF)], axis=1)
        j = w // GROUP
        large = low_vec[:, j * fr : (j + 1) * fr]
        large = jnp.concatenate([large, jnp.zeros((VROWS, 256 - fr), BF)], axis=1)
        large = jnp.where(q == w % GROUP, large, jnp.zeros_like(large))
        ownv_ref[w] = jnp.where(row < 10, small, large)
    sum_v.start()
    expert_service(ring - 2, (2,))
    for s in range(ring):
        sum_v.send_y(s)

    own_loads[3].wait()
    tok[3].wait_recv()
    far_mixed.wait_recv()
    mixed = h1_ref[...] + town_ref[3].astype(F32) + tin_ref[3].astype(F32) + tin_ref[5].astype(F32)
    for e in range(EXPERTS):
        mixed = mixed + jnp.where(expert == e, vec_ref[7 + e : 8 + e, :], 0.0)
    mixed_ref[...] = mixed.astype(BF)

    sum_b.step(0)
    sum_v.step(0)
    expert_service(ring - 1, (0,))
    final_start(0)
    sum_a.step(2)
    sum_b.step(1)
    sum_v.step(1)
    expert_service(ring - 1, (1,))
    final_start(1)
    expert_service(ring - 1, (2,))
    final_start(2)
    for s in range(2, ring):
        if s > 2:
            sum_a.step(s)
        sum_b.step(s)
        sum_v.step(s)
    go_ref[...] = sum_a.finish()
    final_finish()
    last = sum_b.finish()
    gq_ref[...] = last[0:sh]
    gk_ref[...] = last[sh : 2 * sh]
    gv_ref[...] = last[2 * sh : 3 * sh]
    vout_ref[...] = sum_v.finish()
    for copy in pending:
        copy.wait_send()


def output_kernel(fr, mixed_in, ig_in, ug_in, dg_in, go_in, gq_in, gk_in, gv_in, v_in, *outs):
    (mixed, ig, g1, b1, gq, bq, gk, gv, bv, go, bo, g2, b2, gu, bu, gd, bd) = outs
    sh = g1.shape[1]
    mixed[...] = mixed_in[...]
    ig[...] = ig_in[...]
    for ref, src in ((gq, gq_in), (gk, gk_in), (gv, gv_in), (go, go_in)):
        ref[...] = src[...]
    for i, ref in enumerate((g1, b1, bq, bv, bo, g2, b2)):
        ref[...] = v_in[i : i + 1, 0:sh]
    bd[...] = v_in[7:10, 0:sh]
    bu[...] = v_in[10:13, 0:fr]
    gd[...] = dg_in[...].astype(F32)
    ring = ug_in.shape[3] // fr
    for e in range(EXPERTS):
        rows = [ug_in[to, e] for to in range(GROUP)]
        parts = [
            rows[to][:, j * fr : (j + 1) * fr] for j in range(ring) for to in range(GROUP)
        ]
        gu[e] = jnp.concatenate(parts, axis=1).astype(F32)


def body(
    wide,
    narrow,
    activations,
    cotangent,
    item_kinds,
    attn_norm_gain,
    attn_norm_bias,
    query_weight,
    query_bias,
    key_weight,
    value_weight,
    value_bias,
    output_weight,
    output_bias,
    ffn_norm_gain,
    ffn_norm_bias,
    up_weight,
    up_bias,
    down_weight,
    down_bias,
):
    ring = wide // GROUP
    tokens, width = activations.shape
    sh = width // wide
    fr = down_weight.shape[1]
    hidden = fr * ring

    flat = lambda v: v.reshape(1, sh)
    down_parts = down_weight.reshape(EXPERTS, GROUP, sh, width)

    prow = 4 * sh + VROWS
    anyspace = pl.BlockSpec(memory_space=pl.ANY)
    vmem = pl.BlockSpec(memory_space=pltpu.VMEM)
    smem = pl.BlockSpec(memory_space=pltpu.SMEM)
    dma = lambda n: pltpu.SemaphoreType.DMA((max(n, 1),))
    shape = jax.ShapeDtypeStruct
    token_bf = shape((tokens, width), BF)
    fsteps = ring * EXPERTS

    (ap, g, tn, tc, kg, h1, n1, qs, ks, vs, heads, vec, ub) = pl.pallas_call(
        functools.partial(gather_kernel, wide, narrow),
        out_shape=(
            shape((wide, prow, width), BF),
            shape((2, EXPERTS, wide, sh, width), BF),
            shape((GROUP, tokens, width), BF),
            shape((GROUP, tokens, width), BF),
            shape((GROUP, 8, 128), jnp.int32),
            shape((tokens, width), F32),
            token_bf,
            token_bf,
            token_bf,
            token_bf,
            token_bf,
            shape((VROWS, width), F32),
            shape((VROWS, hidden), F32),
        ),
        in_specs=[smem] + [vmem] * 18,
        out_specs=(anyspace,) * 11 + (vmem,) * 2,
        scratch_shapes=[
            pltpu.VMEM((tokens, width), F32),
        ]
        + [pltpu.VMEM((tokens, width), BF)] * 5
        + [
            dma(6),
            pltpu.VMEM((tokens, width), F32),
            pltpu.VMEM((tokens, tokens), F32),
            pltpu.VMEM((4, wide, sh, width), BF),
            pltpu.VMEM((wide, VROWS, 256), BF),
            pltpu.VMEM((tokens, width), BF),
            pltpu.VMEM((prow, width), BF),
            pltpu.VMEM((VROWS, 256), F32),
            pltpu.VMEM((GROUP, EXPERTS, sh, hidden), BF),
            pltpu.VMEM((8, 128), jnp.int32),
            dma(ring),
            dma(ring),
            dma(ring),
            dma(ring),
            dma(2 * ring),
            dma(2 * ring),
            dma(3),
            dma(3),
            dma(fsteps),
            dma(fsteps),
            dma(fsteps),
            dma(fsteps),
            dma(6),
            dma(6),
            dma(3),
            dma(3),
            dma(11),
        ],
        compiler_params=pltpu.CompilerParams(
            collective_id=0, has_side_effects=True, vmem_limit_bytes=VMEM_LIMIT
        ),
        name="gather_attend",
    )(
        item_kinds,
        item_kinds,
        activations,
        cotangent,
        query_weight,
        key_weight,
        value_weight,
        output_weight,
        flat(attn_norm_gain),
        flat(attn_norm_bias),
        flat(query_bias),
        flat(value_bias),
        flat(output_bias),
        flat(ffn_norm_gain),
        flat(ffn_norm_bias),
        down_bias,
        up_bias,
        up_weight,
        down_parts,
    )

    per_member = 3
    rows = tokens // per_member
    full = lambda *dims: pl.BlockSpec(
        dims, lambda i: (0,) * len(dims), pipeline_mode=pl.Buffered(1)
    )
    tiles = GROUP * per_member
    tile = pl.BlockSpec((rows, width), lambda i: (jnp.minimum(i, tiles - 1), 0))
    matrix = pl.BlockSpec((1, width, width), lambda i: (jnp.maximum(i - tiles, 0), 0, 0))
    y, gn, dw, dub = pl.pallas_call(
        functools.partial(expert_kernel, per_member, tiles),
        grid=(tiles + 2 * EXPERTS,),
        out_shape=(
            shape((GROUP * tokens, width), BF),
            shape((GROUP * tokens, width), BF),
            shape((2 * EXPERTS, width, width), BF),
            shape((VROWS, hidden), F32),
        ),
        in_specs=[
            smem,
            tile,
            tile,
            full(2 * EXPERTS, width, width),
            full(VROWS, hidden),
        ],
        out_specs=(tile, tile, matrix, full(VROWS, hidden)),
        scratch_shapes=[
            pltpu.VMEM((2 * EXPERTS, width, width), F32),
        ],
        compiler_params=pltpu.CompilerParams(
            dimension_semantics=("arbitrary",), vmem_limit_bytes=VMEM_LIMIT
        ),
        name="experts",
    )(
        kg,
        tn.reshape(GROUP * tokens, width),
        tc.reshape(GROUP * tokens, width),
        g.reshape(2 * EXPERTS, width, width),
        ub,
    )

    def pack_scratch(rows, lanes=width):
        buf = lambda n: pltpu.VMEM((n, rows, lanes), BF)
        return [
            buf(wide),
            pltpu.VMEM((ring, 2, rows, lanes), BF),
            buf(ring),
            buf(ring),
            buf(max(ring - 1, 1)),
            buf(max(ring - 1, 1)),
            buf(narrow),
        ]

    pack_sems = [dma(2 * ring)] * 2 + [dma(ring)] * 4 + [dma(narrow - 1)] * 2
    slab = (EXPERTS, GROUP, sh, width)
    (mixed, ig, ug, dg, g_out, g_query, g_key, g_value, vout) = pl.pallas_call(
        functools.partial(grad_kernel, wide, narrow),
        out_shape=(
            token_bf,
            shape((tokens, width), F32),
            shape((GROUP, EXPERTS, sh, width), BF),
            shape(slab, BF),
            shape((sh, width), F32),
            shape((sh, width), F32),
            shape((sh, width), F32),
            shape((sh, width), F32),
            shape((VROWS, 256), F32),
        ),
        in_specs=[smem] + [anyspace] * 8 + [vmem] * 2 + [anyspace] * 4,
        out_specs=(vmem, vmem, anyspace, anyspace) + (vmem,) * 5,
        scratch_shapes=[
            pltpu.VMEM((tokens, width), BF),
            pltpu.VMEM((tokens, width), BF),
            pltpu.VMEM((tokens, width), F32),
        ]
        + [pltpu.VMEM((tokens, width), BF)] * 5
        + [
            dma(8),
            pltpu.VMEM((6, tokens, width), BF),
            pltpu.VMEM((4, tokens, width), BF),
            pltpu.VMEM((ring,) + slab[:1] + slab[1:], BF),
            pltpu.VMEM((max(ring - 1, 1),) + slab, BF),
            pltpu.VMEM((max(ring - 1, 1),) + slab, BF),
            pltpu.VMEM((max(narrow // 2, 1),) + slab, BF),
            pltpu.VMEM((3, wide, sh, width), BF),
            pltpu.VMEM((tokens, tokens), F32),
            pltpu.VMEM((tokens, width), BF),
            pltpu.VMEM((tokens, width), BF),
            pltpu.VMEM((tokens, width), BF),
            pltpu.VMEM((tokens, width), BF),
            pltpu.VMEM((VROWS, width), F32),
        ]
        + pack_scratch(sh)
        + pack_scratch(3 * sh)
        + pack_scratch(VROWS, 256)
        + [
            dma(6),
            dma(6),
            dma(fsteps),
            dma(fsteps),
            dma(fsteps),
            dma(fsteps),
            dma(EXPERTS * max(narrow // 2 - 1, 1)),
            dma(EXPERTS * max(narrow // 2 - 1, 1)),
            dma(8 * EXPERTS),
            dma(8 * EXPERTS),
            dma(10 + ring + EXPERTS),
        ]
        + pack_sems
        + pack_sems
        + pack_sems,
        compiler_params=pltpu.CompilerParams(
            collective_id=1, has_side_effects=True, vmem_limit_bytes=VMEM_LIMIT
        ),
        name="gradients",
    )(
        item_kinds,
        activations,
        cotangent,
        h1,
        n1,
        qs,
        ks,
        vs,
        heads,
        vec,
        dub,
        ap,
        y.reshape(GROUP, tokens, width),
        gn.reshape(GROUP, tokens, width),
        dw.reshape(2, EXPERTS, wide, sh, width),
    )

    vec_shape = shape((1, sh), F32)
    mat_shape = shape((sh, width), F32)
    outs = pl.pallas_call(
        functools.partial(output_kernel, fr),
        out_shape=(
            token_bf,
            shape((tokens, width), F32),
            vec_shape,
            vec_shape,
            mat_shape,
            vec_shape,
            mat_shape,
            mat_shape,
            vec_shape,
            mat_shape,
            vec_shape,
            vec_shape,
            vec_shape,
            shape((EXPERTS, sh, GROUP * hidden), F32),
            shape((EXPERTS, fr), F32),
            shape(slab, F32),
            shape((EXPERTS, sh), F32),
        ),
        in_specs=[vmem] * 9,
        out_specs=(vmem,) * 17,
        compiler_params=pltpu.CompilerParams(vmem_limit_bytes=VMEM_LIMIT),
        name="final_outputs",
    )(mixed, ig, ug, dg, g_out, g_query, g_key, g_value, vout)
    outs = list(outs)
    for i in (2, 3, 5, 8, 10, 11, 12):
        outs[i] = outs[i].reshape(sh)
    outs[15] = outs[15].reshape(EXPERTS, fr, width)
    return tuple(outs)


def solution(mesh):
    rows = P(("wide", "narrow"), None)
    return jax.shard_map(
        functools.partial(body, mesh.shape["wide"], mesh.shape["narrow"]),
        mesh=mesh,
        in_specs=(
            rows,
            rows,
            rows,
            P("wide"),
            P("wide"),
            P("wide", None),
            P("wide"),
            P("wide", None),
            P("wide", None),
            P("wide"),
            P("wide", None),
            P("wide"),
            P("wide"),
            P("wide"),
            P(None, "wide", None),
            P(None, "wide"),
            P(None, "wide", None),
            P(None, "wide"),
        ),
        out_specs=(
            rows,
            rows,
            P("wide"),
            P("wide"),
            P("wide", None),
            P("wide"),
            P("wide", None),
            P("wide", None),
            P("wide"),
            P("wide", None),
            P("wide"),
            P("wide"),
            P("wide"),
            P(None, "wide", None),
            P(None, "wide"),
            P(None, "wide", None),
            P(None, "wide"),
        ),
        check_vma=False,
    )
```

```python
import functools

import jax
import jax.numpy as jnp
from jax import lax
from jax.experimental import pallas as pl
from jax.experimental.pallas import tpu as pltpu
from jax.sharding import PartitionSpec as P

HEADS = 12
EXPERTS = 3
IMG_LEN = 197
TXT_LEN = 64
EPS = 1e-05
MASKED = -1e30
GROUP = 4
VROWS = 16
MESH = pl.DeviceIdType.MESH
BF = jnp.bfloat16
F32 = jnp.float32
VMEM_LIMIT = 63 * 1024 * 1024


def dot(a, b):
    return lax.dot_general(a, b, (((1,), (0,)), ((), ())), preferred_element_type=F32)


def dot_nt(a, b):
    return lax.dot_general(a, b, (((1,), (1,)), ((), ())), preferred_element_type=F32)


def dot_tn(a, b):
    return lax.dot_general(a, b, (((0,), (0,)), ((), ())), preferred_element_type=F32)


class Place:
    def __init__(self, wide, narrow):
        self.wide, self.narrow = wide, narrow
        self.ring = wide // GROUP
        w = lax.axis_index("wide")
        self.x = lax.axis_index("narrow")
        self.w = w
        self.a = lax.div(w, GROUP)
        self.q = lax.rem(w, GROUP)
        self.c = lax.rem(w, 2)
        self.y = lax.div(self.q, 2)
        self.h = lax.rem(self.x, 2)
        self.q_core = 2 * self.y + 1 - self.c
        self.q_y = 2 * (1 - self.y) + self.c
        self.q_diag = 2 * (1 - self.y) + 1 - self.c
        self.next = lax.rem(self.a + 1, self.ring)
        self.prev = lax.rem(self.a + self.ring - 1, self.ring)

    def member(self, q):
        return (self.a * GROUP + q, self.x)

    def ring_next(self):
        return (self.next * GROUP + self.q, self.x)

    def ring_prev(self):
        return (self.prev * GROUP + self.q, self.x)

    def pair(self):
        return (self.w, self.x + 1 - 2 * self.h)

    def pair_member(self, q):
        return (self.a * GROUP + q, self.x + 1 - 2 * self.h)

    def other_narrow(self, k):
        return (self.w, lax.rem(self.x + k, self.narrow))

    def back(self, s):
        return lax.rem(self.a - s + 2 * self.ring, self.ring)

    def barrier(self, narrow_all):
        sem = pltpu.get_barrier_semaphore()
        who = [self.member(self.q_core), self.member(self.q_y), self.member(self.q_diag)]
        who += [self.ring_next(), self.ring_prev()]
        if narrow_all:
            who += [self.other_narrow(k) for k in range(1, self.narrow)]
            who += [self.pair_member(m) for m in (self.q_core, self.q_y, self.q_diag)]
        else:
            who += [self.pair()]
        for dev in who:
            pl.semaphore_signal(sem, inc=1, device_id=dev, device_id_type=MESH)
        pl.semaphore_wait(sem, len(who))


def remote(src, dst, sends, recvs, i, dev):
    return pltpu.make_async_remote_copy(
        src_ref=src,
        dst_ref=dst,
        send_sem=sends.at[i],
        recv_sem=recvs.at[i],
        device_id=dev,
        device_id_type=MESH,
    )


def item_bounds(kinds, count):
    start = jnp.int32(0)
    bounds = []
    for i in range(count):
        kind = kinds(i)
        length = jnp.where(
            kind == 0,
            IMG_LEN,
            jnp.where(kind == 1, TXT_LEN, jnp.where(kind == 2, IMG_LEN + TXT_LEN, 0)),
        )
        bounds.append((kind, start, start + length))
        start = start + length
    return bounds


def segments(position, bounds):
    seg = jnp.zeros(position.shape, jnp.int32)
    for _, _, end in bounds:
        seg = seg + jnp.where(position >= end, 1, 0)
    return seg


def expert_of(position, bounds):
    out = jnp.full(position.shape, EXPERTS, jnp.int32)
    for kind, start, end in bounds:
        out = jnp.where((position >= start) & (position < end), kind, out)
    return out


def fill_bias(bias_ref, bounds):
    tokens = bias_ref.shape[0]
    seg_col = segments(lax.broadcasted_iota(jnp.int32, (tokens, 1), 0), bounds)
    seg_row = segments(lax.broadcasted_iota(jnp.int32, (1, tokens), 1), bounds)
    bias_ref[...] = jnp.where(seg_col == seg_row, 0.0, MASKED).astype(F32)


def as_matrix(block):
    n, rows, d = block.shape
    if rows % 16 == 0:
        return block.reshape(n * rows, d)
    return block.astype(F32).reshape(n * rows, d).astype(block.dtype)


def as_slabs(matrix, n):
    total, d = matrix.shape
    rows = total // n
    if rows % 16 == 0:
        return matrix.astype(BF).reshape(n, rows, d)
    return matrix.reshape(n, rows, d).astype(BF)


def normed(v):
    mean = jnp.mean(v, axis=-1, keepdims=True)
    centered = v - mean
    var = jnp.mean(centered * centered, axis=-1, keepdims=True)
    inv = lax.rsqrt(var + EPS)
    return centered * inv, inv


def pair_lanes(p):
    return pl.ds(pl.multiple_of(p * 128, 128), 128)


def softmax_rows(q_half, k2, bias_ref):
    scores = dot_nt(q_half, k2) + bias_ref[...]
    top = jnp.max(scores, axis=1, keepdims=True)
    raw = jnp.exp(scores - top)
    return raw * (1.0 / jnp.sum(raw, axis=1, keepdims=True))


def gather_kernel(
    wide,
    narrow,
    kinds_ref,
    kinds_vec_ref,
    act_ref,
    cot_ref,
    wq_ref,
    wk_ref,
    wv_ref,
    wo_ref,
    g1_ref,
    b1_ref,
    bq_ref,
    bv_ref,
    bo_ref,
    g2_ref,
    b2_ref,
    bd_ref,
    bu_ref,
    up_full_ref,
    down_ref,
    ap_ref,
    g_ref,
    tn_ref,
    tc_ref,
    kg_ref,
    h1_out,
    n1_out,
    q_out,
    k_out,
    v_out,
    heads_out,
    vec_ref,
    ub_ref,
    h1_ref,
    n1_ref,
    q_ref,
    k_ref,
    v_ref,
    heads_ref,
    flush,
    xhat_ref,
    bias_ref,
    wbuf_ref,
    vbuf_ref,
    n2_ref,
    pack_ref,
    small_ref,
    up_ref,
    kpad_ref,
    ring_s,
    ring_r,
    y_s,
    y_r,
    core_s,
    core_r,
    grp_s,
    grp_r,
    fring_s,
    fring_r,
    pair_s,
    pair_r,
    tok_s,
    tok_r,
    kin_s,
    kin_r,
    loc,
):
    place = Place(wide, narrow)
    ring = place.ring
    tokens, width = act_ref.shape
    sh = width // wide
    fr = ub_ref.shape[1] // ring
    a, q, h = place.a, place.q, place.h
    pending = []
    flushes = []

    def keep(i, ref, out):
        copy = pltpu.make_async_copy(ref, out, flush.at[i])
        copy.start()
        flushes.append(copy)


    def go(copy):
        copy.start()
        pending.append(copy)
        return copy

    for i, ref in enumerate((wq_ref, wk_ref, wv_ref, wo_ref)):
        pack_ref[i * sh : (i + 1) * sh, :] = ref[...]
    small_ref[...] = jnp.zeros(small_ref.shape, F32)
    for i, ref in enumerate((g1_ref, b1_ref, bq_ref, bv_ref, bo_ref, g2_ref, b2_ref)):
        small_ref[i : i + 1, 0:sh] = ref[...].astype(F32)
    small_ref[7:10, 0:sh] = bd_ref[...].astype(F32)
    small_ref[10:13, 0:fr] = bu_ref[...].astype(F32)
    pack_ref[4 * sh :, 0:256] = small_ref[...].astype(BF)
    pack_ref[4 * sh :, 256:] = jnp.zeros((VROWS, width - 256), BF)
    kpad_ref[...] = jnp.zeros(kpad_ref.shape, jnp.int32)
    kpad_ref[0:1, 0 : kinds_vec_ref.shape[1]] = kinds_vec_ref[...]

    place.barrier(False)

    own_pack = pltpu.make_async_copy(pack_ref, ap_ref.at[place.w], loc.at[0])
    own_pack.start()

    def slab_copies(s):
        mine = place.back(s) * GROUP + q
        return mine

    def pack_ring(s):
        mine = slab_copies(s)
        src = pack_ref if s == 0 else ap_ref.at[mine]
        return remote(src, ap_ref.at[mine], ring_s, ring_r, s, place.ring_next())

    def pack_y(s):
        mine = slab_copies(s)
        src = pack_ref if s == 0 else ap_ref.at[mine]
        return remote(src, ap_ref.at[mine], y_s, y_r, s, place.member(place.q_y))

    def pack_core(s):
        mine = slab_copies(s)
        src = pack_ref if s == 0 else ap_ref.at[mine]
        return remote(src, ap_ref.at[mine], core_s, core_r, s, place.member(place.q_core))

    def pack_relay(s):
        theirs = place.back(s) * GROUP + place.q_y
        slab = ap_ref.at[theirs]
        return remote(slab, slab, core_s, core_r, ring + s, place.member(place.q_core))

    ring_copies = [go(pack_ring(0))]
    y_copies = [go(pack_y(0))]
    core_copies = [go(pack_core(0))]

    for e in range(EXPERTS):
        rows = up_full_ref[e]
        for to in range(GROUP):
            parts = [
                rows[:, (j * GROUP + to) * fr : (j * GROUP + to + 1) * fr] for j in range(ring)
            ]
            up_ref[to, e] = jnp.concatenate(parts, axis=1)

    def group_send(r, to):
        return remote(
            up_ref.at[to],
            g_ref.at[0, :, place.a * GROUP + q],
            grp_s,
            grp_r,
            r,
            place.member(to),
        )

    own_up = pltpu.make_async_copy(up_ref.at[q], g_ref.at[0, :, place.w], loc.at[1])
    own_down = pltpu.make_async_copy(
        down_ref, g_ref.at[1, :, pl.ds(a * GROUP, GROUP)], loc.at[10]
    )
    others = (place.q_core, place.q_y, place.q_diag)

    group_copies = [go(group_send(r, others[r])) for r in range(3)]
    own_up.start()
    own_down.start()

    own_kinds = pltpu.make_async_copy(kpad_ref, kg_ref.at[q], loc.at[2])
    own_kinds.start()
    kind_copies = [
        go(remote(kpad_ref, kg_ref.at[q], kin_s, kin_r, r, place.member(others[r])))
        for r in range(3)
    ]

    xhat, _ = normed(act_ref[...].astype(F32))
    xhat_ref[...] = xhat
    bounds = item_bounds(lambda i: kinds_ref[0, i], kinds_ref.shape[1])
    fill_bias(bias_ref, bounds)

    def fslab(s, e):
        return g_ref.at[h, e, pl.ds(place.back(s) * GROUP, GROUP)]

    def fring(s, e):
        slab = fslab(s, e)
        return remote(slab, slab, fring_s, fring_r, s * EXPERTS + e, place.ring_next())

    def fpair(s, e):
        slab = fslab(s, e)
        return remote(slab, slab, pair_s, pair_r, s * EXPERTS + e, place.pair())

    fring_copies = {}
    pair_copies = []

    def expert_service(s, chunks=range(EXPERTS)):
        for e in chunks:
            if s > 0:
                fring_copies[s - 1, e].wait_recv()
            if s < ring - 1:
                fring_copies[s, e] = go(fring(s, e))
            if s > 0:
                pair_copies.append(go(fpair(s, e)))

    def pack_service(s):
        ring_copies[s - 1].wait_recv()
        if s < ring - 1:
            ring_copies.append(go(pack_ring(s)))
        y_copies.append(go(pack_y(s)))
        core_copies.append(go(pack_core(s)))

    for s in range(1, ring - 1):
        pack_service(s)
    for copy in group_copies:
        copy.wait_recv()
    own_up.wait()
    own_down.wait()
    expert_service(0)
    pack_service(ring - 1)

    relay_copies = []
    for s in range(ring):
        y_copies[s].wait_recv()
        relay_copies.append(go(pack_relay(s)))
    for copy in core_copies:
        copy.wait_recv()
    for copy in relay_copies:
        copy.wait_recv()
    own_pack.wait()

    def load_weight(i):
        return pltpu.make_async_copy(
            ap_ref.at[:, pl.ds(i * sh, sh), :], wbuf_ref.at[i], loc.at[3 + i]
        )

    load_vec = pltpu.make_async_copy(
        ap_ref.at[:, pl.ds(4 * sh, VROWS), pl.ds(0, 256)], vbuf_ref, loc.at[7]
    )
    load_vec.start()
    loads = [load_weight(i) for i in range(4)]
    for load in loads:
        load.start()

    def token_copies(src_own, ref, base):
        own = remote(src_own, ref.at[q], tok_s, tok_r, base, place.member(place.q_y))
        core = remote(src_own, ref.at[q], tok_s, tok_r, base + 1, place.member(place.q_core))
        far = ref.at[place.q_y]
        relay = remote(far, far, tok_s, tok_r, base + 2, place.member(place.q_core))
        return own, core, relay

    own_cot = pltpu.make_async_copy(cot_ref, tc_ref.at[q], loc.at[8])
    own_cot.start()
    cot_y, cot_core, cot_relay = token_copies(cot_ref, tc_ref, 0)
    go(cot_y)
    go(cot_core)

    expert_service(1)
    load_vec.wait()
    vec_ref[...] = jnp.concatenate([vbuf_ref[w][:, :sh] for w in range(wide)], axis=1).astype(F32)
    ub_ref[...] = jnp.concatenate(
        [vbuf_ref[j * GROUP + q][:, :fr] for j in range(ring)], axis=1
    ).astype(F32)

    n1_ref[...] = (xhat_ref[...] * vec_ref[0:1, :] + vec_ref[1:2, :]).astype(BF)
    loads[0].wait()
    q_ref[...] = (dot(n1_ref[...], as_matrix(wbuf_ref[0])) + vec_ref[2:3, :]).astype(BF)
    loads[1].wait()
    k_ref[...] = dot(n1_ref[...], as_matrix(wbuf_ref[1])).astype(BF)
    loads[2].wait()
    v_ref[...] = (dot(n1_ref[...], as_matrix(wbuf_ref[2])) + vec_ref[3:4, :]).astype(BF)
    keep(0, n1_ref, n1_out)
    keep(1, q_ref, q_out)
    keep(2, k_ref, k_out)
    keep(3, v_ref, v_out)
    loads[3].wait()

    pairs = width // 128
    low = lax.broadcasted_iota(jnp.int32, (tokens, 128), 1) < 64

    def attend(p, carry):
        lanes = pair_lanes(p)
        q2, k2, v2 = q_ref[:, lanes] * 0.125, k_ref[:, lanes], v_ref[:, lanes]
        zero = jnp.zeros_like(q2)
        first = softmax_rows(jnp.where(low, q2, zero), k2, bias_ref).astype(BF)
        out_low = dot(first, v2)
        second = softmax_rows(jnp.where(low, zero, q2), k2, bias_ref).astype(BF)
        out_high = dot(second, v2)
        heads_ref[:, lanes] = jnp.where(low, out_low, out_high).astype(BF)
        return carry

    lax.fori_loop(0, pairs, attend, 0)

    inside = lax.broadcasted_iota(jnp.int32, (tokens, 1), 0) < bounds[-1][2]
    attn = dot(heads_ref[...], as_matrix(wbuf_ref[3])) + vec_ref[4:5, :]
    h1 = act_ref[...].astype(F32) + jnp.where(inside, attn, 0.0)
    h1_ref[...] = h1
    keep(4, heads_ref, heads_out)
    keep(5, h1_ref, h1_out)
    xhat2, _ = normed(h1)
    n2_ref[...] = (xhat2 * vec_ref[5:6, :] + vec_ref[6:7, :]).astype(BF)

    own_n2 = pltpu.make_async_copy(n2_ref, tn_ref.at[q], loc.at[9])
    own_n2.start()
    n2_y, n2_core, n2_relay = token_copies(n2_ref, tn_ref, 3)
    go(n2_y)
    go(n2_core)
    for s in range(2, ring - 2):
        expert_service(s)
    expert_service(ring - 2)
    cot_y.wait_recv()
    go(cot_relay)
    n2_y.wait_recv()
    go(n2_relay)
    expert_service(ring - 1)
    cot_core.wait_recv()
    cot_relay.wait_recv()
    n2_core.wait_recv()
    n2_relay.wait_recv()
    for copy in kind_copies:
        copy.wait_recv()
    for copy in pair_copies:
        copy.wait_recv()
    for copy in pending:
        copy.wait_send()
    own_kinds.wait()
    for copy in flushes:
        copy.wait()
    own_cot.wait()
    own_n2.wait()


def expert_kernel(
    per_member,
    tiles,
    kinds_ref,
    n2_ref,
    cot_ref,
    g_ref,
    ub_ref,
    y_ref,
    gn_ref,
    dw_ref,
    dub_ref,
    acc_ref,
):
    step = pl.program_id(0)
    working = step < tiles
    rows = n2_ref.shape[0]
    tile = jnp.minimum(step, tiles - 1)
    member = lax.div(tile, per_member)
    row0 = lax.rem(tile, per_member) * rows
    bounds = item_bounds(lambda i: kinds_ref[member, 0, i], 8)
    position = lax.broadcasted_iota(jnp.int32, (rows, 1), 0) + row0
    present = []
    for e in range(EXPERTS):
        here = False
        for kind, start, end in bounds:
            here = here | ((kind == e) & (start < row0 + rows) & (end > row0) & (end > start))
        present.append(here)
    count = sum(here.astype(jnp.int32) for here in present)
    @pl.when(step == 0)
    def _():
        acc_ref[...] = jnp.zeros(acc_ref.shape, F32)
        dub_ref[...] = jnp.zeros(dub_ref.shape, F32)

    def run(which):
        expert = expert_of(position, bounds)
        masks = [expert == e for e in which]
        mine = functools.reduce(jnp.logical_or, masks)
        n2, cot = n2_ref[...], cot_ref[...]

        def merged(product):
            out = product(which[0])
            for e, mask in zip(which[1:], masks[1:]):
                out = jnp.where(mask, product(e), out)
            return out

        def bias(e):
            later = jnp.where(e == 1, ub_ref[11:12, :], ub_ref[12:13, :])
            return jnp.where(e == 0, ub_ref[10:11, :], later)

        pre = merged(lambda e: dot(n2, g_ref[e]) + bias(e))
        ga = merged(lambda e: dot_nt(cot, g_ref[EXPERTS + e]))
        half_cdf = 0.5 + 0.5 * lax.erf(pre * 0.7071067811865476)
        slope = half_cdf + pre * (0.3989422804014327 * jnp.exp(-0.5 * pre * pre))
        act = (pre * half_cdf).astype(BF)
        grad = jnp.where(mine, ga * slope, 0.0).astype(BF)
        out = merged(lambda e: dot(act, g_ref[EXPERTS + e]))
        y_ref[...] = jnp.where(mine, out, 0.0).astype(BF)
        gn_ref[...] = merged(lambda e: dot_nt(grad, g_ref[e])).astype(BF)
        for e, mask in zip(which, masks):
            part = grad if len(which) == 1 else jnp.where(mask, grad, jnp.zeros_like(grad))
            acc_ref[e] += dot_tn(n2, part)
            acc_ref[EXPERTS + e] += dot_tn(act, jnp.where(mask, cot, jnp.zeros_like(cot)))
            total = jnp.sum(part.astype(F32), axis=0, keepdims=True)
            for i in range(EXPERTS):
                dub_ref[10 + i : 11 + i, :] += jnp.where(e == i, total, 0.0)

    lowest = jnp.where(present[0], 0, jnp.where(present[1], 1, 2))
    highest = jnp.where(present[2], 2, jnp.where(present[1], 1, 0))

    @pl.when(working & (count == 1))
    def _():
        run((lowest,))

    @pl.when(working & (count == 2))
    def _():
        run((lowest, highest))

    @pl.when(working & (count == 3))
    def _():
        run((0, 1, 2))

    @pl.when(working & (count == 0))
    def _():
        y_ref[...] = jnp.zeros(y_ref.shape, BF)
        gn_ref[...] = jnp.zeros(gn_ref.shape, BF)

    @pl.when(jnp.logical_not(working))
    def _():
        dw_ref[0] = acc_ref[step - tiles].astype(BF)


class PackSum:
    def __init__(self, place, own, core_in, y_out, y_in, hop_out, hop_in, last, sems):
        self.place = place
        self.own, self.core_in = own, core_in
        self.y_out, self.y_in = y_out, y_in
        self.hop_out, self.hop_in = hop_out, hop_in
        self.last = last
        (self.core_s, self.core_r, self.y_s, self.y_r) = sems[:4]
        (self.hop_s, self.hop_r, self.x_s, self.x_r) = sems[4:]
        self.copies = []

    def go(self, copy):
        copy.start()
        self.copies.append(copy)
        return copy

    def start(self):
        place = self.place
        self.core = {}
        for s in range(place.ring):
            d = place.back(s + 1)
            for far in (1, 0):
                yy = (1 - place.y) if far else place.y
                src = self.own.at[d * GROUP + 2 * yy + 1 - place.c]
                self.core[s, far] = self.go(
                    remote(
                        src,
                        self.core_in.at[s, far],
                        self.core_s,
                        self.core_r,
                        2 * s + far,
                        place.member(place.q_core),
                    )
                )
        self.to_y = {}
        self.hop = {}

    def load(self, ref, *index):
        return ref[index].astype(F32)

    def send_y(self, s):
        place = self.place
        d = place.back(s + 1)
        self.core[s, 1].wait_recv()
        total = self.load(self.own, d * GROUP + place.q_y) + self.load(self.core_in, s, 1)
        self.y_out[s] = total.astype(BF)
        self.to_y[s] = self.go(
            remote(
                self.y_out.at[s],
                self.y_in.at[s],
                self.y_s,
                self.y_r,
                s,
                place.member(place.q_y),
            )
        )

    def step(self, s):
        place = self.place
        d = place.back(s + 1)
        self.core[s, 0].wait_recv()
        self.to_y[s].wait_recv()
        total = self.load(self.own, d * GROUP + place.q) + self.load(self.core_in, s, 0)
        total = total + self.load(self.y_in, s)
        if s > 0:
            self.hop[s - 1].wait_recv()
            total = total + self.load(self.hop_in, s - 1)
        if s < place.ring - 1:
            self.hop_out[s] = total.astype(BF)
            self.hop[s] = self.go(
                remote(
                    self.hop_out.at[s],
                    self.hop_in.at[s],
                    self.hop_s,
                    self.hop_r,
                    s,
                    place.ring_next(),
                )
            )
        else:
            self.last[place.x] = total.astype(BF)
            self.spread = [
                self.go(
                    remote(
                        self.last.at[place.x],
                        self.last.at[place.x],
                        self.x_s,
                        self.x_r,
                        k - 1,
                        place.other_narrow(k),
                    )
                )
                for k in range(1, place.narrow)
            ]

    def finish(self):
        for copy in self.spread:
            copy.wait_recv()
        total = self.load(self.last, 0)
        for i in range(1, self.place.narrow):
            total = total + self.load(self.last, i)
        for copy in self.copies:
            copy.wait_send()
        return total


def grad_kernel(
    wide,
    narrow,
    kinds_ref,
    act_in,
    cot_in,
    h1_in,
    n1_in,
    q_in,
    k_in,
    v_in,
    heads_in,
    vec_ref,
    dub_ref,
    ap_ref,
    yp_ref,
    gnp_ref,
    dw_ref,
    mixed_ref,
    ig_ref,
    ug_ref,
    dg_ref,
    go_ref,
    gq_ref,
    gk_ref,
    gv_ref,
    vout_ref,
    act_ref,
    cot_ref,
    h1_ref,
    n1_ref,
    q_ref,
    k_ref,
    v_ref,
    heads_ref,
    arrive,
    tin_ref,
    town_ref,
    pin_ref,
    fout_ref,
    fin_ref,
    flast_ref,
    wbuf_ref,
    bias_ref,
    ga_ref,
    ghd_ref,
    dk_ref,
    dv_ref,
    vg_ref,
    owna_ref,
    cina_ref,
    youta_ref,
    yina_ref,
    houta_ref,
    hina_ref,
    lasta_ref,
    ownb_ref,
    cinb_ref,
    youtb_ref,
    yinb_ref,
    houtb_ref,
    hinb_ref,
    lastb_ref,
    ownv_ref,
    cinv_ref,
    youtv_ref,
    yinv_ref,
    houtv_ref,
    hinv_ref,
    lastv_ref,
    tok_s,
    tok_r,
    pair_s,
    pair_r,
    fring_s,
    fring_r,
    fx_s,
    fx_r,
    last_s,
    last_r,
    loc,
    *pack_sems,
):
    place = Place(wide, narrow)
    ring = place.ring
    tokens, width = act_in.shape
    sh = width // wide
    fr = dub_ref.shape[1] // ring
    a, q, h = place.a, place.q, place.h
    pending = []

    def go(copy):
        copy.start()
        pending.append(copy)
        return copy

    place.barrier(True)

    tok = []
    for i, (ref, whose) in enumerate(
        ((gnp_ref, place.q_diag), (gnp_ref, place.q_core), (yp_ref, place.q_diag), (yp_ref, place.q_core))
    ):
        tok.append(
            go(remote(ref.at[whose], tin_ref.at[i], tok_s, tok_r, i, place.member(place.q_core)))
        )
    own_loads = []
    for i, (ref, whose) in enumerate(
        ((gnp_ref, place.q_y), (gnp_ref, q), (yp_ref, place.q_y), (yp_ref, q))
    ):
        load = pltpu.make_async_copy(ref.at[whose], town_ref.at[i], loc.at[i])
        load.start()
        own_loads.append(load)

    pairs_in = {}

    def pair_send(s):
        d = place.back(s + 1)
        for e in range(EXPERTS):
            pairs_in[s, e] = go(
                remote(
                    dw_ref.at[1 - h, e, pl.ds(d * GROUP, GROUP)],
                    pin_ref.at[s, e],
                    pair_s,
                    pair_r,
                    s * EXPERTS + e,
                    place.pair(),
                )
            )

    pair_send(0)
    mine = lax.div(place.x, 2)

    def own_slot(s):
        return flast_ref.at[mine] if s == ring - 1 else fout_ref.at[s]

    load_dw = []
    for s in range(ring):
        own = dw_ref.at[h, :, pl.ds(place.back(s + 1) * GROUP, GROUP)]
        load_dw.append(pltpu.make_async_copy(own, own_slot(s), loc.at[10 + s]))
        load_dw[s].start()
    load_w = [
        pltpu.make_async_copy(
            ap_ref.at[:, pl.ds(i * sh, sh), :], wbuf_ref.at[i % 3], loc.at[5 + i]
        )
        for i in range(4)
    ]
    for i in (3, 1, 2):
        load_w[i].start()

    fhop = {}
    flast_copies = {}

    def expert_service(s, chunks=range(EXPERTS)):
        slot = own_slot(s)
        for e in chunks:
            if e == 0:
                load_dw[s].wait()
            pairs_in[s, e].wait_recv()
            total = slot[e].astype(F32) + pin_ref[s, e].astype(F32)
            if s > 0:
                fhop[s - 1, e].wait_recv()
                total = total + fin_ref[s - 1, e].astype(F32)
            slot[e] = total.astype(BF)
            if s < ring - 1:
                fhop[s, e] = go(
                    remote(
                        fout_ref.at[s, e],
                        fin_ref.at[s, e],
                        fring_s,
                        fring_r,
                        s * EXPERTS + e,
                        place.ring_next(),
                    )
                )
            else:
                for k in range(1, narrow // 2):
                    slab = flast_ref.at[mine, e]
                    flast_copies[e, k] = remote(
                        slab,
                        slab,
                        fx_s,
                        fx_r,
                        (k - 1) * EXPERTS + e,
                        place.other_narrow(2 * k),
                    )
                    flast_copies[e, k].start()

    others = (place.q_core, place.q_y, place.q_diag)

    def piece(r, e):
        return remote(
            flast_ref.at[0, e, others[r]],
            ug_ref.at[q, e],
            last_s,
            last_r,
            r * EXPERTS + e,
            place.member(others[r]),
        )

    everyone = others + (q,)

    def far_piece(r, e):
        return remote(
            flast_ref.at[0, e, everyone[r]],
            ug_ref.at[q, e],
            last_s,
            last_r,
            (4 + r) * EXPERTS + e,
            place.pair_member(everyone[r]),
        )

    own_piece = [
        pltpu.make_async_copy(flast_ref.at[0, e, q], ug_ref.at[q, e], loc.at[10 + ring + e])
        for e in range(EXPERTS)
    ]
    own_down = pltpu.make_async_copy(flast_ref.at[0], dg_ref, loc.at[9])
    send_down = [
        remote(flast_ref.at[0, e], dg_ref.at[e], last_s, last_r, 3 * EXPERTS + e, place.pair())
        for e in range(EXPERTS)
    ]
    def final_start(e):
        for k in range(1, narrow // 2):
            flast_copies[e, k].wait_recv()
            flast_copies[e, k].wait_send()
        if narrow > 2:
            total = flast_ref[0, e].astype(F32)
            for i in range(1, narrow // 2):
                total = total + flast_ref[i, e].astype(F32)
            flast_ref[0, e] = total.astype(BF)

        @pl.when(h == 0)
        def _():
            for r in range(3):
                far_piece(r, e).start()
                piece(r, e).start()
            far_piece(3, e).start()
            own_piece[e].start()

        @pl.when(h == 1)
        def _():
            send_down[e].start()

    def final_finish():
        @pl.when(h == 0)
        def _():
            for e in range(EXPERTS):
                for r in range(3):
                    piece(r, e).wait_recv()
                    piece(r, e).wait_send()
                for r in range(4):
                    far_piece(r, e).wait_send()
                own_piece[e].wait()
                send_down[e].wait_recv()

        @pl.when(h == 1)
        def _():
            own_down.start()
            for e in range(EXPERTS):
                send_down[e].wait_send()
                for r in range(4):
                    far_piece(r, e).wait_recv()
            own_down.wait()

    def far_send(i, n):
        own_loads[i].wait()
        tok[i].wait_recv()
        town_ref[i] = (town_ref[i].astype(F32) + tin_ref[i].astype(F32)).astype(BF)
        return go(
            remote(
                town_ref.at[i], tin_ref.at[4 + n], tok_s, tok_r, 4 + n, place.member(place.q_y)
            )
        )

    kept = (
        (cot_in, cot_ref),
        (h1_in, h1_ref),
        (heads_in, heads_ref),
        (q_in, q_ref),
        (k_in, k_ref),
        (v_in, v_ref),
        (n1_in, n1_ref),
        (act_in, act_ref),
    )
    loads = [
        pltpu.make_async_copy(src, dst, arrive.at[i]) for i, (src, dst) in enumerate(kept)
    ]
    for load in loads:
        load.start()
    far_gn = far_send(0, 0)
    bounds = item_bounds(lambda i: kinds_ref[0, i], kinds_ref.shape[1])
    fill_bias(bias_ref, bounds)
    position = lax.broadcasted_iota(jnp.int32, (tokens, 1), 0)
    expert = expert_of(position, bounds)
    inside = position < bounds[-1][2]
    vg_ref[...] = dub_ref[...]
    loads[0].wait()
    cot = cot_ref[...].astype(F32)
    for e in range(EXPERTS):
        vg_ref[7 + e : 8 + e, :] = jnp.sum(
            jnp.where(expert == e, cot, 0.0), axis=0, keepdims=True
        )

    pair_send(1)
    expert_service(0)
    own_loads[1].wait()
    tok[1].wait_recv()
    far_gn.wait_recv()
    pair_send(2)
    far_mixed = far_send(2, 1)
    gn2 = town_ref[1].astype(F32) + tin_ref[1].astype(F32) + tin_ref[4].astype(F32)
    loads[1].wait()
    hat, inv = normed(h1_ref[...])
    vg_ref[5:6, :] = jnp.sum(gn2 * hat, axis=0, keepdims=True)
    vg_ref[6:7, :] = jnp.sum(gn2, axis=0, keepdims=True)
    r = gn2 * vec_ref[5:6, :]
    r_mean = jnp.mean(r, axis=-1, keepdims=True)
    rn_mean = jnp.mean(r * hat, axis=-1, keepdims=True)
    gh = cot_ref[...].astype(F32) + (r - r_mean - hat * rn_mean) * inv
    ig_ref[...] = gh
    grad_attn = jnp.where(inside, gh, 0.0).astype(BF)
    ga_ref[...] = grad_attn
    vg_ref[4:5, :] = jnp.sum(grad_attn.astype(F32), axis=0, keepdims=True)
    sum_a = PackSum(
        place,
        owna_ref,
        cina_ref,
        youta_ref,
        yina_ref,
        houta_ref,
        hina_ref,
        lasta_ref,
        pack_sems[:8],
    )
    sum_b = PackSum(
        place,
        ownb_ref,
        cinb_ref,
        youtb_ref,
        yinb_ref,
        houtb_ref,
        hinb_ref,
        lastb_ref,
        pack_sems[8:16],
    )
    sum_v = PackSum(
        place,
        ownv_ref,
        cinv_ref,
        youtv_ref,
        yinv_ref,
        houtv_ref,
        hinv_ref,
        lastv_ref,
        pack_sems[16:],
    )
    for i in range(2, 8):
        loads[i].wait()
    owna_ref[...] = as_slabs(dot_tn(heads_ref[...], ga_ref[...]), wide)
    sum_a.start()
    load_w[3].wait()
    ghd_ref[...] = dot_nt(ga_ref[...], as_matrix(wbuf_ref[0])).astype(BF)
    load_w[0].start()
    for s in range(ring):
        sum_a.send_y(s)
    expert_service(1)
    for s in range(3, ring):
        pair_send(s)

    low = lax.broadcasted_iota(jnp.int32, (tokens, 128), 1) < 64
    dq_ref = ga_ref

    def attend_back(p, carry):
        lanes = pair_lanes(p)
        q2, k2, v2 = q_ref[:, lanes] * 0.125, k_ref[:, lanes], v_ref[:, lanes]
        g2 = ghd_ref[:, lanes]
        zero = jnp.zeros_like(q2)
        dq, dk, dv = [], [], []
        for half in (low, jnp.logical_not(low)):
            qh = jnp.where(half, q2, zero)
            gr = jnp.where(half, g2, zero)
            probs = softmax_rows(qh, k2, bias_ref)
            grad_probs = dot_nt(gr, v2)
            inner = jnp.sum(probs * grad_probs, axis=1, keepdims=True)
            grad_scores = (probs * (grad_probs - inner)).astype(BF)
            dq.append(dot(grad_scores, k2))
            dk.append(dot_tn(grad_scores, qh))
            dv.append(dot_tn(probs.astype(BF), gr))
        dq_ref[:, lanes] = (jnp.where(low, dq[0], dq[1]) * 0.125).astype(BF)
        dk_ref[:, lanes] = (dk[0] + dk[1]).astype(BF)
        dv_ref[:, lanes] = (dv[0] + dv[1]).astype(BF)
        return carry

    pairs = width // 128
    lax.fori_loop(0, pairs // 2, attend_back, 0)
    sum_a.step(0)
    lax.fori_loop(pairs // 2, pairs, attend_back, 0)
    sum_a.step(1)
    for s in range(2, ring - 2):
        expert_service(s)
    expert_service(ring - 2, (0,))

    for i, ref in enumerate((dq_ref, dk_ref, dv_ref)):
        ownb_ref[:, i * sh : (i + 1) * sh, :] = as_slabs(dot_tn(n1_ref[...], ref[...]), wide)
    sum_b.start()
    expert_service(ring - 2, (1,))
    sum_a.step(2)

    vg_ref[2:3, :] = jnp.sum(dq_ref[...].astype(F32), axis=0, keepdims=True)
    vg_ref[3:4, :] = jnp.sum(dv_ref[...].astype(F32), axis=0, keepdims=True)
    load_w[0].wait()
    gn1 = dot_nt(dq_ref[...], as_matrix(wbuf_ref[0]))
    load_w[1].wait()
    gn1 = gn1 + dot_nt(dk_ref[...], as_matrix(wbuf_ref[1]))
    load_w[2].wait()
    gn1 = gn1 + dot_nt(dv_ref[...], as_matrix(wbuf_ref[2]))
    for s in range(ring):
        sum_b.send_y(s)
    hat, inv = normed(act_ref[...].astype(F32))
    vg_ref[0:1, :] = jnp.sum(gn1 * hat, axis=0, keepdims=True)
    vg_ref[1:2, :] = jnp.sum(gn1, axis=0, keepdims=True)
    r = gn1 * vec_ref[0:1, :]
    r_mean = jnp.mean(r, axis=-1, keepdims=True)
    rn_mean = jnp.mean(r * hat, axis=-1, keepdims=True)
    ig_ref[...] = ig_ref[...] + (r - r_mean - hat * rn_mean) * inv

    low_vec = vg_ref[...].astype(BF)
    row = lax.broadcasted_iota(jnp.int32, (VROWS, 1), 0)

    for w in range(wide):
        small = low_vec[:, w * sh : (w + 1) * sh]
        small = jnp.concatenate([small, jnp.zeros((VROWS, 256 - sh), BF)], axis=1)
        j = w // GROUP
        large = low_vec[:, j * fr : (j + 1) * fr]
        large = jnp.concatenate([large, jnp.zeros((VROWS, 256 - fr), BF)], axis=1)
        large = jnp.where(q == w % GROUP, large, jnp.zeros_like(large))
        ownv_ref[w] = jnp.where(row < 10, small, large)
    sum_v.start()
    expert_service(ring - 2, (2,))
    for s in range(3, ring):
        sum_a.step(s)
    for s in range(ring):
        sum_v.send_y(s)

    own_loads[3].wait()
    tok[3].wait_recv()
    far_mixed.wait_recv()
    mixed = h1_ref[...] + town_ref[3].astype(F32) + tin_ref[3].astype(F32) + tin_ref[5].astype(F32)
    for e in range(EXPERTS):
        mixed = mixed + jnp.where(expert == e, vec_ref[7 + e : 8 + e, :], 0.0)
    mixed_ref[...] = mixed.astype(BF)

    sum_b.step(0)
    sum_v.step(0)
    expert_service(ring - 1, (0,))
    final_start(0)
    sum_b.step(1)
    sum_v.step(1)
    expert_service(ring - 1, (1,))
    final_start(1)
    expert_service(ring - 1, (2,))
    final_start(2)
    for s in range(2, ring):
        sum_b.step(s)
        sum_v.step(s)
    go_ref[...] = sum_a.finish()
    final_finish()
    last = sum_b.finish()
    gq_ref[...] = last[0:sh]
    gk_ref[...] = last[sh : 2 * sh]
    gv_ref[...] = last[2 * sh : 3 * sh]
    vout_ref[...] = sum_v.finish()
    for copy in pending:
        copy.wait_send()


def output_kernel(fr, mixed_in, ig_in, ug_in, dg_in, go_in, gq_in, gk_in, gv_in, v_in, *outs):
    (mixed, ig, g1, b1, gq, bq, gk, gv, bv, go, bo, g2, b2, gu, bu, gd, bd) = outs
    sh = g1.shape[1]
    mixed[...] = mixed_in[...]
    ig[...] = ig_in[...]
    for ref, src in ((gq, gq_in), (gk, gk_in), (gv, gv_in), (go, go_in)):
        ref[...] = src[...]
    for i, ref in enumerate((g1, b1, bq, bv, bo, g2, b2)):
        ref[...] = v_in[i : i + 1, 0:sh]
    bd[...] = v_in[7:10, 0:sh]
    bu[...] = v_in[10:13, 0:fr]
    gd[...] = dg_in[...].astype(F32)
    ring = ug_in.shape[3] // fr
    for e in range(EXPERTS):
        rows = [ug_in[to, e] for to in range(GROUP)]
        parts = [
            rows[to][:, j * fr : (j + 1) * fr] for j in range(ring) for to in range(GROUP)
        ]
        gu[e] = jnp.concatenate(parts, axis=1).astype(F32)


def body(
    wide,
    narrow,
    activations,
    cotangent,
    item_kinds,
    attn_norm_gain,
    attn_norm_bias,
    query_weight,
    query_bias,
    key_weight,
    value_weight,
    value_bias,
    output_weight,
    output_bias,
    ffn_norm_gain,
    ffn_norm_bias,
    up_weight,
    up_bias,
    down_weight,
    down_bias,
):
    ring = wide // GROUP
    tokens, width = activations.shape
    sh = width // wide
    fr = down_weight.shape[1]
    hidden = fr * ring

    flat = lambda v: v.reshape(1, sh)
    down_parts = down_weight.reshape(EXPERTS, GROUP, sh, width)

    prow = 4 * sh + VROWS
    anyspace = pl.BlockSpec(memory_space=pl.ANY)
    vmem = pl.BlockSpec(memory_space=pltpu.VMEM)
    smem = pl.BlockSpec(memory_space=pltpu.SMEM)
    dma = lambda n: pltpu.SemaphoreType.DMA((max(n, 1),))
    shape = jax.ShapeDtypeStruct
    token_bf = shape((tokens, width), BF)
    fsteps = ring * EXPERTS

    (ap, g, tn, tc, kg, h1, n1, qs, ks, vs, heads, vec, ub) = pl.pallas_call(
        functools.partial(gather_kernel, wide, narrow),
        out_shape=(
            shape((wide, prow, width), BF),
            shape((2, EXPERTS, wide, sh, width), BF),
            shape((GROUP, tokens, width), BF),
            shape((GROUP, tokens, width), BF),
            shape((GROUP, 8, 128), jnp.int32),
            shape((tokens, width), F32),
            token_bf,
            token_bf,
            token_bf,
            token_bf,
            token_bf,
            shape((VROWS, width), F32),
            shape((VROWS, hidden), F32),
        ),
        in_specs=[smem] + [vmem] * 18,
        out_specs=(anyspace,) * 11 + (vmem,) * 2,
        scratch_shapes=[
            pltpu.VMEM((tokens, width), F32),
        ]
        + [pltpu.VMEM((tokens, width), BF)] * 5
        + [
            dma(6),
            pltpu.VMEM((tokens, width), F32),
            pltpu.VMEM((tokens, tokens), F32),
            pltpu.VMEM((4, wide, sh, width), BF),
            pltpu.VMEM((wide, VROWS, 256), BF),
            pltpu.VMEM((tokens, width), BF),
            pltpu.VMEM((prow, width), BF),
            pltpu.VMEM((VROWS, 256), F32),
            pltpu.VMEM((GROUP, EXPERTS, sh, hidden), BF),
            pltpu.VMEM((8, 128), jnp.int32),
            dma(ring),
            dma(ring),
            dma(ring),
            dma(ring),
            dma(2 * ring),
            dma(2 * ring),
            dma(3),
            dma(3),
            dma(fsteps),
            dma(fsteps),
            dma(fsteps),
            dma(fsteps),
            dma(6),
            dma(6),
            dma(3),
            dma(3),
            dma(11),
        ],
        compiler_params=pltpu.CompilerParams(
            collective_id=0, has_side_effects=True, vmem_limit_bytes=VMEM_LIMIT
        ),
        name="gather_attend",
    )(
        item_kinds,
        item_kinds,
        activations,
        cotangent,
        query_weight,
        key_weight,
        value_weight,
        output_weight,
        flat(attn_norm_gain),
        flat(attn_norm_bias),
        flat(query_bias),
        flat(value_bias),
        flat(output_bias),
        flat(ffn_norm_gain),
        flat(ffn_norm_bias),
        down_bias,
        up_bias,
        up_weight,
        down_parts,
    )

    per_member = 3
    rows = tokens // per_member
    full = lambda *dims: pl.BlockSpec(
        dims, lambda i: (0,) * len(dims), pipeline_mode=pl.Buffered(1)
    )
    tiles = GROUP * per_member
    tile = pl.BlockSpec((rows, width), lambda i: (jnp.minimum(i, tiles - 1), 0))
    matrix = pl.BlockSpec((1, width, width), lambda i: (jnp.maximum(i - tiles, 0), 0, 0))
    y, gn, dw, dub = pl.pallas_call(
        functools.partial(expert_kernel, per_member, tiles),
        grid=(tiles + 2 * EXPERTS,),
        out_shape=(
            shape((GROUP * tokens, width), BF),
            shape((GROUP * tokens, width), BF),
            shape((2 * EXPERTS, width, width), BF),
            shape((VROWS, hidden), F32),
        ),
        in_specs=[
            smem,
            tile,
            tile,
            full(2 * EXPERTS, width, width),
            full(VROWS, hidden),
        ],
        out_specs=(tile, tile, matrix, full(VROWS, hidden)),
        scratch_shapes=[
            pltpu.VMEM((2 * EXPERTS, width, width), F32),
        ],
        compiler_params=pltpu.CompilerParams(
            dimension_semantics=("arbitrary",), vmem_limit_bytes=VMEM_LIMIT
        ),
        name="experts",
    )(
        kg,
        tn.reshape(GROUP * tokens, width),
        tc.reshape(GROUP * tokens, width),
        g.reshape(2 * EXPERTS, width, width),
        ub,
    )

    def pack_scratch(rows, lanes=width):
        buf = lambda n: pltpu.VMEM((n, rows, lanes), BF)
        return [
            buf(wide),
            pltpu.VMEM((ring, 2, rows, lanes), BF),
            buf(ring),
            buf(ring),
            buf(max(ring - 1, 1)),
            buf(max(ring - 1, 1)),
            buf(narrow),
        ]

    pack_sems = [dma(2 * ring)] * 2 + [dma(ring)] * 4 + [dma(narrow - 1)] * 2
    slab = (EXPERTS, GROUP, sh, width)
    (mixed, ig, ug, dg, g_out, g_query, g_key, g_value, vout) = pl.pallas_call(
        functools.partial(grad_kernel, wide, narrow),
        out_shape=(
            token_bf,
            shape((tokens, width), F32),
            shape((GROUP, EXPERTS, sh, width), BF),
            shape(slab, BF),
            shape((sh, width), F32),
            shape((sh, width), F32),
            shape((sh, width), F32),
            shape((sh, width), F32),
            shape((VROWS, 256), F32),
        ),
        in_specs=[smem] + [anyspace] * 8 + [vmem] * 2 + [anyspace] * 4,
        out_specs=(vmem, vmem, anyspace, anyspace) + (vmem,) * 5,
        scratch_shapes=[
            pltpu.VMEM((tokens, width), BF),
            pltpu.VMEM((tokens, width), BF),
            pltpu.VMEM((tokens, width), F32),
        ]
        + [pltpu.VMEM((tokens, width), BF)] * 5
        + [
            dma(8),
            pltpu.VMEM((6, tokens, width), BF),
            pltpu.VMEM((4, tokens, width), BF),
            pltpu.VMEM((ring,) + slab[:1] + slab[1:], BF),
            pltpu.VMEM((max(ring - 1, 1),) + slab, BF),
            pltpu.VMEM((max(ring - 1, 1),) + slab, BF),
            pltpu.VMEM((max(narrow // 2, 1),) + slab, BF),
            pltpu.VMEM((3, wide, sh, width), BF),
            pltpu.VMEM((tokens, tokens), F32),
            pltpu.VMEM((tokens, width), BF),
            pltpu.VMEM((tokens, width), BF),
            pltpu.VMEM((tokens, width), BF),
            pltpu.VMEM((tokens, width), BF),
            pltpu.VMEM((VROWS, width), F32),
        ]
        + pack_scratch(sh)
        + pack_scratch(3 * sh)
        + pack_scratch(VROWS, 256)
        + [
            dma(6),
            dma(6),
            dma(fsteps),
            dma(fsteps),
            dma(fsteps),
            dma(fsteps),
            dma(EXPERTS * max(narrow // 2 - 1, 1)),
            dma(EXPERTS * max(narrow // 2 - 1, 1)),
            dma(8 * EXPERTS),
            dma(8 * EXPERTS),
            dma(10 + ring + EXPERTS),
        ]
        + pack_sems
        + pack_sems
        + pack_sems,
        compiler_params=pltpu.CompilerParams(
            collective_id=1, has_side_effects=True, vmem_limit_bytes=VMEM_LIMIT
        ),
        name="gradients",
    )(
        item_kinds,
        activations,
        cotangent,
        h1,
        n1,
        qs,
        ks,
        vs,
        heads,
        vec,
        dub,
        ap,
        y.reshape(GROUP, tokens, width),
        gn.reshape(GROUP, tokens, width),
        dw.reshape(2, EXPERTS, wide, sh, width),
    )

    vec_shape = shape((1, sh), F32)
    mat_shape = shape((sh, width), F32)
    outs = pl.pallas_call(
        functools.partial(output_kernel, fr),
        out_shape=(
            token_bf,
            shape((tokens, width), F32),
            vec_shape,
            vec_shape,
            mat_shape,
            vec_shape,
            mat_shape,
            mat_shape,
            vec_shape,
            mat_shape,
            vec_shape,
            vec_shape,
            vec_shape,
            shape((EXPERTS, sh, GROUP * hidden), F32),
            shape((EXPERTS, fr), F32),
            shape(slab, F32),
            shape((EXPERTS, sh), F32),
        ),
        in_specs=[vmem] * 9,
        out_specs=(vmem,) * 17,
        compiler_params=pltpu.CompilerParams(vmem_limit_bytes=VMEM_LIMIT),
        name="final_outputs",
    )(mixed, ig, ug, dg, g_out, g_query, g_key, g_value, vout)
    outs = list(outs)
    for i in (2, 3, 5, 8, 10, 11, 12):
        outs[i] = outs[i].reshape(sh)
    outs[15] = outs[15].reshape(EXPERTS, fr, width)
    return tuple(outs)


def solution(mesh):
    rows = P(("wide", "narrow"), None)
    return jax.shard_map(
        functools.partial(body, mesh.shape["wide"], mesh.shape["narrow"]),
        mesh=mesh,
        in_specs=(
            rows,
            rows,
            rows,
            P("wide"),
            P("wide"),
            P("wide", None),
            P("wide"),
            P("wide", None),
            P("wide", None),
            P("wide"),
            P("wide", None),
            P("wide"),
            P("wide"),
            P("wide"),
            P(None, "wide", None),
            P(None, "wide"),
            P(None, "wide", None),
            P(None, "wide"),
        ),
        out_specs=(
            rows,
            rows,
            P("wide"),
            P("wide"),
            P("wide", None),
            P("wide"),
            P("wide", None),
            P("wide", None),
            P("wide"),
            P("wide", None),
            P("wide"),
            P("wide"),
            P("wide"),
            P(None, "wide", None),
            P(None, "wide"),
            P(None, "wide", None),
            P(None, "wide"),
        ),
        check_vma=False,
    )
```
